32 devices in a mesh: dp: 2 (over core), mp: 16 (over z, y, x).
Axes of the slice: x: 2, y: 2, z: 4, core: 2. Of those that a mesh axis runs over, the one named last changes fastest.
Arguments:
- inputs: bfloat16 [4, 8192, 768], P('dp', 'mp'), may hold values from -6 to 6
- cotangent: bfloat16 [4, 8192, 768], P('dp', 'mp'), may hold values from -6 to 6
- norm_gain: float32 [2, 2, 768], replicated, may hold values from 0.5 to 1.5
- norm_bias: float32 [2, 2, 768], replicated, may hold values from -1.5 to 1.5
- in_weight: bfloat16 [2, 768, 3, 768], P(None, None, None, 'mp'), may hold values from -0.21875 to 0.21875
- kernels: bfloat16 [2, 2, 768, 2048], P(None, None, 'mp'), may hold values from -0.125 to 0.125
- out_weight: bfloat16 [2, 768, 768], P(None, 'mp'), may hold values from -0.21875 to 0.21875
- up_weight: bfloat16 [2, 768, 3072], P(None, None, 'mp'), may hold values from -0.21875 to 0.21875
- down_weight: bfloat16 [2, 3072, 768], P(None, 'mp'), may hold values from -0.109375 to 0.109375
- taps_kept: int32 [2], replicated, may hold values from 1024 to 2048, as said below
Outputs:
- output: float32 [4, 8192, 768], P('dp', 'mp')
- input_grad: float32 [4, 8192, 768], P('dp', 'mp')
- gain_grad: float32 [2, 2, 768], replicated
- bias_grad: float32 [2, 2, 768], replicated
- in_grad: float32 [2, 768, 3, 768], P(None, None, None, 'mp')
- kernel_grad: float32 [2, 2, 768, 2048], P(None, None, 'mp')
- out_grad: float32 [2, 768, 768], P(None, 'mp')
- up_grad: float32 [2, 768, 3072], P(None, None, 'mp')
- down_grad: float32 [2, 3072, 768], P(None, 'mp')
The draws below stay inside these ranges and needn't reach their ends.
Inputs may be any that keep to these rules, and one draw needn't show every extreme that they name: Each block's kernels use taps 0 .. taps_kept - 1 only; in every draw one of the 2 blocks uses all 2048.
All inputs are finite; a program needn't handle non-finite values.
Results may differ from the reference program's by a relative error of at most 0.024.
Values may be sent and summed in bfloat16 or wider, within the bound.
No kernel may reach another device: no remote copies, remote signals or barrier semaphores. Data moves between devices by JAX's collectives and lax.ppermute only.
A program may use at most 896 MiB of HBM per device.

```python
import jax
import jax.numpy as jnp
from jax import lax

D = 768
FF = 3072
TAPS = 2048
L = 8192
LAYERS = 2
SEQS = 4


def draw_taps_kept(key, part):
    key = jax.random.fold_in(key, 7)
    first_key, second_key = jax.random.split(key)
    shorter = jax.random.randint(first_key, (LAYERS,), TAPS // 2, TAPS + 1)
    full_layer = jax.random.randint(second_key, (), 0, LAYERS)
    return jnp.where(jnp.arange(LAYERS) == full_layer, TAPS, shorter).astype(jnp.int32)


def levels(own_key, shape, shards, low, top_value):
    gain, own = 1.0, jax.random.fold_in(own_key, 6)
    for position, blocks in shards:
        heights = jnp.exp(jax.random.uniform(jax.random.fold_in(own, position), (blocks,), jnp.float32, low / len(shards), top_value / len(shards)))
        gain = gain * jnp.repeat(heights, shape[position] // blocks).reshape([-1 if axis == position else 1 for axis in range(len(shape))])
    return gain


def noise(own_key, extent, deviation, bound, cuts=(), held_as=jnp.bfloat16):
    gain = levels(own_key, extent, cuts, -0.22, 0.18) if cuts else 1.0
    values = jax.random.normal(own_key, extent, jnp.float32) * deviation * gain
    return jnp.minimum(jnp.maximum(values, -bound), bound).astype(held_as)


def setup_inputs(seed: int = 0) -> dict:
    seeds = jax.random.split(jax.random.key(seed), 11)
    return {
        "inputs": noise(seeds[0], (SEQS, L, D), 1.0, 6.0, ((0, 2), (1, 16))),
        "cotangent": noise(seeds[1], (SEQS, L, D), 1.0, 6.0, ((0, 2), (1, 16))),
        "norm_gain": jnp.clip(1.0 + 0.1 * jax.random.normal(seeds[2], (LAYERS, 2, D), jnp.float32), 0.5, 1.5),
        "norm_bias": noise(seeds[3], (LAYERS, 2, D), 0.3, 1.5, (), jnp.float32),
        "in_weight": noise(seeds[4], (LAYERS, D, 3, D), D ** -0.5, 0.21875, ((3, 16),)),
        "kernels": noise(seeds[5], (LAYERS, 2, D, TAPS), TAPS ** -0.5, 0.125, ((2, 16),)),
        "out_weight": noise(seeds[6], (LAYERS, D, D), D ** -0.5, 0.21875, ((1, 16),)),
        "up_weight": noise(seeds[7], (LAYERS, D, FF), D ** -0.5, 0.21875, ((2, 16),)),
        "down_weight": noise(seeds[8], (LAYERS, FF, D), FF ** -0.5, 0.109375, ((1, 16),)),
        "taps_kept": draw_taps_kept(jax.random.fold_in(seeds[10], 71), 0),
    }


@jax.custom_vjp
def low(v):
    return lax.optimization_barrier(v.astype(jnp.bfloat16)).astype(jnp.float32)

@jax.custom_vjp
def low_back(v):
    return v

def low_keep(v):
    return (low(v), None)

def low_pass(kept, grad):
    return (grad,)

def back_keep(v):
    return (v, None)

def back_low(kept, grad):
    return (low(grad),)
low.defvjp(low_keep, low_pass)
low_back.defvjp(back_keep, back_low)
EPS = 1e-05

def product(left_side, right_side):
    return jnp.dot(left_side, right_side, preferred_element_type=jnp.float32, precision=lax.Precision.HIGHEST)

def normalize(stream, gain_row, shift_row):
    average = lax.optimization_barrier(jnp.mean(stream, axis=-1, keepdims=True))
    centered = stream - average
    variance = lax.optimization_barrier(jnp.mean(centered * centered, axis=-1, keepdims=True))
    return centered * lax.rsqrt(variance + EPS) * gain_row + shift_row

def causal_conv(kernel_now, signal):
    length = signal.shape[0]
    fft_size = 2 * length
    spectrum = jnp.fft.rfft(signal, n=fft_size, axis=0) * jnp.fft.rfft(kernel_now.T, n=fft_size, axis=0)
    return jnp.fft.irfft(spectrum, n=fft_size, axis=0)[:length]

def block_forward(stream, weights, taps_kept):
    norm_gain, norm_bias, in_weight, kernels, out_weight, up_weight, down_weight = weights
    tap_mask = (jnp.arange(TAPS)[None, :] < taps_kept[:, None]).astype(jnp.float32)
    for layer_idx in range(LAYERS):
        first_normalized = low(normalize(stream, norm_gain[layer_idx, 0], norm_bias[layer_idx, 0]))
        mixed_in = product(first_normalized, in_weight[layer_idx].reshape(D, 3 * D))
        mixed_in = low(low_back(mixed_in))
        gate_one = mixed_in[:, :D]
        gate_two = mixed_in[:, D:2 * D]
        values_in = mixed_in[:, 2 * D:]
        kernel_pair = kernels[layer_idx] * tap_mask[layer_idx][None, None, :]
        conv_one = low_back(causal_conv(kernel_pair[0], values_in))
        carried = low(gate_one * conv_one)
        conv_two = low_back(causal_conv(kernel_pair[1], carried))
        gated_out = low(low_back(gate_two * conv_two))
        stream = stream + low_back(product(gated_out, out_weight[layer_idx]))
        second_normalized = low(normalize(stream, norm_gain[layer_idx, 1], norm_bias[layer_idx, 1]))
        preactivation = low_back(product(second_normalized, up_weight[layer_idx]))
        hidden = low(jax.nn.gelu(preactivation, approximate=False))
        stream = stream + low_back(product(hidden, down_weight[layer_idx]))
    return stream

def reference(inputs, cotangent, norm_gain, norm_bias, in_weight, kernels, out_weight, up_weight, down_weight, taps_kept):
    params = (norm_gain.astype(jnp.float32), norm_bias.astype(jnp.float32), in_weight.astype(jnp.float32), kernels.astype(jnp.float32), out_weight.astype(jnp.float32), up_weight.astype(jnp.float32), down_weight.astype(jnp.float32))

    def forward(stream_in, *weights):
        return block_forward(stream_in, weights, taps_kept)

    def one_sequence(totals, pair):
        stream, upstream = pair
        result, pullback = jax.vjp(forward, stream, *params)
        grad_all = pullback(upstream)
        new_totals = tuple((total + grad_one for total, grad_one in zip(totals, grad_all[1:])))
        return (new_totals, (result, grad_all[0]))
    zero_grads = tuple((jnp.zeros_like(weight_one) for weight_one in params))
    totals, (output, input_grad) = lax.scan(one_sequence, zero_grads, (inputs.astype(jnp.float32), cotangent.astype(jnp.float32)))
    return (output, input_grad, totals[0], totals[1], totals[2], totals[3], totals[4], totals[5], totals[6])
```

```python
import functools
import math

import jax
import jax.numpy as jnp
import ml_dtypes
import numpy as np
from jax import lax
from jax.experimental import pallas as pl
from jax.experimental.pallas import tpu as pltpu
from jax.sharding import PartitionSpec as P

EPS = 1e-05
LANES = 128
RADIX = 32
HALF = RADIX // 2
FREQS = HALF + 1
POINTS = LANES * RADIX
SPAN = POINTS // 2
BF16 = jnp.bfloat16
F32 = jnp.float32
VMEM_BYTES = 56 * 2**20
PASSES = 1


def params():
    return pltpu.CompilerParams(vmem_limit_bytes=VMEM_BYTES)


def whole(array):
    rank = array.ndim
    return pl.BlockSpec(array.shape, lambda *_: (0,) * rank, pipeline_mode=pl.Buffered(1))


def add(a, b):
    if a is None:
        return b
    return a if b is None else a + b


def sub(a, b):
    if b is None:
        return a
    return -b if a is None else a - b


def tidy(v):
    for exact in (0.0, 1.0, -1.0):
        if abs(v - exact) < 1e-12:
            return exact
    return v


def scaled(v, factor):
    if v is None or factor == 0.0:
        return None
    if factor == 1.0:
        return v
    return -v if factor == -1.0 else v * factor


def turn(z, angle):
    re, im = z
    c, s = tidy(math.cos(angle)), tidy(math.sin(angle))
    if re is not None and im is not None and abs(abs(c) - abs(s)) < 1e-12:
        r = math.copysign(abs(c), c)
        if c * s > 0:
            return ((re - im) * r, (re + im) * r)
        return ((re + im) * r, (im - re) * r)
    return (sub(scaled(re, c), scaled(im, s)), add(scaled(im, c), scaled(re, s)))


def analyse(x):
    n = len(x)
    if n == 1:
        return [(x[0], None)]
    even, odd = analyse(x[0::2]), analyse(x[1::2])
    if n == 2:
        return [(add(even[0][0], odd[0][0]), None), (sub(even[0][0], odd[0][0]), None)]
    half, quarter = n // 2, n // 4
    out = [None] * (half + 1)
    for k in range(quarter + 1):
        t = turn(odd[k], -2 * math.pi * k / n)
        out[k] = (add(even[k][0], t[0]), add(even[k][1], t[1]))
        if k != quarter:
            out[half - k] = (sub(even[k][0], t[0]), sub(t[1], even[k][1]))
    return out


def synthesise(x, n, upper):
    if n == 2:
        return [sub(x[0][0], x[1][0]) if upper else add(x[0][0], x[1][0])]
    half, quarter = n // 2, n // 4
    even, odd = [], []
    for k in range(quarter + 1):
        a, b = x[k], x[half - k]
        if k == 0:
            even.append((add(a[0], b[0]), None))
            odd.append((sub(a[0], b[0]), None))
        elif k == quarter:
            even.append((a[0] * 2.0, None))
            odd.append((a[1] * -2.0, None))
        else:
            even.append((add(a[0], b[0]), sub(a[1], b[1])))
            odd.append(turn((sub(a[0], b[0]), add(a[1], b[1])), 2 * math.pi * k / n))
    out = [None] * half
    out[0::2] = synthesise(even, half, upper)
    out[1::2] = synthesise(odd, half, upper)
    return out


def split_bf16(matrix):
    matrix = matrix.astype(np.float32)
    high = matrix.astype(ml_dtypes.bfloat16)
    low = (matrix - high.astype(np.float32)).astype(ml_dtypes.bfloat16)
    return jnp.asarray(np.stack([high, low][: 1 if PASSES == 1 else 2]))


def tables():
    j = np.arange(LANES)
    angle = 2 * np.pi * np.outer(j, j) / LANES
    c, s = np.cos(angle), np.sin(angle)
    twist = 2 * np.pi * np.outer(np.arange(FREQS), j) / POINTS
    return [
        split_bf16(np.block([[c, -s], [s, c]])),
        split_bf16(np.block([[c, s], [-s, c]]) / POINTS),
        jnp.asarray(np.cos(twist), F32),
        jnp.asarray(np.sin(twist), F32),
    ]


def lane_product(a, matrix):
    high = a.astype(BF16)
    y = jnp.dot(high, matrix[0], preferred_element_type=F32)
    if PASSES > 1:
        y = y + jnp.dot(high, matrix[1], preferred_element_type=F32)
    if PASSES > 2:
        low = (a - high.astype(F32)).astype(BF16)
        y = y + jnp.dot(low, matrix[0], preferred_element_type=F32)
    return y


class Convolver:
    def __init__(self, sources, groups, pieces, blocks, rows, refs):
        self.sources, self.groups, self.pieces = sources, groups, pieces
        self.blocks, self.rows = blocks, rows
        self.forward, self.backward, self.cos, self.sin, self.left, self.right, self.freq = refs

    def places(self):
        for i in range(self.sources * self.groups * self.pieces):
            chunk, piece = divmod(i, self.pieces)
            group, source = divmod(chunk, self.sources)
            begin = (group * self.pieces + piece) * LANES
            yield i, source, slice(begin, begin + LANES)

    def load(self, ref, dst):
        for i, source, lanes in self.places():
            dst[i] = ref[source, :, lanes].astype(F32)

    def store(self, src, ref, part=None):
        for i, source, lanes in self.places():
            if part is None:
                ref[source, :, lanes] = src[i].astype(ref.dtype)
            else:
                ref[source, part, :, lanes] = src[i].astype(ref.dtype)

    def subtiles(self):
        return [pl.ds(8 * t, 8) for t in range(self.rows // 8)]

    def spectrum(self, read, count, base):
        for b in range(count):
            for rows in self.subtiles():
                x = analyse([read(b, i, rows) for i in range(HALF)] + [None] * HALF)
                for f, (re, im) in enumerate(x):
                    if f:
                        c, s = self.cos[f : f + 1, :], self.sin[f : f + 1, :]
                        if im is None:
                            re, im = re * c, -(re * s)
                        else:
                            re, im = re * c + im * s, im * c - re * s
                    self.left[b * FREQS + f, rows, 0:LANES] = re
                    self.left[b * FREQS + f, rows, LANES:] = jnp.zeros_like(re) if im is None else im
            y = lane_product(self.stacked(b), self.forward)
            begin = (base + b) * FREQS
            self.freq[begin : begin + FREQS] = y.reshape(FREQS, self.rows, 2 * LANES)

    def stacked(self, b):
        return self.left[b * FREQS : (b + 1) * FREQS].reshape(FREQS * self.rows, 2 * LANES)

    def entry(self, row, rows):
        return self.freq[row, rows, 0:LANES], self.freq[row, rows, LANES:]

    def window(self, base, b, f, rows, ahead):
        re, im = self.entry((base + b) * FREQS + f, rows)
        other = b + 1 if ahead else b - 1
        if not ahead and f % 2:
            re, im = -re, -im
        if 0 <= other < self.blocks:
            ore, oim = self.entry((base + other) * FREQS + f, rows)
            if ahead and f % 2:
                return re - ore, im - oim
            return re + ore, im + oim
        return re, im

    def inverse(self, b, upper, write):
        y = lane_product(self.stacked(b), self.backward)
        begin = b * FREQS
        self.right[begin : begin + FREQS] = y.reshape(FREQS, self.rows, 2 * LANES)
        for rows in self.subtiles():
            parts = []
            for f in range(FREQS):
                re = self.right[begin + f, rows, 0:LANES]
                im = self.right[begin + f, rows, LANES:]
                c, s = self.cos[f : f + 1, :], self.sin[f : f + 1, :]
                if f == 0:
                    parts.append((re, None))
                elif f == HALF:
                    parts.append((re * c - im * s, None))
                else:
                    parts.append((re * c - im * s, im * c + re * s))
            for i, value in enumerate(synthesise(parts, RADIX, upper)):
                write(b, i, rows, value)

    def convolve(self, signal, kernel, ahead, write):
        for b in range(self.blocks):
            for rows in self.subtiles():
                for f in range(FREQS):
                    re, im = self.window(signal, b, f, rows, ahead)
                    kre, kim = self.entry(kernel * FREQS + f, rows)
                    if ahead:
                        pre, pim = re * kre + im * kim, im * kre - re * kim
                    else:
                        pre, pim = re * kre - im * kim, re * kim + im * kre
                    self.left[b * FREQS + f, rows, 0:LANES] = pre
                    self.left[b * FREQS + f, rows, LANES:] = pim
            self.inverse(b, not ahead, write)

    def taps(self, signal, grads, write):
        for rows in self.subtiles():
            for f in range(FREQS):
                re = im = None
                for b in range(self.blocks):
                    gre, gim = self.window(grads, b, f, rows, True)
                    sre, sim = self.entry((signal + b) * FREQS + f, rows)
                    re = add(re, sre * gre + sim * gim)
                    im = add(im, sre * gim - sim * gre)
                self.left[f, rows, 0:LANES] = re
                self.left[f, rows, LANES:] = im
        self.inverse(0, False, write)


def kernel_reader(k_ref, j):
    def read(_, i, rows):
        value = k_ref[j, :, i * LANES : (i + 1) * LANES].astype(F32)
        return value[rows.start : rows.start + rows.size]

    return read


def mix_body(shape, v_ref, g_ref, k_ref, *refs):
    (fwd, bwd, cos, sin, out_ref, one_ref, carried_ref, xs, gs, left, right, freq) = refs
    cv = Convolver(*shape, v_ref.shape[1], (fwd, bwd, cos, sin, left, right, freq))
    n = cv.blocks
    cv.load(v_ref, xs)
    cv.load(g_ref, gs)

    def read(b, i, rows):
        return xs[b * HALF + i, rows, :]

    cv.spectrum(kernel_reader(k_ref, 0), 1, n)
    cv.spectrum(kernel_reader(k_ref, 1), 1, n + 1)
    cv.spectrum(read, n, 0)

    def gate(b, i, rows, value):
        r = b * HALF + i
        xs[r, rows, :] = (gs[r, rows, :] * value).astype(BF16).astype(F32)
        gs[r, rows, :] = value

    cv.convolve(0, n, False, gate)
    one_ref[...] = gs[...].astype(BF16)
    carried_ref[...] = xs[...].astype(BF16)
    cv.spectrum(read, n, 0)

    def keep(b, i, rows, value):
        gs[b * HALF + i, rows, :] = value

    cv.convolve(0, n + 1, False, keep)
    cv.store(gs, out_ref)


def unmix_body(shape, d_ref, v_ref, g_ref, one_ref, carried_ref, k_ref, *refs):
    (fwd, bwd, cos, sin, out_ref, dk_ref, xs, gs, left, right, freq) = refs
    cv = Convolver(*shape, v_ref.shape[1], (fwd, bwd, cos, sin, left, right, freq))
    n = cv.blocks
    cv.load(d_ref, xs)
    cv.load(g_ref, gs)

    def read(b, i, rows):
        return xs[b * HALF + i, rows, :]

    def read_carried(b, i, rows):
        return carried_ref[b * HALF + i].astype(F32)[rows.start : rows.start + rows.size]

    def put(j):
        def write(_, i, rows, value):
            dk_ref[j, rows, i * LANES : (i + 1) * LANES] = value

        return write

    cv.spectrum(kernel_reader(k_ref, 1), 1, 2 * n)
    cv.spectrum(read, n, 0)
    cv.spectrum(read_carried, n, n)
    cv.taps(n, 0, put(1))

    def gate(b, i, rows, value):
        r = b * HALF + i
        xs[r, rows, :] = (gs[r, rows, :] * value).astype(BF16).astype(F32)
        gs[r, rows, :] = value

    cv.convolve(0, 2 * n, True, gate)
    gs[...] = gs[...] * one_ref[...].astype(F32)
    cv.store(gs, out_ref, 0)
    cv.spectrum(read, n, 0)
    cv.load(v_ref, xs)
    cv.spectrum(kernel_reader(k_ref, 0), 1, 2 * n)
    cv.spectrum(read, n, n)
    cv.taps(n, 0, put(0))

    def keep(b, i, rows, value):
        gs[b * HALF + i, rows, :] = value

    cv.convolve(0, 2 * n, True, keep)
    cv.store(gs, out_ref, 1)


def conv_sizes(gates):
    sources, groups, _, shard, length = gates.shape
    tile = 16
    pieces = length // (groups * LANES)
    total = sources * length
    return sources, groups, shard, length, tile, pieces, total // LANES, total // SPAN


def conv_scratch(tile, rows, blocks, spectra):
    return [
        pltpu.VMEM((rows, tile, LANES), F32),
        pltpu.VMEM((rows, tile, LANES), F32),
        pltpu.VMEM((blocks * FREQS, tile, 2 * LANES), F32),
        pltpu.VMEM((blocks * FREQS, tile, 2 * LANES), F32),
        pltpu.VMEM((spectra * FREQS, tile, 2 * LANES), F32),
    ]


def mix(gates, taps):
    q, g, shard, length, tile, pieces, rows, blocks = conv_sizes(gates)
    consts = tables()
    by_source = (q, None, None, tile, length)
    nat = pl.BlockSpec((None, rows, tile, LANES), lambda a, b: (a, 0, b, 0))
    return pl.pallas_call(
        functools.partial(mix_body, (q, g, pieces, blocks)),
        grid=(g, shard // tile),
        in_specs=[
            pl.BlockSpec(by_source, lambda a, b: (0, a, 1, b, 0)),
            pl.BlockSpec(by_source, lambda a, b: (0, a, 0, b, 0)),
            pl.BlockSpec((None, 2, tile, SPAN), lambda a, b: (a, 0, b, 0)),
        ]
        + [whole(c) for c in consts],
        out_specs=[pl.BlockSpec((q, None, tile, length), lambda a, b: (0, a, b, 0)), nat, nat],
        out_shape=[
            jax.ShapeDtypeStruct((q, g, shard, length), BF16),
            jax.ShapeDtypeStruct((g, rows, shard, LANES), BF16),
            jax.ShapeDtypeStruct((g, rows, shard, LANES), BF16),
        ],
        scratch_shapes=conv_scratch(tile, rows, blocks, blocks + 2),
        compiler_params=params(),
        name="mix",
    )(gates, gates, taps, *consts)


def unmix(grads, gates, conv_one, carried, taps):
    q, g, shard, length, tile, pieces, rows, blocks = conv_sizes(gates)
    consts = tables()
    by_source = (q, None, None, tile, length)
    nat = pl.BlockSpec((None, rows, tile, LANES), lambda a, b: (a, 0, b, 0))
    kern = pl.BlockSpec((None, 2, tile, SPAN), lambda a, b: (a, 0, b, 0))
    return pl.pallas_call(
        functools.partial(unmix_body, (q, g, pieces, blocks)),
        grid=(g, shard // tile),
        in_specs=[
            pl.BlockSpec((q, None, tile, length), lambda a, b: (0, a, b, 0)),
            pl.BlockSpec(by_source, lambda a, b: (0, a, 1, b, 0)),
            pl.BlockSpec(by_source, lambda a, b: (0, a, 0, b, 0)),
            nat,
            nat,
            kern,
        ]
        + [whole(c) for c in consts],
        out_specs=[
            pl.BlockSpec((q, None, 2, tile, length), lambda a, b: (0, a, 0, b, 0)),
            kern,
        ],
        out_shape=[
            jax.ShapeDtypeStruct((q, g, 2, shard, length), BF16),
            jax.ShapeDtypeStruct((g, 2, shard, SPAN), F32),
        ],
        scratch_shapes=conv_scratch(tile, rows, blocks, 2 * blocks + 1),
        compiler_params=params(),
        name="unmix",
    )(grads, gates, gates, conv_one, carried, taps, *consts)


def standardise(stream):
    average = jnp.mean(stream, axis=0, keepdims=True)
    centered = stream - average
    inv_std = lax.rsqrt(jnp.mean(centered * centered, axis=0, keepdims=True) + EPS)
    return centered * inv_std, inv_std


def standardise_back(grad, gain, stream):
    unit, inv_std = standardise(stream)
    g = grad * gain
    mean_grad = jnp.mean(g, axis=0, keepdims=True)
    mean_cross = jnp.mean(g * unit, axis=0, keepdims=True)
    back = inv_std * (g - mean_grad - unit * mean_cross)
    gain_part = jnp.sum(grad * unit, axis=1, keepdims=True)
    bias_part = jnp.sum(grad, axis=1, keepdims=True)
    return back, gain_part, bias_part


def transposed(x):
    return jnp.transpose(x.astype(F32))


def gelu_pair(x):
    z = jnp.abs(x) * math.sqrt(0.5)
    t = 1.0 / (1.0 + 0.3275911 * z)
    e = jnp.exp(-(z * z))
    poly = t * (
        0.127414796 + t * (-0.142248368 + t * (0.710706871 + t * (-0.726576014 + t * 0.530702714)))
    )
    tail = poly * e
    phi = jnp.where(x >= 0, 1.0 - tail, tail)
    return x * phi, phi + x * (e * (1.0 / math.sqrt(2 * math.pi)))


def first(axis_is_zero, refs, cut, body):
    if len(refs) == 1:
        body(refs[0].at[:, 0 : 2 * cut], refs[0].at[:, 2 * cut : 3 * cut])
        return

    @pl.when(axis_is_zero)
    def _():
        body(refs[0], refs[1].at[:, 0:cut])

    @pl.when(jnp.logical_not(axis_is_zero))
    def _():
        body(refs[1], refs[0].at[:, 0:cut])


class Pieces:
    def __init__(self, arrays, begin, rows):
        self.arrays, self.begin, self.rows = arrays, begin, rows

    def specs(self):
        mp, _, width = self.arrays[0].shape
        block = self.begin // self.rows
        shape = (mp, self.rows, width)
        spec = pl.BlockSpec(shape, lambda *_: (0, block, 0), pipeline_mode=pl.Buffered(1))
        return [spec] * len(self.arrays)

    def __len__(self):
        return len(self.arrays)


SCALARS = pl.BlockSpec(memory_space=pltpu.SMEM)


def by_channel(blocks, groups):
    peers = blocks.shape[0] // groups
    order = [h * peers + q for q in range(peers) for h in range(groups)]
    return jnp.concatenate([blocks[m : m + 1] for m in order], axis=0)


def project_body(natural, ways, groups, place_ref, x_ref, gain_ref, bias_ref, *rest):
    dense, rest = rest[:ways], rest[ways:]
    if natural:
        s_ref, op_ref, two_ref, n_ref, pair_w, value_w = rest
        x = transposed(x_ref[...])
        s_ref[...] = x
    else:
        op_ref, two_ref, n_ref, pair_w, value_w = rest
        x = x_ref[...]
    mp, cut, t = two_ref.shape

    @pl.when(pl.program_id(0) == 0)
    def _():
        def body(pair, value):
            pair_w[...] = by_channel(pair, groups)
            value_w[...] = by_channel(value, groups)

        first(place_ref[0] == 0, dense, cut, body)

    unit, _ = standardise(x)
    normed = unit * gain_ref[...] + bias_ref[...]
    n_ref[...] = transposed(normed).astype(BF16)
    normed = normed.astype(BF16)
    width = normed.shape[0]
    y = jnp.dot(
        pair_w[...].reshape(mp * 2 * cut, width), normed, preferred_element_type=F32
    )
    y = y.astype(BF16).reshape(mp, 2, cut, t)
    op_ref[:, 0] = y[:, 0]
    two_ref[...] = y[:, 1]
    y = jnp.dot(value_w[...].reshape(mp * cut, width), normed, preferred_element_type=F32)
    op_ref[:, 1] = y.astype(BF16).reshape(mp, cut, t)


def token_tile(length):
    return min(length, 256)


def project(natural, groups, place, x, dense, gain, bias, cut):
    mp, _, width = dense.arrays[0].shape
    length = x.shape[0] if natural else x.shape[1]
    t = token_tile(length)
    tall = pl.BlockSpec((t, width), lambda i: (i, 0))
    flat = pl.BlockSpec((width, t), lambda i: (0, i))
    out_specs = [
        pl.BlockSpec((mp, 2, cut, t), lambda i: (0, 0, 0, i)),
        pl.BlockSpec((mp, cut, t), lambda i: (0, 0, i)),
        tall,
    ]
    out_shape = [
        jax.ShapeDtypeStruct((mp, 2, cut, length), BF16),
        jax.ShapeDtypeStruct((mp, cut, length), BF16),
        jax.ShapeDtypeStruct((length, width), BF16),
    ]
    if natural:
        out_specs.insert(0, flat)
        out_shape.insert(0, jax.ShapeDtypeStruct((width, length), F32))
    return pl.pallas_call(
        functools.partial(project_body, natural, len(dense), groups),
        grid=(length // t,),
        in_specs=[SCALARS, tall if natural else flat, whole(gain), whole(bias)] + dense.specs(),
        out_specs=out_specs,
        out_shape=out_shape,
        scratch_shapes=[
            pltpu.VMEM((mp, 2 * cut, width), BF16),
            pltpu.VMEM((mp, cut, width), BF16),
        ],
        compiler_params=params(),
        name="project",
    )(place, x, gain, bias, *dense.arrays)


def ff_chunks(refs):
    mp, rows, width = refs[0].shape
    part = rows // 2
    step = min(mp, width // part)
    size = step * part
    for p, ref in enumerate(refs):
        for j in range(mp // step):
            begin = (p * (mp // step) + j) * size
            yield ref, slice(j * step, (j + 1) * step), part, slice(begin, begin + size)


def forward_body(natural, ways, s_ref, c_ref, g_ref, wo_ref, gain_ref, bias_ref, *rest):
    ff, rest = rest[:ways], rest[ways:]
    s1_ref, s2_ref, h_ref, d_ref, n_ref, gated_ref, wo_t, down_t = rest
    width = ff[0].shape[-1]

    @pl.when(pl.program_id(0) == 0)
    def _():
        wo_t[...] = transposed(wo_ref[...]).astype(BF16)
        for ref, blocks, part, units in ff_chunks(ff):
            block = ref[blocks, part:, :].reshape(units.stop - units.start, width)
            down_t[:, units] = transposed(block).astype(BF16)

    gated = (g_ref[...].astype(F32) * c_ref[...].astype(F32)).astype(BF16)
    gated_ref[...] = gated
    s1 = s_ref[...] + jnp.dot(wo_t[...], gated, preferred_element_type=F32)
    s1_ref[...] = s1
    unit, _ = standardise(s1)
    normed = unit * gain_ref[...] + bias_ref[...]
    n_ref[...] = transposed(normed).astype(BF16)
    normed = normed.astype(BF16)
    total = s1
    for ref, blocks, part, units in ff_chunks(ff):
        up = ref[blocks, 0:part, :].reshape(units.stop - units.start, width)
        hidden, slope = gelu_pair(jnp.dot(up, normed, preferred_element_type=F32))
        hidden = hidden.astype(BF16)
        h_ref[units, :] = hidden
        d_ref[units, :] = slope.astype(BF16)
        total = total + jnp.dot(down_t[:, units], hidden, preferred_element_type=F32)
    s2_ref[...] = transposed(total) if natural else total


def forward_block(natural, stream, conv_two, gate_two, w_out, ff, gain, bias):
    width, length = stream.shape
    channels = w_out.shape[0]
    hidden = len(ff) * ff.arrays[0].shape[0] * ff.rows // 2
    t = token_tile(length)
    tall = pl.BlockSpec((t, width), lambda i: (i, 0))
    flat = pl.BlockSpec((width, t), lambda i: (0, i))
    chan = pl.BlockSpec((channels, t), lambda i: (0, i))
    high = pl.BlockSpec((hidden, t), lambda i: (0, i))
    last = (length, width) if natural else (width, length)
    return pl.pallas_call(
        functools.partial(forward_body, natural, len(ff)),
        grid=(length // t,),
        in_specs=[flat, chan, chan, whole(w_out), whole(gain), whole(bias)] + ff.specs(),
        out_specs=[flat, tall if natural else flat, high, high, tall, chan],
        out_shape=[
            jax.ShapeDtypeStruct((width, length), F32),
            jax.ShapeDtypeStruct(last, F32),
            jax.ShapeDtypeStruct((hidden, length), BF16),
            jax.ShapeDtypeStruct((hidden, length), BF16),
            jax.ShapeDtypeStruct((length, width), BF16),
            jax.ShapeDtypeStruct((channels, length), BF16),
        ],
        scratch_shapes=[pltpu.VMEM((width, channels), BF16), pltpu.VMEM((width, hidden), BF16)],
        compiler_params=params(),
        name="forward_block",
    )(stream, conv_two, gate_two, w_out, gain, bias, *ff.arrays)


def backward_body(natural, ways, gs_ref, d_ref, s1_ref, c_ref, g_ref, wo_ref, gain_ref, *rest):
    ff, rest = rest[:ways], rest[ways:]
    pre_ref, gs1_ref, gc_ref, two_ref, dm_ref, do_ref, gain_out, bias_out, up_n = rest
    width = ff[0].shape[-1]

    @pl.when(pl.program_id(0) == 0)
    def _():
        gain_out[...] = jnp.zeros_like(gain_out)
        bias_out[...] = jnp.zeros_like(bias_out)
        for ref, blocks, part, units in ff_chunks(ff):
            block = ref[blocks, 0:part, :].reshape(units.stop - units.start, width)
            up_n[:, units] = transposed(block).astype(BF16)

    if natural:
        dm_ref[...] = gs_ref[...]
        grad = transposed(gs_ref[...])
    else:
        grad = gs_ref[...]
        dm_ref[...] = transposed(grad).astype(BF16)
    dm = grad.astype(BF16)
    total = None
    for ref, blocks, part, units in ff_chunks(ff):
        down = ref[blocks, part:, :].reshape(units.stop - units.start, width)
        pre = jnp.dot(down, dm, preferred_element_type=F32) * d_ref[units, :].astype(F32)
        pre = pre.astype(BF16)
        pre_ref[units, :] = pre
        total = add(total, jnp.dot(up_n[:, units], pre, preferred_element_type=F32))
    back, gain_part, bias_part = standardise_back(total, gain_ref[...], s1_ref[...])
    gain_out[...] += gain_part
    bias_out[...] += bias_part
    grad = grad + back
    gs1_ref[...] = grad
    do_ref[...] = transposed(grad).astype(BF16)
    gated = jnp.dot(wo_ref[...], grad.astype(BF16), preferred_element_type=F32)
    gated = gated.astype(BF16).astype(F32)
    gc_ref[...] = (gated * g_ref[...].astype(F32)).astype(BF16)
    two_ref[...] = (gated * c_ref[...].astype(F32)).astype(BF16)


def backward_block(natural, grad, slope, s1, conv_two, gate_two, w_out, ff, gain):
    width, length = s1.shape
    channels = w_out.shape[0]
    hidden = slope.shape[0]
    t = token_tile(length)
    tall = pl.BlockSpec((t, width), lambda i: (i, 0))
    flat = pl.BlockSpec((width, t), lambda i: (0, i))
    chan = pl.BlockSpec((channels, t), lambda i: (0, i))
    high = pl.BlockSpec((hidden, t), lambda i: (0, i))
    column = pl.BlockSpec((width, 1), lambda i: (0, 0))
    return pl.pallas_call(
        functools.partial(backward_body, natural, len(ff)),
        grid=(length // t,),
        in_specs=[tall if natural else flat, high, flat, chan, chan]
        + [whole(w_out), whole(gain)]
        + ff.specs(),
        out_specs=[high, flat, chan, chan, tall, tall, column, column],
        out_shape=[
            jax.ShapeDtypeStruct((hidden, length), BF16),
            jax.ShapeDtypeStruct((width, length), F32),
            jax.ShapeDtypeStruct((channels, length), BF16),
            jax.ShapeDtypeStruct((channels, length), BF16),
            jax.ShapeDtypeStruct((length, width), BF16),
            jax.ShapeDtypeStruct((length, width), BF16),
            jax.ShapeDtypeStruct((width, 1), F32),
            jax.ShapeDtypeStruct((width, 1), F32),
        ],
        scratch_shapes=[pltpu.VMEM((width, hidden), BF16)],
        compiler_params=params(),
        name="backward_block",
    )(grad, slope, s1, conv_two, gate_two, w_out, gain, *ff.arrays)


def unproject_body(natural, ways, groups, place_ref, gm_ref, two_ref, s_ref, gs_ref, gain_ref, *rest):
    dense, rest = rest[:ways], rest[ways:]
    out_ref, gain_out, bias_out, pair_t, value_t = rest
    mp, cut, t = two_ref.shape
    width = dense[0].shape[-1]

    @pl.when(pl.program_id(0) == 0)
    def _():
        gain_out[...] = jnp.zeros_like(gain_out)
        bias_out[...] = jnp.zeros_like(bias_out)

        def body(pair, value):
            rows = by_channel(pair, groups).reshape(mp * 2 * cut, width)
            pair_t[...] = transposed(rows).astype(BF16)
            rows = by_channel(value, groups).reshape(mp * cut, width)
            value_t[...] = transposed(rows).astype(BF16)

        first(place_ref[0] == 0, dense, cut, body)

    pair = jnp.concatenate([gm_ref[:, 0:1], two_ref[...][:, None]], axis=1)
    grad = jnp.dot(pair_t[...], pair.reshape(mp * 2 * cut, t), preferred_element_type=F32)
    value = gm_ref[:, 1].reshape(mp * cut, t)
    grad = grad + jnp.dot(value_t[...], value, preferred_element_type=F32)
    back, gain_part, bias_part = standardise_back(grad, gain_ref[...], s_ref[...])
    gain_out[...] += gain_part
    bias_out[...] += bias_part
    result = gs_ref[...] + back
    out_ref[...] = transposed(result) if natural else result


def unproject(natural, groups, place, grad_mixed, grad_two, dense, stream, grad, gain):
    width, length = stream.shape
    mp, cut, _ = grad_two.shape
    t = token_tile(length)
    tall = pl.BlockSpec((t, width), lambda i: (i, 0))
    flat = pl.BlockSpec((width, t), lambda i: (0, i))
    column = pl.BlockSpec((width, 1), lambda i: (0, 0))
    last = (length, width) if natural else (width, length)
    return pl.pallas_call(
        functools.partial(unproject_body, natural, len(dense), groups),
        grid=(length // t,),
        in_specs=[
            SCALARS,
            pl.BlockSpec((mp, 2, cut, t), lambda i: (0, 0, 0, i)),
            pl.BlockSpec((mp, cut, t), lambda i: (0, 0, i)),
            flat,
            flat,
            whole(gain),
        ]
        + dense.specs(),
        out_specs=[tall if natural else flat, column, column],
        out_shape=[
            jax.ShapeDtypeStruct(last, F32),
            jax.ShapeDtypeStruct((width, 1), F32),
            jax.ShapeDtypeStruct((width, 1), F32),
        ],
        scratch_shapes=[
            pltpu.VMEM((width, mp * 2 * cut), BF16),
            pltpu.VMEM((width, mp * cut), BF16),
        ],
        compiler_params=params(),
        name="unproject",
    )(place, grad_mixed, grad_two, stream, grad, gain, *dense.arrays)


GROUP = 8


def spread(out, rows, low, values):
    count = values.shape[0]
    for i in range(count):
        out[i ^ low, rows, :] = values[i]


def by_way(way, ways, a, b):
    if ways == 1:
        return jnp.concatenate([a, b], axis=1)
    return jnp.where(way == 0, a, b)


def early_body(ways, _, place_ref, pre_ref, h_ref, two_ref, gated_ref, n1_ref, n2_ref, dm_ref, do_ref, *outs):
    low = place_ref[1] % GROUP
    width = n2_ref.shape[-1]
    _, count, part, length = pre_ref.shape
    cut = two_ref.shape[1]
    a = jnp.dot(
        two_ref[...].reshape(count * cut, length), n1_ref[...], preferred_element_type=F32
    ).astype(BF16).reshape(count, cut, width)
    b = jnp.dot(
        gated_ref[...].reshape(count * cut, length), do_ref[...], preferred_element_type=F32
    ).astype(BF16).reshape(count, cut, width)
    for w in range(ways):
        rows = by_way(place_ref[0] ^ w, ways, a, b)
        spread(outs[w], slice(2 * part, 2 * part + rows.shape[1]), low, rows)
        for ref, right, begin in ((pre_ref, n2_ref, 0), (h_ref, dm_ref, part)):
            y = jnp.dot(
                ref[w].reshape(count * part, length), right[...], preferred_element_type=F32
            )
            y = y.astype(BF16).reshape(count, part, width)
            spread(outs[w], slice(begin, begin + part), low, y)


def grad_call(body, name, ways, place, mp, rows, width, plain, mixed, fixed, before=()):
    def spec(a, mixed):
        if not mixed:
            shape = (a.shape[0], GROUP) + a.shape[2:]
            return pl.BlockSpec(shape, lambda i, place: (0, i ^ (place[1] // GROUP), 0, 0))
        shape = (GROUP, None) + a.shape[2:]
        zeros = (0,) * (a.ndim - 2)
        runs = a.shape[0] // GROUP

        def index(i, place):
            run = i ^ (place[1] // GROUP)
            return (lax.rem(run, runs), run // runs) + zeros

        return pl.BlockSpec(shape, index)

    def kept(a):
        return pl.BlockSpec(a.shape, lambda i, place: (0, 0), pipeline_mode=pl.Buffered(1))

    out = pl.BlockSpec((GROUP, rows, width), lambda i, place: (i, 0, 0))
    return pl.pallas_call(
        functools.partial(body, ways, len(before)),
        grid_spec=pltpu.PrefetchScalarGridSpec(
            num_scalar_prefetch=1,
            grid=(mp // GROUP,),
            in_specs=[spec(a, False) for a in plain]
            + [spec(a, True) for a in mixed]
            + [kept(a) for a in fixed]
            + [pl.BlockSpec(memory_space=pl.ANY)] * len(before),
            out_specs=[out] * ways,
        ),
        out_shape=[jax.ShapeDtypeStruct((mp, rows, width), BF16)] * ways,
        compiler_params=params(),
        name=name,
    )(place, *plain, *mixed, *fixed, *before)


def early_grads(ways, groups, place, pre, hidden, two, gated, n1, n2, dm, do):
    mp, cut, length = two.shape
    shape = (ways, mp, pre.shape[0] // (ways * mp), length)
    rows = 2 * shape[2] + 2 * cut // ways
    plain = [pre.reshape(shape), hidden.reshape(shape)]
    mixed = [x.reshape(mp // groups, groups, cut, length) for x in (two, gated)]
    width = n1.shape[1]
    return grad_call(
        early_body, "early_grads", ways, place, mp, rows, width, plain, mixed, [n1, n2, dm, do]
    )


def late_body(ways, before, place_ref, gm_ref, n1_ref, *outs):
    outs = outs[before:]
    low = place_ref[1] % GROUP
    count, _, cut, length = gm_ref.shape
    width = n1_ref.shape[-1]
    a, b = (
        jnp.dot(
            gm_ref[:, j].reshape(count * cut, length), n1_ref[...], preferred_element_type=F32
        ).astype(BF16).reshape(count, cut, width)
        for j in range(2)
    )
    for w in range(ways):
        rows = by_way(place_ref[0] ^ w, ways, a, b)
        spread(outs[w], slice(0, rows.shape[1]), low, rows)


def late_grads(ways, groups, place, grad_mixed, n1, before=()):
    mp, _, cut, length = grad_mixed.shape
    rows = 2 * cut // ways
    width = n1.shape[1]
    mixed = [grad_mixed.reshape(mp // groups, groups, 2, cut, length)]
    return grad_call(
        late_body, "late_grads", ways, place, mp, rows, width, [], mixed, [n1], before
    )


def together(*arrays):
    return lax.optimization_barrier(arrays)


def flip(x, axis, size, bit):
    return lax.ppermute(x, axis, [(i, i ^ bit) for i in range(size)])


def butterfly(x, sizes):
    for axis, size in sizes:
        bit = 1
        while bit < size:
            x = x + flip(x, axis, size, bit)
            bit *= 2
    return x


def stage_order(mp, swapped):
    bits = list(range(mp.bit_length() - 1))
    first = [1, 0] if swapped else [0, 1]
    return first + bits[2:]


def total(parts):
    value = parts[0].astype(F32)
    for part in parts[1:]:
        value = value + part.astype(F32)
    return value


class Hop:
    def __init__(self, x, axis, size, bit):
        self.args = x, axis, size, bit

    def start(self):
        return flip(*self.args)


def scatter_chain(terms, mp, order):
    bits = mp.bit_length() - 1
    terms = [t.reshape((2,) * bits + t.shape[1:]) for t in terms]
    left = list(range(bits - 1, -1, -1))
    for bit in order:
        axis = left.index(bit)
        left.remove(bit)
        take = lambda t, k: lax.index_in_dim(t, k, axis, keepdims=False)
        sent = total([take(t, 1) for t in terms]).astype(BF16)
        got = yield Hop(sent, "mp", mp, 1 << bit)
        terms = [take(t, 0) for t in terms] + [got]
    return total(terms)


def gather_chain(x, mp, order):
    me = lax.axis_index("mp")
    done = []
    for bit in order:
        got = yield Hop(x, "mp", mp, 1 << bit)
        upper = (me >> bit) % 2 == 1
        axis = sum(b > bit for b in done)
        x = jnp.stack([jnp.where(upper, got, x), jnp.where(upper, x, got)], axis=axis)
        done.append(bit)
    return x.reshape((mp,) + x.shape[len(done) :])


def chip_chain(pieces, dp):
    if len(pieces) == 1:
        return pieces
    got = yield Hop(pieces[1], "dp", dp, 1)
    return [pieces[0], got]


def spread_chain(x, ways, dp):
    if ways == 1:
        x = yield from sum_chain(x, [("dp", dp)])
        return (x.astype(BF16),)
    x = x.astype(BF16)
    got = yield Hop(x, "dp", dp, 1)
    zero = lax.axis_index("dp") == 0
    return jnp.where(zero, x, got), jnp.where(zero, got, x)


def sum_chain(x, sizes):
    for axis, size in sizes:
        bit = 1
        while bit < size:
            x = x + (yield Hop(x, axis, size, bit))
            bit *= 2
    return x


class Chains:
    def __init__(self):
        self.waiting, self.results = {}, {}

    def add(self, name, chain):
        self.step(name, chain, None)

    def step(self, name, chain, value):
        try:
            self.waiting[name] = chain, chain.send(value)
        except StopIteration as end:
            self.waiting.pop(name, None)
            self.results[name] = end.value

    def operands(self):
        return [hop.args[0] for _, hop in self.waiting.values()]

    def start(self):
        names = list(self.waiting)
        return names, [self.waiting[n][1].start() for n in names]

    def finish(self, started, *others):
        names, got = started
        tied = together(*got, *others)
        for name, value in zip(names, tied):
            self.step(name, self.waiting[name][0], value)
        return tied[len(names) :]


def gathered_sum(terms, whole_rows, dp):
    y = lax.psum_scatter(total(terms).astype(BF16), "mp", scatter_dimension=0, tiled=True)[0]
    if whole_rows:
        y = butterfly(y.astype(F32), [("dp", dp)]).astype(BF16)
    return y


def program(dp, mp, inputs, cotangent, norm_gain, norm_bias, in_weight, kernels, *rest):
    out_weight, up_weight, down_weight, taps_kept = rest
    layers = in_weight.shape[0]
    groups, chunk, width = inputs.shape
    peers = mp // groups
    shard, hidden = in_weight.shape[3], up_weight.shape[2]
    length = groups * chunk
    cut = -(-shard // 16) * 16
    ways = 2 if dp == 2 and shard == cut and hidden % 32 == 0 else 1
    part = hidden // ways
    dense_rows = 4 * cut // ways
    me, way = lax.axis_index("mp"), lax.axis_index("dp")
    place = jnp.stack([way, me]).astype(jnp.int32)
    still = jnp.stack([way, jnp.zeros_like(me)]).astype(jnp.int32)
    zero_half = me // peers == 0
    swap = [(i, (i + peers) % mp) for i in range(mp)]
    halves = [[h * peers + q for q in range(peers)] for h in range(groups)]

    def ordered(own, got):
        return jnp.stack([jnp.where(zero_half, own, got), jnp.where(zero_half, got, own)])

    def pick(x):
        return jnp.where(zero_half, x[0], x[1]), jnp.where(zero_half, x[1], x[0])

    def to_one_sequence(x):
        own, other = pick(x)
        return ordered(own, lax.ppermute(other, "mp", swap)).reshape(length, width)

    def to_two_sequences(x):
        own, other = pick(x.reshape(groups, chunk, width))
        got = lax.ppermute(other.astype(BF16), "mp", swap)
        return ordered(own, got.astype(F32))

    def exchange(x):
        return lax.all_to_all(
            x, "mp", split_axis=0, concat_axis=0, tiled=True, axis_index_groups=halves
        )

    def widen(x, axis):
        pads = [(0, 0)] * x.ndim
        pads[axis] = (0, cut - shard)
        return x if cut == shard else jnp.pad(x, pads)

    dense = [jnp.transpose(in_weight[:, :, j], (0, 2, 1)) for j in range(3)] + [out_weight]
    dense = jnp.concatenate([widen(d, 1) for d in dense], axis=1)
    up = jnp.transpose(up_weight, (0, 2, 1))

    def my_rows(x, rows):
        return lax.dynamic_slice_in_dim(x, way * rows, rows, 1) if ways > 1 else x

    dense = my_rows(dense, dense_rows)
    ff = jnp.concatenate([my_rows(up, part), my_rows(down_weight, part)], axis=1)

    def gather(x):
        x = lax.all_gather(x, "mp", axis=0)
        return [x, flip(x, "dp", dp, 1)] if ways > 1 else [x]

    def gathered(x):
        return lax.all_gather(x, "mp", axis=0)

    def shared(x):
        return [x, flip(x, "dp", dp, 1)] if ways > 1 else [x]

    stream = to_one_sequence(inputs)
    def out_matrix(pieces):
        begin = pieces.begin + dense_rows - cut
        rows = [a[:, begin : begin + cut] for a in pieces.arrays]
        rows = jnp.where(way == 1, rows[0], rows[1]) if ways > 1 else rows[0]
        rows = rows.reshape(groups, peers, cut, width)
        return jnp.swapaxes(rows, 0, 1).reshape(mp * cut, width)

    keep = jnp.arange(kernels.shape[-1])[None, :] < taps_kept[:, None]
    kept = jnp.where(keep[:, None, None, :], kernels, jnp.zeros_like(kernels))
    kept = widen(kept, 2)
    taps = []

    chains = Chains()
    for i in range(2):
        rows = ff[0, i * part : (i + 1) * part]
        chains.add(i, gather_chain(rows, mp, stage_order(mp, i)[::-1]))
    chains.finish(chains.start())
    dense_mine = gathered(dense[0])
    dense_mine, stream = chains.finish(chains.start(), dense_mine, stream)
    dense_all = [Pieces(shared(dense_mine), 0, dense_rows)]
    ff_all = []

    gains = norm_gain[..., None]
    biases = norm_bias[..., None]
    saved, out_all = [], []
    for layer in range(layers):
        natural = layer == 0
        more = layer + 1 < layers
        if natural:
            started = chains.start()
        got = project(
            natural,
            groups,
            place,
            stream,
            dense_all[layer],
            gains[layer, 0],
            biases[layer, 0],
            cut,
        )
        if natural:
            stream, got = got[0], got[1:]
        operand, gate_two, normed_one = got
        out_all.append(out_matrix(dense_all[layer]))
        if natural:
            (operand,) = chains.finish(started, operand)
            started = chains.start()
        if more:
            mine, operand = together(dense[layer + 1], operand)
            dense_mine = gathered(mine)
        if natural:
            mine, operand = together(kept[layer], operand)
            got_taps = lax.ppermute(mine, "mp", swap)
        gates = exchange(operand.reshape(peers, groups, 2, cut, length))
        if natural:
            while len(chains.waiting):
                gates, got_taps = chains.finish(started, gates, got_taps)
                started = chains.start()
            ff_mine = jnp.concatenate([chains.results.pop(i) for i in range(2)], axis=1)
            ff_pair = shared(ff_mine)
        taps.append(ordered(kept[layer], got_taps))
        conv_two, conv_one, carried = mix(gates, taps[layer])
        if natural:
            conv_two, *ff_pair = together(conv_two, *ff_pair)
        else:
            ff_mine, conv_two = together(ff_mine, conv_two)
            ff_pair = shared(ff_mine)
        ff_all.append(Pieces(ff_pair, 0, 2 * part))
        if more:
            mine, conv_two = together(ff[layer + 1], conv_two)
            ff_mine = gathered(mine)
        conv_two = exchange(conv_two).reshape(mp * cut, length)
        if natural:
            grad, conv_two = together(cotangent, conv_two)
            grad = to_one_sequence(grad)
        if more:
            dense_mine, mine, conv_two = together(dense_mine, kept[layer + 1], conv_two)
            got_taps = lax.ppermute(mine, "mp", swap)
            dense_all.append(Pieces(shared(dense_mine), 0, dense_rows))
        gate_two = gate_two.reshape(mp * cut, length)
        s1, s2, active, slope, normed_two, gated = forward_block(
            layer == layers - 1,
            stream,
            conv_two,
            gate_two,
            out_all[layer],
            ff_all[layer],
            gains[layer, 1],
            biases[layer, 1],
        )
        if more:
            s2, grad, got_taps, *arrays = together(s2, grad, got_taps, *dense_all[-1].arrays)
            dense_all[-1].arrays = arrays
        saved.append(
            (stream, normed_one, gates, conv_one, carried, conv_two, gate_two)
            + (s1, active, slope, normed_two, gated)
        )
        stream = s2
    own_output, other = pick(stream.reshape(groups, chunk, width))
    got_output = lax.ppermute(other.astype(BF16), "mp", swap)

    gain_rows, bias_rows = [None] * layers, [None] * layers
    early_out, late_out, dks = [None] * layers, [None] * layers, [None] * layers
    later = None
    for layer in reversed(range(layers)):
        (s0, normed_one, gates, conv_one, carried, conv_two, gate_two) = saved[layer][:7]
        (s1, active, slope, normed_two, gated) = saved[layer][7:]
        pre, grad, grad_conv, grad_two, dm, do, gain_two, bias_two = backward_block(
            layer == layers - 1,
            grad,
            slope,
            s1,
            conv_two,
            gate_two,
            out_all[layer],
            ff_all[layer],
            gains[layer, 1],
        )
        waiting = []
        if later is not None:
            mixed, grad_conv = together(later[0], grad_conv)
            waiting = late_grads(ways, groups, place, mixed, later[1])
        grad_conv = exchange(grad_conv.reshape(peers, groups, cut, length))
        grad_two = grad_two.reshape(mp, cut, length)
        where_to = still if layer else place
        early = early_grads(
            ways, groups, where_to, pre, active, grad_two, gated, normed_one, normed_two, dm, do
        )
        if layer == layers - 1:
            grad_conv, got_output = together(grad_conv, got_output)
        else:
            grad_conv, got_dk = together(grad_conv, got_dk)
            dks[layer + 1] = own_dk.astype(F32) + got_dk.astype(F32)
        grad_conv, *both = together(grad_conv, *early, *waiting)
        early, waiting = both[:ways], both[ways:]
        chains.add("early", chip_chain(early, dp))
        if later is not None:
            chains.add("waiting", chip_chain(waiting, dp))
        started = chains.start()
        grad_mixed, dk = unmix(grad_conv, gates, conv_one, carried, taps[layer])
        (grad_mixed,) = chains.finish(started, grad_mixed)
        grad_mixed = exchange(grad_mixed).reshape(mp, 2, cut, length)
        own_dk, other_dk = pick(dk.astype(BF16))
        got_dk = lax.ppermute(other_dk, "mp", swap)
        early = chains.results["early"]
        gain_rows[layer], bias_rows[layer] = [None, gain_two], [None, bias_two]
        if layer:
            early_out[layer] = gathered_sum(early, ways == 1, dp)
            if later is not None:
                late_out[layer + 1] = gathered_sum(chains.results["waiting"], ways == 1, dp)
            later = grad_mixed, normed_one
        else:
            if later is not None:
                pairs = zip(early, chains.results["waiting"])
                early = [jnp.concatenate(pair, axis=1) for pair in pairs]
            rows = early[0].shape[1]
            middle = rows // 32 * 16
            spans = ((0, middle), (middle, rows))
            for i, (a, b) in enumerate(spans):
                terms = [e[:, a:b] for e in early]
                chains.add(i, scatter_chain(terms, mp, stage_order(mp, i)))
            before = chains.operands()
            started = chains.start()
            late = late_grads(ways, groups, place, grad_mixed, normed_one, before)
            got_dk, grad_mixed, *late = chains.finish(started, got_dk, grad_mixed, *late)
            dks[0] = own_dk.astype(F32) + got_dk.astype(F32)
            dk = jnp.stack(dks)
            chains.add("late", chip_chain(late, dp))
            chains.add("dk", sum_chain(dk.astype(BF16).astype(F32), [("dp", dp)]))
            started = chains.start()
        grad, gain_one, bias_one = unproject(
            layer == 0,
            groups,
            place,
            grad_mixed,
            grad_two,
            dense_all[layer],
            s0,
            grad,
            gains[layer, 0],
        )
        gain_rows[layer][0], bias_rows[layer][0] = gain_one, bias_one
    grad, gain_rows[0][0] = chains.finish(started, grad, gain_rows[0][0])
    own, other = pick(grad.reshape(groups, chunk, width))
    swapped = lax.ppermute(other.astype(BF16), "mp", swap)
    norms = jnp.stack([jnp.stack([jnp.stack(r) for r in rows]) for rows in (gain_rows, bias_rows)])
    chains.add("norms", sum_chain(norms[..., 0], [("dp", dp), ("mp", mp)]))
    chains.add("late", scatter_chain(chains.results.pop("late"), mp, stage_order(mp, 0)))
    while chains.waiting:
        chains.finish(chains.start())
        if 0 in chains.results and 1 in chains.results:
            rest = jnp.concatenate([chains.results.pop(i) for i in range(2)], axis=0)
            chains.add("rest", spread_chain(rest, ways, dp))
        if "late" in chains.results:
            chains.add("last", spread_chain(chains.results.pop("late"), ways, dp))
    input_grad = ordered(own, swapped.astype(F32))
    output = ordered(own_output, got_output.astype(F32))
    dk = chains.results["dk"][:, :, :shard]
    tap_out = jnp.where(keep[:, None, None, :], dk, 0.0)
    norms = chains.results["norms"]

    def both_ways(x):
        if ways == 1:
            return (x.astype(F32),)
        got = flip(x, "dp", dp, 1)
        pair = jnp.where(way == 0, x, got), jnp.where(way == 0, got, x)
        return tuple(p.astype(F32) for p in pair)

    rest = [x.astype(F32) for x in chains.results["rest"]]
    tall = 2 * part + 2 * cut // ways
    early_out = [[r[:tall] for r in rest]] + [both_ways(e) for e in early_out[1:]]
    late_out[0] = [x.astype(F32) for x in chains.results["last"]]
    if layers > 1:
        late_out[1] = [r[tall:] for r in rest]
    late_out[2:] = [both_ways(x) for x in late_out[2:]]

    parts = [[] for _ in range(6)]
    for early, late in zip(early_out, late_out):
        if ways == 1:
            e, l = early[0], late[0]
            up, down = e[:part], e[part : 2 * part]
            two, out = e[2 * part : 2 * part + cut], e[2 * part + cut :]
            one, value = l[:cut], l[cut:]
        else:
            up = jnp.concatenate([e[:part] for e in early], axis=0)
            down = jnp.concatenate([e[part : 2 * part] for e in early], axis=0)
            two, out = early[0][2 * part :], early[1][2 * part :]
            one, value = late
        for store, x in zip(parts, (one, two, value, out, up, down)):
            store.append(x)
    one, two, value, out, up, down = (jnp.stack(p) for p in parts)
    in_out = jnp.stack([one, two, value], axis=1)[:, :, :shard]
    return (
        output,
        input_grad,
        norms[0],
        norms[1],
        jnp.transpose(in_out, (0, 3, 1, 2)),
        tap_out,
        out[:, :shard],
        jnp.transpose(up, (0, 2, 1)),
        down,
    )


def solution(mesh):
    sizes = dict(mesh.shape)
    specs = (
        P("dp", "mp", None),
        P("dp", "mp", None),
        P(),
        P(),
        P(None, None, None, "mp"),
        P(None, None, "mp", None),
        P(None, "mp", None),
        P(None, None, "mp"),
        P(None, "mp", None),
    )
    return jax.shard_map(
        functools.partial(program, sizes["dp"], sizes["mp"]),
        mesh=mesh,
        in_specs=specs + (P(),),
        out_specs=specs,
        check_vma=False,
    )
```

```python
import functools
import math

import jax
import jax.numpy as jnp
import ml_dtypes
import numpy as np
from jax import lax
from jax.experimental import pallas as pl
from jax.experimental.pallas import tpu as pltpu
from jax.sharding import PartitionSpec as P

EPS = 1e-05
LANES = 128
RADIX = 32
HALF = RADIX // 2
FREQS = HALF + 1
POINTS = LANES * RADIX
SPAN = POINTS // 2
BF16 = jnp.bfloat16
F32 = jnp.float32
VMEM_BYTES = 56 * 2**20
PASSES = 1


def params():
    return pltpu.CompilerParams(vmem_limit_bytes=VMEM_BYTES)


def whole(array):
    rank = array.ndim
    return pl.BlockSpec(array.shape, lambda *_: (0,) * rank, pipeline_mode=pl.Buffered(1))


def add(a, b):
    if a is None:
        return b
    return a if b is None else a + b


def sub(a, b):
    if b is None:
        return a
    return -b if a is None else a - b


def tidy(v):
    for exact in (0.0, 1.0, -1.0):
        if abs(v - exact) < 1e-12:
            return exact
    return v


def scaled(v, factor):
    if v is None or factor == 0.0:
        return None
    if factor == 1.0:
        return v
    return -v if factor == -1.0 else v * factor


def turn(z, angle):
    re, im = z
    c, s = tidy(math.cos(angle)), tidy(math.sin(angle))
    if re is not None and im is not None and abs(abs(c) - abs(s)) < 1e-12:
        r = math.copysign(abs(c), c)
        if c * s > 0:
            return ((re - im) * r, (re + im) * r)
        return ((re + im) * r, (im - re) * r)
    return (sub(scaled(re, c), scaled(im, s)), add(scaled(im, c), scaled(re, s)))


def analyse(x):
    n = len(x)
    if n == 1:
        return [(x[0], None)]
    even, odd = analyse(x[0::2]), analyse(x[1::2])
    if n == 2:
        return [(add(even[0][0], odd[0][0]), None), (sub(even[0][0], odd[0][0]), None)]
    half, quarter = n // 2, n // 4
    out = [None] * (half + 1)
    for k in range(quarter + 1):
        t = turn(odd[k], -2 * math.pi * k / n)
        out[k] = (add(even[k][0], t[0]), add(even[k][1], t[1]))
        if k != quarter:
            out[half - k] = (sub(even[k][0], t[0]), sub(t[1], even[k][1]))
    return out


def synthesise(x, n, upper):
    if n == 2:
        return [sub(x[0][0], x[1][0]) if upper else add(x[0][0], x[1][0])]
    half, quarter = n // 2, n // 4
    even, odd = [], []
    for k in range(quarter + 1):
        a, b = x[k], x[half - k]
        if k == 0:
            even.append((add(a[0], b[0]), None))
            odd.append((sub(a[0], b[0]), None))
        elif k == quarter:
            even.append((a[0] * 2.0, None))
            odd.append((a[1] * -2.0, None))
        else:
            even.append((add(a[0], b[0]), sub(a[1], b[1])))
            odd.append(turn((sub(a[0], b[0]), add(a[1], b[1])), 2 * math.pi * k / n))
    out = [None] * half
    out[0::2] = synthesise(even, half, upper)
    out[1::2] = synthesise(odd, half, upper)
    return out


def split_bf16(matrix):
    matrix = matrix.astype(np.float32)
    high = matrix.astype(ml_dtypes.bfloat16)
    low = (matrix - high.astype(np.float32)).astype(ml_dtypes.bfloat16)
    return jnp.asarray(np.stack([high, low][: 1 if PASSES == 1 else 2]))


def tables():
    j = np.arange(LANES)
    angle = 2 * np.pi * np.outer(j, j) / LANES
    c, s = np.cos(angle), np.sin(angle)
    twist = 2 * np.pi * np.outer(np.arange(FREQS), j) / POINTS
    return [
        split_bf16(np.block([[c, -s], [s, c]])),
        split_bf16(np.block([[c, s], [-s, c]]) / POINTS),
        jnp.asarray(np.cos(twist), F32),
        jnp.asarray(np.sin(twist), F32),
    ]


def lane_product(a, matrix):
    high = a.astype(BF16)
    y = jnp.dot(high, matrix[0], preferred_element_type=F32)
    if PASSES > 1:
        y = y + jnp.dot(high, matrix[1], preferred_element_type=F32)
    if PASSES > 2:
        low = (a - high.astype(F32)).astype(BF16)
        y = y + jnp.dot(low, matrix[0], preferred_element_type=F32)
    return y


class Convolver:
    def __init__(self, sources, groups, pieces, blocks, rows, refs):
        self.sources, self.groups, self.pieces = sources, groups, pieces
        self.blocks, self.rows = blocks, rows
        self.forward, self.backward, self.cos, self.sin, self.left, self.right, self.freq = refs

    def places(self):
        for i in range(self.sources * self.groups * self.pieces):
            chunk, piece = divmod(i, self.pieces)
            group, source = divmod(chunk, self.sources)
            begin = (group * self.pieces + piece) * LANES
            yield i, source, slice(begin, begin + LANES)

    def load(self, ref, dst):
        for i, source, lanes in self.places():
            dst[i] = ref[source, :, lanes].astype(F32)

    def store(self, src, ref, part=None):
        for i, source, lanes in self.places():
            if part is None:
                ref[source, :, lanes] = src[i].astype(ref.dtype)
            else:
                ref[source, part, :, lanes] = src[i].astype(ref.dtype)

    def subtiles(self):
        return [pl.ds(8 * t, 8) for t in range(self.rows // 8)]

    def spectrum(self, read, count, base):
        for b in range(count):
            for rows in self.subtiles():
                x = analyse([read(b, i, rows) for i in range(HALF)] + [None] * HALF)
                for f, (re, im) in enumerate(x):
                    if f:
                        c, s = self.cos[f : f + 1, :], self.sin[f : f + 1, :]
                        if im is None:
                            re, im = re * c, -(re * s)
                        else:
                            re, im = re * c + im * s, im * c - re * s
                    self.left[b * FREQS + f, rows, 0:LANES] = re
                    self.left[b * FREQS + f, rows, LANES:] = jnp.zeros_like(re) if im is None else im
            y = lane_product(self.stacked(b), self.forward)
            begin = (base + b) * FREQS
            self.freq[begin : begin + FREQS] = y.reshape(FREQS, self.rows, 2 * LANES)

    def stacked(self, b):
        return self.left[b * FREQS : (b + 1) * FREQS].reshape(FREQS * self.rows, 2 * LANES)

    def entry(self, row, rows):
        return self.freq[row, rows, 0:LANES], self.freq[row, rows, LANES:]

    def window(self, base, b, f, rows, ahead):
        re, im = self.entry((base + b) * FREQS + f, rows)
        other = b + 1 if ahead else b - 1
        if not ahead and f % 2:
            re, im = -re, -im
        if 0 <= other < self.blocks:
            ore, oim = self.entry((base + other) * FREQS + f, rows)
            if ahead and f % 2:
                return re - ore, im - oim
            return re + ore, im + oim
        return re, im

    def inverse(self, b, upper, write):
        y = lane_product(self.stacked(b), self.backward)
        begin = b * FREQS
        self.right[begin : begin + FREQS] = y.reshape(FREQS, self.rows, 2 * LANES)
        for rows in self.subtiles():
            parts = []
            for f in range(FREQS):
                re = self.right[begin + f, rows, 0:LANES]
                im = self.right[begin + f, rows, LANES:]
                c, s = self.cos[f : f + 1, :], self.sin[f : f + 1, :]
                if f == 0:
                    parts.append((re, None))
                elif f == HALF:
                    parts.append((re * c - im * s, None))
                else:
                    parts.append((re * c - im * s, im * c + re * s))
            for i, value in enumerate(synthesise(parts, RADIX, upper)):
                write(b, i, rows, value)

    def convolve(self, signal, kernel, ahead, write):
        for b in range(self.blocks):
            for rows in self.subtiles():
                for f in range(FREQS):
                    re, im = self.window(signal, b, f, rows, ahead)
                    kre, kim = self.entry(kernel * FREQS + f, rows)
                    if ahead:
                        pre, pim = re * kre + im * kim, im * kre - re * kim
                    else:
                        pre, pim = re * kre - im * kim, re * kim + im * kre
                    self.left[b * FREQS + f, rows, 0:LANES] = pre
                    self.left[b * FREQS + f, rows, LANES:] = pim
            self.inverse(b, not ahead, write)

    def taps(self, signal, grads, write):
        for rows in self.subtiles():
            for f in range(FREQS):
                re = im = None
                for b in range(self.blocks):
                    gre, gim = self.window(grads, b, f, rows, True)
                    sre, sim = self.entry((signal + b) * FREQS + f, rows)
                    re = add(re, sre * gre + sim * gim)
                    im = add(im, sre * gim - sim * gre)
                self.left[f, rows, 0:LANES] = re
                self.left[f, rows, LANES:] = im
        self.inverse(0, False, write)


def kernel_reader(k_ref, j):
    def read(_, i, rows):
        value = k_ref[j, :, i * LANES : (i + 1) * LANES].astype(F32)
        return value[rows.start : rows.start + rows.size]

    return read


def mix_body(shape, v_ref, g_ref, k_ref, *refs):
    (fwd, bwd, cos, sin, out_ref, one_ref, carried_ref, xs, gs, left, right, freq) = refs
    cv = Convolver(*shape, v_ref.shape[1], (fwd, bwd, cos, sin, left, right, freq))
    n = cv.blocks
    cv.load(v_ref, xs)
    cv.load(g_ref, gs)

    def read(b, i, rows):
        return xs[b * HALF + i, rows, :]

    cv.spectrum(kernel_reader(k_ref, 0), 1, n)
    cv.spectrum(kernel_reader(k_ref, 1), 1, n + 1)
    cv.spectrum(read, n, 0)

    def gate(b, i, rows, value):
        r = b * HALF + i
        xs[r, rows, :] = (gs[r, rows, :] * value).astype(BF16).astype(F32)
        gs[r, rows, :] = value

    cv.convolve(0, n, False, gate)
    one_ref[...] = gs[...].astype(BF16)
    carried_ref[...] = xs[...].astype(BF16)
    cv.spectrum(read, n, 0)

    def keep(b, i, rows, value):
        gs[b * HALF + i, rows, :] = value

    cv.convolve(0, n + 1, False, keep)
    cv.store(gs, out_ref)


def unmix_body(shape, d_ref, v_ref, g_ref, one_ref, carried_ref, k_ref, *refs):
    (fwd, bwd, cos, sin, out_ref, dk_ref, xs, gs, left, right, freq) = refs
    cv = Convolver(*shape, v_ref.shape[1], (fwd, bwd, cos, sin, left, right, freq))
    n = cv.blocks
    cv.load(d_ref, xs)
    cv.load(g_ref, gs)

    def read(b, i, rows):
        return xs[b * HALF + i, rows, :]

    def read_carried(b, i, rows):
        return carried_ref[b * HALF + i].astype(F32)[rows.start : rows.start + rows.size]

    def put(j):
        def write(_, i, rows, value):
            dk_ref[j, rows, i * LANES : (i + 1) * LANES] = value

        return write

    cv.spectrum(kernel_reader(k_ref, 1), 1, 2 * n)
    cv.spectrum(read, n, 0)
    cv.spectrum(read_carried, n, n)
    cv.taps(n, 0, put(1))

    def gate(b, i, rows, value):
        r = b * HALF + i
        xs[r, rows, :] = (gs[r, rows, :] * value).astype(BF16).astype(F32)
        gs[r, rows, :] = value

    cv.convolve(0, 2 * n, True, gate)
    gs[...] = gs[...] * one_ref[...].astype(F32)
    cv.store(gs, out_ref, 0)
    cv.spectrum(read, n, 0)
    cv.load(v_ref, xs)
    cv.spectrum(kernel_reader(k_ref, 0), 1, 2 * n)
    cv.spectrum(read, n, n)
    cv.taps(n, 0, put(0))

    def keep(b, i, rows, value):
        gs[b * HALF + i, rows, :] = value

    cv.convolve(0, 2 * n, True, keep)
    cv.store(gs, out_ref, 1)


def conv_sizes(gates):
    sources, groups, _, shard, length = gates.shape
    tile = 16
    pieces = length // (groups * LANES)
    total = sources * length
    return sources, groups, shard, length, tile, pieces, total // LANES, total // SPAN


def conv_scratch(tile, rows, blocks, spectra):
    return [
        pltpu.VMEM((rows, tile, LANES), F32),
        pltpu.VMEM((rows, tile, LANES), F32),
        pltpu.VMEM((blocks * FREQS, tile, 2 * LANES), F32),
        pltpu.VMEM((blocks * FREQS, tile, 2 * LANES), F32),
        pltpu.VMEM((spectra * FREQS, tile, 2 * LANES), F32),
    ]


def mix(gates, taps):
    q, g, shard, length, tile, pieces, rows, blocks = conv_sizes(gates)
    consts = tables()
    by_source = (q, None, None, tile, length)
    nat = pl.BlockSpec((None, rows, tile, LANES), lambda a, b: (a, 0, b, 0))
    return pl.pallas_call(
        functools.partial(mix_body, (q, g, pieces, blocks)),
        grid=(g, shard // tile),
        in_specs=[
            pl.BlockSpec(by_source, lambda a, b: (0, a, 1, b, 0)),
            pl.BlockSpec(by_source, lambda a, b: (0, a, 0, b, 0)),
            pl.BlockSpec((None, 2, tile, SPAN), lambda a, b: (a, 0, b, 0)),
        ]
        + [whole(c) for c in consts],
        out_specs=[pl.BlockSpec((q, None, tile, length), lambda a, b: (0, a, b, 0)), nat, nat],
        out_shape=[
            jax.ShapeDtypeStruct((q, g, shard, length), BF16),
            jax.ShapeDtypeStruct((g, rows, shard, LANES), BF16),
            jax.ShapeDtypeStruct((g, rows, shard, LANES), BF16),
        ],
        scratch_shapes=conv_scratch(tile, rows, blocks, blocks + 2),
        compiler_params=params(),
        name="mix",
    )(gates, gates, taps, *consts)


def unmix(grads, gates, conv_one, carried, taps):
    q, g, shard, length, tile, pieces, rows, blocks = conv_sizes(gates)
    consts = tables()
    by_source = (q, None, None, tile, length)
    nat = pl.BlockSpec((None, rows, tile, LANES), lambda a, b: (a, 0, b, 0))
    kern = pl.BlockSpec((None, 2, tile, SPAN), lambda a, b: (a, 0, b, 0))
    return pl.pallas_call(
        functools.partial(unmix_body, (q, g, pieces, blocks)),
        grid=(g, shard // tile),
        in_specs=[
            pl.BlockSpec((q, None, tile, length), lambda a, b: (0, a, b, 0)),
            pl.BlockSpec(by_source, lambda a, b: (0, a, 1, b, 0)),
            pl.BlockSpec(by_source, lambda a, b: (0, a, 0, b, 0)),
            nat,
            nat,
            kern,
        ]
        + [whole(c) for c in consts],
        out_specs=[
            pl.BlockSpec((q, None, 2, tile, length), lambda a, b: (0, a, 0, b, 0)),
            kern,
        ],
        out_shape=[
            jax.ShapeDtypeStruct((q, g, 2, shard, length), BF16),
            jax.ShapeDtypeStruct((g, 2, shard, SPAN), F32),
        ],
        scratch_shapes=conv_scratch(tile, rows, blocks, 2 * blocks + 1),
        compiler_params=params(),
        name="unmix",
    )(grads, gates, gates, conv_one, carried, taps, *consts)


def standardise(stream):
    average = jnp.mean(stream, axis=0, keepdims=True)
    centered = stream - average
    inv_std = lax.rsqrt(jnp.mean(centered * centered, axis=0, keepdims=True) + EPS)
    return centered * inv_std, inv_std


def standardise_back(grad, gain, stream):
    unit, inv_std = standardise(stream)
    g = grad * gain
    mean_grad = jnp.mean(g, axis=0, keepdims=True)
    mean_cross = jnp.mean(g * unit, axis=0, keepdims=True)
    back = inv_std * (g - mean_grad - unit * mean_cross)
    gain_part = jnp.sum(grad * unit, axis=1, keepdims=True)
    bias_part = jnp.sum(grad, axis=1, keepdims=True)
    return back, gain_part, bias_part


def transposed(x):
    return jnp.transpose(x.astype(F32))


def gelu_pair(x):
    z = jnp.abs(x) * math.sqrt(0.5)
    t = 1.0 / (1.0 + 0.3275911 * z)
    e = jnp.exp(-(z * z))
    poly = t * (
        0.127414796 + t * (-0.142248368 + t * (0.710706871 + t * (-0.726576014 + t * 0.530702714)))
    )
    tail = poly * e
    phi = jnp.where(x >= 0, 1.0 - tail, tail)
    return x * phi, phi + x * (e * (1.0 / math.sqrt(2 * math.pi)))


def first(axis_is_zero, refs, cut, body):
    if len(refs) == 1:
        body(refs[0].at[:, 0 : 2 * cut], refs[0].at[:, 2 * cut : 3 * cut])
        return

    @pl.when(axis_is_zero)
    def _():
        body(refs[0], refs[1].at[:, 0:cut])

    @pl.when(jnp.logical_not(axis_is_zero))
    def _():
        body(refs[1], refs[0].at[:, 0:cut])


class Pieces:
    def __init__(self, arrays, begins, rows):
        self.arrays, self.begins, self.rows = arrays, begins, rows

    def specs(self):
        mp, _, width = self.arrays[0].shape
        shape = (mp, self.rows, width)
        return [
            pl.BlockSpec(
                shape, lambda *_, at=begin // self.rows: (0, at, 0), pipeline_mode=pl.Buffered(1)
            )
            for begin in self.begins
        ]

    def __len__(self):
        return len(self.arrays)


SCALARS = pl.BlockSpec(memory_space=pltpu.SMEM)


def by_channel(blocks, groups):
    peers = blocks.shape[0] // groups
    order = [h * peers + q for q in range(peers) for h in range(groups)]
    return jnp.concatenate([blocks[m : m + 1] for m in order], axis=0)


def project_body(natural, ways, groups, place_ref, x_ref, gain_ref, bias_ref, *rest):
    dense, rest = rest[:ways], rest[ways:]
    if natural:
        s_ref, op_ref, two_ref, n_ref, pair_w, value_w = rest
        x = transposed(x_ref[...])
        s_ref[...] = x
    else:
        op_ref, two_ref, n_ref, pair_w, value_w = rest
        x = x_ref[...]
    mp, cut, t = two_ref.shape

    @pl.when(pl.program_id(0) == 0)
    def _():
        def body(pair, value):
            pair_w[...] = by_channel(pair, groups)
            value_w[...] = by_channel(value, groups)

        first(place_ref[0] == 0, dense, cut, body)

    unit, _ = standardise(x)
    normed = unit * gain_ref[...] + bias_ref[...]
    n_ref[...] = transposed(normed).astype(BF16)
    normed = normed.astype(BF16)
    width = normed.shape[0]
    y = jnp.dot(
        pair_w[...].reshape(mp * 2 * cut, width), normed, preferred_element_type=F32
    )
    y = y.astype(BF16).reshape(mp, 2, cut, t)
    op_ref[:, 0] = y[:, 0]
    two_ref[...] = y[:, 1]
    y = jnp.dot(value_w[...].reshape(mp * cut, width), normed, preferred_element_type=F32)
    op_ref[:, 1] = y.astype(BF16).reshape(mp, cut, t)


def token_tile(length, most=256):
    return min(length, most)


def project(natural, groups, place, x, dense, gain, bias, cut):
    mp, _, width = dense.arrays[0].shape
    length = x.shape[0] if natural else x.shape[1]
    t = token_tile(length)
    tall = pl.BlockSpec((t, width), lambda i: (i, 0))
    flat = pl.BlockSpec((width, t), lambda i: (0, i))
    out_specs = [
        pl.BlockSpec((mp, 2, cut, t), lambda i: (0, 0, 0, i)),
        pl.BlockSpec((mp, cut, t), lambda i: (0, 0, i)),
        tall,
    ]
    out_shape = [
        jax.ShapeDtypeStruct((mp, 2, cut, length), BF16),
        jax.ShapeDtypeStruct((mp, cut, length), BF16),
        jax.ShapeDtypeStruct((length, width), BF16),
    ]
    if natural:
        out_specs.insert(0, flat)
        out_shape.insert(0, jax.ShapeDtypeStruct((width, length), F32))
    return pl.pallas_call(
        functools.partial(project_body, natural, len(dense), groups),
        grid=(length // t,),
        in_specs=[SCALARS, tall if natural else flat, whole(gain), whole(bias)] + dense.specs(),
        out_specs=out_specs,
        out_shape=out_shape,
        scratch_shapes=[
            pltpu.VMEM((mp, 2 * cut, width), BF16),
            pltpu.VMEM((mp, cut, width), BF16),
        ],
        compiler_params=params(),
        name="project",
    )(place, x, gain, bias, *dense.arrays)


def ff_chunks(refs):
    mp, rows, width = refs[0].shape
    part = rows // 2
    step = min(mp, width // part)
    size = step * part
    for p, ref in enumerate(refs):
        for j in range(mp // step):
            begin = (p * (mp // step) + j) * size
            yield ref, slice(j * step, (j + 1) * step), part, slice(begin, begin + size)


def forward_body(natural, ways, s_ref, c_ref, g_ref, wo_ref, gain_ref, bias_ref, *rest):
    ff, rest = rest[:ways], rest[ways:]
    s1_ref, s2_ref, h_ref, d_ref, n_ref, gated_ref, wo_t, down_t = rest
    width = ff[0].shape[-1]

    @pl.when(pl.program_id(0) == 0)
    def _():
        wo_t[...] = transposed(wo_ref[...]).astype(BF16)
        for ref, blocks, part, units in ff_chunks(ff):
            block = ref[blocks, part:, :].reshape(units.stop - units.start, width)
            down_t[:, units] = transposed(block).astype(BF16)

    gated = (g_ref[...].astype(F32) * c_ref[...].astype(F32)).astype(BF16)
    gated_ref[...] = gated
    s1 = s_ref[...] + jnp.dot(wo_t[...], gated, preferred_element_type=F32)
    s1_ref[...] = s1
    unit, _ = standardise(s1)
    normed = unit * gain_ref[...] + bias_ref[...]
    n_ref[...] = transposed(normed).astype(BF16)
    normed = normed.astype(BF16)
    total = s1
    for ref, blocks, part, units in ff_chunks(ff):
        up = ref[blocks, 0:part, :].reshape(units.stop - units.start, width)
        hidden, slope = gelu_pair(jnp.dot(up, normed, preferred_element_type=F32))
        hidden = hidden.astype(BF16)
        h_ref[units, :] = hidden
        d_ref[units, :] = slope.astype(BF16)
        total = total + jnp.dot(down_t[:, units], hidden, preferred_element_type=F32)
    s2_ref[...] = transposed(total) if natural else total


def forward_block(natural, stream, conv_two, gate_two, w_out, ff, gain, bias):
    width, length = stream.shape
    channels = w_out.shape[0]
    hidden = len(ff) * ff.arrays[0].shape[0] * ff.rows // 2
    t = token_tile(length)
    tall = pl.BlockSpec((t, width), lambda i: (i, 0))
    flat = pl.BlockSpec((width, t), lambda i: (0, i))
    chan = pl.BlockSpec((channels, t), lambda i: (0, i))
    high = pl.BlockSpec((hidden, t), lambda i: (0, i))
    last = (length, width) if natural else (width, length)
    return pl.pallas_call(
        functools.partial(forward_body, natural, len(ff)),
        grid=(length // t,),
        in_specs=[flat, chan, chan, whole(w_out), whole(gain), whole(bias)] + ff.specs(),
        out_specs=[flat, tall if natural else flat, high, high, tall, chan],
        out_shape=[
            jax.ShapeDtypeStruct((width, length), F32),
            jax.ShapeDtypeStruct(last, F32),
            jax.ShapeDtypeStruct((hidden, length), BF16),
            jax.ShapeDtypeStruct((hidden, length), BF16),
            jax.ShapeDtypeStruct((length, width), BF16),
            jax.ShapeDtypeStruct((channels, length), BF16),
        ],
        scratch_shapes=[pltpu.VMEM((width, channels), BF16), pltpu.VMEM((width, hidden), BF16)],
        compiler_params=params(),
        name="forward_block",
    )(stream, conv_two, gate_two, w_out, gain, bias, *ff.arrays)


def backward_body(natural, ways, gs_ref, d_ref, s1_ref, c_ref, g_ref, wo_ref, gain_ref, *rest):
    ff, rest = rest[:ways], rest[ways:]
    pre_ref, gs1_ref, gc_ref, two_ref, dm_ref, do_ref, gain_out, bias_out, up_n = rest
    width = ff[0].shape[-1]

    @pl.when(pl.program_id(0) == 0)
    def _():
        gain_out[...] = jnp.zeros_like(gain_out)
        bias_out[...] = jnp.zeros_like(bias_out)
        for ref, blocks, part, units in ff_chunks(ff):
            block = ref[blocks, 0:part, :].reshape(units.stop - units.start, width)
            up_n[:, units] = transposed(block).astype(BF16)

    if natural:
        dm_ref[...] = gs_ref[...]
        grad = transposed(gs_ref[...])
    else:
        grad = gs_ref[...]
        dm_ref[...] = transposed(grad).astype(BF16)
    dm = grad.astype(BF16)
    total = None
    for ref, blocks, part, units in ff_chunks(ff):
        down = ref[blocks, part:, :].reshape(units.stop - units.start, width)
        pre = jnp.dot(down, dm, preferred_element_type=F32) * d_ref[units, :].astype(F32)
        pre = pre.astype(BF16)
        pre_ref[units, :] = pre
        total = add(total, jnp.dot(up_n[:, units], pre, preferred_element_type=F32))
    back, gain_part, bias_part = standardise_back(total, gain_ref[...], s1_ref[...])
    gain_out[...] += gain_part
    bias_out[...] += bias_part
    grad = grad + back
    gs1_ref[...] = grad
    do_ref[...] = transposed(grad).astype(BF16)
    gated = jnp.dot(wo_ref[...], grad.astype(BF16), preferred_element_type=F32)
    gated = gated.astype(BF16).astype(F32)
    gc_ref[...] = (gated * g_ref[...].astype(F32)).astype(BF16)
    two_ref[...] = (gated * c_ref[...].astype(F32)).astype(BF16)


def backward_block(natural, grad, slope, s1, conv_two, gate_two, w_out, ff, gain):
    width, length = s1.shape
    channels = w_out.shape[0]
    hidden = slope.shape[0]
    t = token_tile(length, 512)
    tall = pl.BlockSpec((t, width), lambda i: (i, 0))
    flat = pl.BlockSpec((width, t), lambda i: (0, i))
    chan = pl.BlockSpec((channels, t), lambda i: (0, i))
    high = pl.BlockSpec((hidden, t), lambda i: (0, i))
    column = pl.BlockSpec((width, 1), lambda i: (0, 0))
    return pl.pallas_call(
        functools.partial(backward_body, natural, len(ff)),
        grid=(length // t,),
        in_specs=[tall if natural else flat, high, flat, chan, chan]
        + [whole(w_out), whole(gain)]
        + ff.specs(),
        out_specs=[high, flat, chan, chan, tall, tall, column, column],
        out_shape=[
            jax.ShapeDtypeStruct((hidden, length), BF16),
            jax.ShapeDtypeStruct((width, length), F32),
            jax.ShapeDtypeStruct((channels, length), BF16),
            jax.ShapeDtypeStruct((channels, length), BF16),
            jax.ShapeDtypeStruct((length, width), BF16),
            jax.ShapeDtypeStruct((length, width), BF16),
            jax.ShapeDtypeStruct((width, 1), F32),
            jax.ShapeDtypeStruct((width, 1), F32),
        ],
        scratch_shapes=[pltpu.VMEM((width, hidden), BF16)],
        compiler_params=params(),
        name="backward_block",
    )(grad, slope, s1, conv_two, gate_two, w_out, gain, *ff.arrays)


def unproject_body(natural, ways, groups, place_ref, gm_ref, two_ref, s_ref, gs_ref, gain_ref, *rest):
    dense, rest = rest[:ways], rest[ways:]
    out_ref, gain_out, bias_out, pair_t, value_t = rest
    mp, cut, t = two_ref.shape
    width = dense[0].shape[-1]

    @pl.when(pl.program_id(0) == 0)
    def _():
        gain_out[...] = jnp.zeros_like(gain_out)
        bias_out[...] = jnp.zeros_like(bias_out)

        def body(pair, value):
            rows = by_channel(pair, groups).reshape(mp * 2 * cut, width)
            pair_t[...] = transposed(rows).astype(BF16)
            rows = by_channel(value, groups).reshape(mp * cut, width)
            value_t[...] = transposed(rows).astype(BF16)

        first(place_ref[0] == 0, dense, cut, body)

    pair = jnp.concatenate([gm_ref[:, 0:1], two_ref[...][:, None]], axis=1)
    grad = jnp.dot(pair_t[...], pair.reshape(mp * 2 * cut, t), preferred_element_type=F32)
    value = gm_ref[:, 1].reshape(mp * cut, t)
    grad = grad + jnp.dot(value_t[...], value, preferred_element_type=F32)
    back, gain_part, bias_part = standardise_back(grad, gain_ref[...], s_ref[...])
    gain_out[...] += gain_part
    bias_out[...] += bias_part
    result = gs_ref[...] + back
    out_ref[...] = transposed(result) if natural else result


def unproject(natural, groups, place, grad_mixed, grad_two, dense, stream, grad, gain):
    width, length = stream.shape
    mp, cut, _ = grad_two.shape
    t = token_tile(length)
    tall = pl.BlockSpec((t, width), lambda i: (i, 0))
    flat = pl.BlockSpec((width, t), lambda i: (0, i))
    column = pl.BlockSpec((width, 1), lambda i: (0, 0))
    last = (length, width) if natural else (width, length)
    return pl.pallas_call(
        functools.partial(unproject_body, natural, len(dense), groups),
        grid=(length // t,),
        in_specs=[
            SCALARS,
            pl.BlockSpec((mp, 2, cut, t), lambda i: (0, 0, 0, i)),
            pl.BlockSpec((mp, cut, t), lambda i: (0, 0, i)),
            flat,
            flat,
            whole(gain),
        ]
        + dense.specs(),
        out_specs=[tall if natural else flat, column, column],
        out_shape=[
            jax.ShapeDtypeStruct(last, F32),
            jax.ShapeDtypeStruct((width, 1), F32),
            jax.ShapeDtypeStruct((width, 1), F32),
        ],
        scratch_shapes=[
            pltpu.VMEM((width, mp * 2 * cut), BF16),
            pltpu.VMEM((width, mp * cut), BF16),
        ],
        compiler_params=params(),
        name="unproject",
    )(place, grad_mixed, grad_two, stream, grad, gain, *dense.arrays)


GROUP = 8


class Plain:
    def __init__(self, ways, mp, left, right):
        self.left = left.reshape(ways, mp, left.shape[0] // (ways * mp), left.shape[1])
        self.rows, self.rights = self.left.shape[2], [right]

    def lefts(self):
        _, _, part, length = self.left.shape
        shape = (self.left.shape[0], GROUP, part, length)
        spec = pl.BlockSpec(shape, lambda i, place: (0, i ^ (place[1] // GROUP), 0, 0))
        return [(self.left, spec)]

    def pieces(self, way, lefts, rights):
        ways, count, part, length = lefts[0].shape
        for w in range(ways):
            y = rows_product(lefts[0][w].reshape(count * part, length), rights[0])
            yield y.reshape(count, part, -1)


class Mixed:
    def __init__(self, ways, groups, lefts, rights):
        self.ways, self.rights = ways, rights
        self.arrays = [
            x.reshape((x.shape[0] // groups, groups) + x.shape[1:]) for x in lefts
        ]
        self.rows = 2 * self.arrays[0].shape[-2] // ways

    def lefts(self):
        result = []
        for x in self.arrays:
            shape = (GROUP, None) + x.shape[2:]
            zeros = (0,) * (x.ndim - 2)
            runs = x.shape[0] // GROUP

            def index(i, place, runs=runs, zeros=zeros):
                run = i ^ (place[1] // GROUP)
                return (lax.rem(run, runs), run // runs) + zeros

            result.append((x, pl.BlockSpec(shape, index)))
        return result

    def pieces(self, way, lefts, rights):
        if len(lefts) == 1:
            lefts = [lefts[0].at[:, 0], lefts[0].at[:, 1]]
        made = []
        for left, right in zip(lefts, (rights * 2)[:2]):
            count, cut, length = left.shape
            y = rows_product(left[...].reshape(count * cut, length), right)
            made.append(y.reshape(count, cut, -1))
        a, b = made
        for w in range(self.ways):
            if self.ways == 1:
                yield jnp.concatenate([a, b], axis=1)
            else:
                yield jnp.where(way ^ w == 0, a, b)


def rows_product(left, right):
    return jnp.dot(left, right[...], preferred_element_type=F32).astype(BF16)


def grads_body(ways, jobs, before, place_ref, *refs):
    counts = [len(job.lefts()) for job in jobs]
    lefts, refs = refs[: sum(counts)], refs[sum(counts) :]
    rights, refs = refs[: sum(len(j.rights) for j in jobs)], refs[sum(len(j.rights) for j in jobs) :]
    outs = refs[before:]
    low = place_ref[1] % GROUP
    begin = 0
    for job, count in zip(jobs, counts):
        mine, lefts = lefts[:count], lefts[count:]
        right, rights = rights[: len(job.rights)], rights[len(job.rights) :]
        for out, values in zip(outs, job.pieces(place_ref[0], list(mine), list(right))):
            for i in range(GROUP):
                out[i ^ low, begin : begin + job.rows, :] = values[i]
        begin += job.rows


def weight_grads(name, ways, mp, place, jobs, before=()):
    width = jobs[0].rights[0].shape[1]
    rows = sum(job.rows for job in jobs)
    lefts = [pair for job in jobs for pair in job.lefts()]
    rights = [right for job in jobs for right in job.rights]

    def kept(a):
        return pl.BlockSpec(a.shape, lambda i, place: (0, 0), pipeline_mode=pl.Buffered(1))

    out = pl.BlockSpec((GROUP, rows, width), lambda i, place: (i, 0, 0))
    return pl.pallas_call(
        functools.partial(grads_body, ways, jobs, len(before)),
        grid_spec=pltpu.PrefetchScalarGridSpec(
            num_scalar_prefetch=1,
            grid=(mp // GROUP,),
            in_specs=[spec for _, spec in lefts]
            + [kept(a) for a in rights]
            + [pl.BlockSpec(memory_space=pl.ANY)] * len(before),
            out_specs=[out] * ways,
        ),
        out_shape=[jax.ShapeDtypeStruct((mp, rows, width), BF16)] * ways,
        compiler_params=params(),
        name=name,
    )(place, *[x for x, _ in lefts], *rights, *before)


def together(*arrays):
    return lax.optimization_barrier(arrays)


def flip(x, axis, size, bit):
    return lax.ppermute(x, axis, [(i, i ^ bit) for i in range(size)])


def dp_sum(x, dp):
    return butterfly(x, [("dp", dp)])


def butterfly(x, sizes):
    for axis, size in sizes:
        bit = 1
        while bit < size:
            x = x + flip(x, axis, size, bit)
            bit *= 2
    return x


def stage_order(mp, swapped):
    bits = list(range(mp.bit_length() - 1))
    first = [[1], [0]] if swapped else [[0], [1]]
    return first + [bits[i : i + 2] for i in range(2, len(bits), 2)]


def total(parts):
    value = parts[0].astype(F32)
    for part in parts[1:]:
        value = value + part.astype(F32)
    return value


class Hop:
    def __init__(self, x, axis, size, mask):
        self.x, self.where = x, (axis, size, mask)

    def start(self):
        return flip(self.x, *self.where)


def masks(bits):
    return [sum(((k >> i) & 1) << b for i, b in enumerate(bits)) for k in range(1 << len(bits))]


def scatter_steps(terms, left, mp, stages):
    for stage in stages:
        axes = [left.index(b) for b in stage]
        left = [b for b in left if b not in stage]

        def take(t, k):
            index = [slice(None)] * t.ndim
            for i, axis in enumerate(axes):
                index[axis] = (k >> i) & 1
            return t[tuple(index)]

        sums = [
            total([take(t, k) for t in terms]).astype(BF16) for k in range(1 << len(stage))
        ]
        got = yield [Hop(x, "mp", mp, mask) for x, mask in zip(sums[1:], masks(stage)[1:])]
        terms = sums[:1] + got
    return terms


def scatter_chain(terms, mp, stages, split=False):
    bits = mp.bit_length() - 1
    left = list(range(bits - 1, -1, -1))
    terms = [t.reshape((2,) * bits + t.shape[1:]) for t in terms]
    if split:
        rows = terms[0].shape[-2]
        middle = (rows // 2 + 15) // 16 * 16
        orders = stages[:2], stages[1::-1]
        parts = [
            scatter_steps([t[..., span, :] for t in terms], left, mp, order)
            for span, order in zip((slice(0, middle), slice(middle, rows)), orders)
        ]
        hops = [next(part) for part in parts]
        got = yield hops[0] + hops[1]
        hops = [part.send([x]) for part, x in zip(parts, got)]
        got = yield hops[0] + hops[1]
        ended = []
        for part, x in zip(parts, got):
            try:
                part.send([x])
            except StopIteration as end:
                ended.append(end.value)
        terms = [jnp.concatenate(pair, axis=-2) for pair in zip(*ended)]
        left = [b for b in left if b not in stages[0] + stages[1]]
        stages = stages[2:]
    terms = yield from scatter_steps(terms, left, mp, stages)
    return total(terms)


def in_two(x):
    high = x.astype(BF16)
    return jnp.concatenate([high, (x - high.astype(F32)).astype(BF16)], axis=0)


def from_two(x):
    half = x.shape[0] // 2
    return x[:half].astype(F32) + x[half:].astype(F32)


def last_chain(terms, norms, mp, stages):
    bits = mp.bit_length() - 1
    left = list(range(bits - 1, -1, -1))
    terms = [t.reshape((2,) * bits + t.shape[1:]) for t in terms]
    width = norms.shape[1]
    for stage in stages:
        axes = [left.index(b) for b in stage]
        left = [b for b in left if b not in stage]
        sums = []
        for k in range(1 << len(stage)):
            index = [slice(None)] * terms[0].ndim
            for i, axis in enumerate(axes):
                index[axis] = (k >> i) & 1
            sums.append(total([t[tuple(index)] for t in terms]).astype(BF16))
        own = in_two(norms)
        shape, rows = sums[0].shape, sums[0].size // width
        got = yield [
            Hop(jnp.concatenate([x.reshape(rows, width), own], axis=0), "mp", mp, mask)
            for x, mask in zip(sums[1:], masks(stage)[1:])
        ]
        terms = sums[:1] + [x[:rows].reshape(shape) for x in got]
        values = [from_two(x) for x in [own] + [x[rows:] for x in got]]
        while len(values) > 1:
            values = [a + b for a, b in zip(values[0::2], values[1::2])]
        norms = values[0]
    return total(terms), norms


def gather_chain(x, mp, stages):
    me = lax.axis_index("mp")
    done = []
    for stage in stages:
        got = yield [Hop(x, "mp", mp, mask) for mask in masks(stage)[1:]]
        pieces = [x] + got
        place = sum(((me >> b) & 1) << i for i, b in enumerate(stage))
        count = len(pieces)
        if count == 2:
            pieces = [jnp.where(place == a, x, got[0]) for a in range(2)]
        else:
            pieces = [
                lax.select_n(place, *[pieces[a ^ v] for v in range(count)]) for a in range(count)
            ]
        for i, bit in enumerate(stage):
            axis = sum(b > bit for b in done)
            pieces = [
                jnp.stack([pieces[j], pieces[j + 1]], axis=axis) for j in range(0, len(pieces), 2)
            ]
            done.append(bit)
        x = pieces[0]
    return x.reshape((mp,) + x.shape[len(done) :])


def chip_chain(pieces, dp):
    if len(pieces) == 1:
        return pieces
    got = yield [Hop(pieces[1], "dp", dp, 1)]
    return [pieces[0]] + got


class Chains:
    def __init__(self):
        self.waiting, self.results = {}, {}

    def add(self, name, chain):
        self.step(name, chain, None)

    def step(self, name, chain, value):
        try:
            self.waiting[name] = chain, chain.send(value)
        except StopIteration as end:
            self.waiting.pop(name, None)
            self.results[name] = end.value

    def hops(self):
        return [hop for _, hops in self.waiting.values() for hop in hops]

    def operands(self):
        return [hop.x for hop in self.hops()]

    def tie(self, *others):
        hops = self.hops()
        tied = together(*[hop.x for hop in hops], *others)
        for hop, x in zip(hops, tied):
            hop.x = x
        return tied[len(hops) :]

    def start(self):
        return {name: [hop.start() for hop in hops] for name, (_, hops) in self.waiting.items()}

    def finish(self, started, *others):
        flat = [x for got in started.values() for x in got]
        tied = list(together(*flat, *others))
        for name, got in started.items():
            mine, tied = tied[: len(got)], tied[len(got) :]
            self.step(name, self.waiting[name][0], mine)
        return tied


def program(dp, mp, inputs, cotangent, norm_gain, norm_bias, in_weight, kernels, *rest):
    out_weight, up_weight, down_weight, taps_kept = rest
    layers = in_weight.shape[0]
    groups, chunk, width = inputs.shape
    peers = mp // groups
    shard, hidden = in_weight.shape[3], up_weight.shape[2]
    length = groups * chunk
    cut = -(-shard // 16) * 16
    ways = 2 if dp == 2 and shard == cut and hidden % 32 == 0 else 1
    part = hidden // ways
    dense_rows = 4 * cut // ways
    me, way = lax.axis_index("mp"), lax.axis_index("dp")
    place = jnp.stack([way, me]).astype(jnp.int32)
    zero_half = me // peers == 0
    swap = [(i, (i + peers) % mp) for i in range(mp)]
    halves = [[h * peers + q for q in range(peers)] for h in range(groups)]

    def ordered(own, got):
        return jnp.stack([jnp.where(zero_half, own, got), jnp.where(zero_half, got, own)])

    def pick(x):
        return jnp.where(zero_half, x[0], x[1]), jnp.where(zero_half, x[1], x[0])

    def to_one_sequence(x):
        own, other = pick(x)
        return ordered(own, lax.ppermute(other, "mp", swap)).reshape(length, width)

    def to_two_sequences(x):
        own, other = pick(x.reshape(groups, chunk, width))
        got = lax.ppermute(other.astype(BF16), "mp", swap)
        return ordered(own, got.astype(F32))

    def exchange(x):
        return lax.all_to_all(
            x, "mp", split_axis=0, concat_axis=0, tiled=True, axis_index_groups=halves
        )

    def widen(x, axis):
        pads = [(0, 0)] * x.ndim
        pads[axis] = (0, cut - shard)
        return x if cut == shard else jnp.pad(x, pads)

    dense = [jnp.transpose(in_weight[:, :, j], (0, 2, 1)) for j in range(3)] + [out_weight]
    dense = jnp.concatenate([widen(d, 1) for d in dense], axis=1)
    up = jnp.transpose(up_weight, (0, 2, 1))

    def my_rows(x, rows):
        return lax.dynamic_slice_in_dim(x, way * rows, rows, 1) if ways > 1 else x

    dense = my_rows(dense, dense_rows)
    ff = jnp.concatenate([my_rows(up, part), my_rows(down_weight, part)], axis=1)

    def gather(x):
        x = lax.all_gather(x, "mp", axis=0)
        return [x, flip(x, "dp", dp, 1)] if ways > 1 else [x]

    def gathered(x):
        return lax.all_gather(x, "mp", axis=0)

    def shared(x):
        return [x, flip(x, "dp", dp, 1)] if ways > 1 else [x]

    def out_matrix(pieces):
        skip = dense_rows - cut
        rows = [
            a[:, begin + skip : begin + dense_rows]
            for a, begin in zip(pieces.arrays, pieces.begins)
        ]
        rows = jnp.where(way == 1, rows[0], rows[1]) if ways > 1 else rows[0]
        rows = rows.reshape(groups, peers, cut, width)
        return jnp.swapaxes(rows, 0, 1).reshape(mp * cut, width)

    keep = jnp.arange(kernels.shape[-1])[None, :] < taps_kept[:, None]
    kept = jnp.where(keep[:, None, None, :], kernels, jnp.zeros_like(kernels))
    kept = widen(kept, 2)
    taps = []

    chains = Chains()
    bits = mp.bit_length() - 1
    for i in range(2):
        rows = dense[0, i * dense_rows // 2 : (i + 1) * dense_rows // 2]
        stages = [[b] for b in range(bits - 1, 1, -1)] + [[1 - i], [i]]
        chains.add(i, gather_chain(rows, mp, stages))
    own, other = pick(inputs)
    mine, other = chains.tie(ff[0], other)
    ff_mine = gathered(mine)
    (other,) = chains.finish(chains.start(), other)
    moves = [other[: chunk // 2], other[chunk // 2 :], kept[0]]
    moved = []
    while len(moved) < 3:
        now = moves[len(moved)]
        started = chains.start()
        got = lax.ppermute(now, "mp", swap)
        if len(moved) < 2:
            got, moves[len(moved) + 1] = chains.finish(started, got, moves[len(moved) + 1])
        else:
            (got,) = chains.finish(started, got)
        moved.append(got)
    while chains.waiting:
        chains.finish(chains.start())
    dense_mine = jnp.concatenate([chains.results.pop(i) for i in range(2)], axis=1)
    other = jnp.concatenate(moved[:2], axis=0)
    got_taps = moved[2]
    stream = ordered(own, other).reshape(length, width)
    none = [0] * ways
    dense_all = [Pieces(shared(dense_mine), none, dense_rows)]
    ff_all = []

    gains = norm_gain[..., None]
    biases = norm_bias[..., None]
    saved, out_all = [], []
    own_grad, grad = pick(cotangent)
    less = chunk // 32 * 12
    halves_of_grad = [grad[:less], grad[less:]]
    for layer in range(layers):
        natural = layer == 0
        more = layer + 1 < layers
        got = project(
            natural,
            groups,
            place,
            stream,
            dense_all[layer],
            gains[layer, 0],
            biases[layer, 0],
            cut,
        )
        if natural:
            stream, got = got[0], got[1:]
        operand, gate_two, normed_one = got
        if natural:
            ff_mine, operand = together(ff_mine, operand)
            ff_pair = shared(ff_mine)
        if more:
            mine, operand = together(dense[layer + 1], operand)
            dense_next = gathered(mine)
        gates = exchange(operand.reshape(peers, groups, 2, cut, length))
        taps.append(ordered(kept[layer], got_taps))
        if natural:
            gates, *ff_pair = together(gates, *ff_pair)
        else:
            ff_mine, gates = together(ff_mine, gates)
            ff_pair = shared(ff_mine)
        conv_two, conv_one, carried = mix(gates, taps[layer])
        conv_two, *ff_pair = together(conv_two, *ff_pair)
        ff_all.append(Pieces(ff_pair, none, 2 * part))
        out_all.append(out_matrix(dense_all[layer]))
        if more:
            mine, conv_two = together(ff[layer + 1], conv_two)
            ff_mine = gathered(mine)
        conv_two = exchange(conv_two).reshape(mp * cut, length)
        if more:
            got_taps, conv_two = together(kept[layer + 1], conv_two)
            got_taps = lax.ppermute(got_taps, "mp", swap)
        half = None
        if layer >= layers - 2:
            half = halves_of_grad[layer - layers + 2]
            half, conv_two = together(half, conv_two)
            half = lax.ppermute(half, "mp", swap)
        gate_two = gate_two.reshape(mp * cut, length)
        s1, s2, active, slope, normed_two, gated = forward_block(
            layer == layers - 1,
            stream,
            conv_two,
            gate_two,
            out_all[layer],
            ff_all[layer],
            gains[layer, 1],
            biases[layer, 1],
        )
        if half is not None:
            half, s2 = together(half, s2)
            halves_of_grad[layer - layers + 2] = half
        if more:
            dense_next, got_taps, s2 = together(dense_next, got_taps, s2)
            dense_all.append(Pieces(shared(dense_next), none, dense_rows))
        saved.append(
            (stream, normed_one, gates, conv_one, carried, conv_two, gate_two)
            + (s1, active, slope, normed_two, gated)
        )
        stream = s2
    own_output, other = pick(stream.reshape(groups, chunk, width))
    other = other.astype(BF16)
    got_output = lax.ppermute(other[: chunk // 2], "mp", swap)
    other_output = other[chunk // 2 :]
    grad = ordered(own_grad, jnp.concatenate(halves_of_grad, axis=0)).reshape(length, width)

    gain_rows, bias_rows = [None] * layers, [None] * layers
    dks = [None] * layers
    later = None
    for layer in reversed(range(layers)):
        (s0, normed_one, gates, conv_one, carried, conv_two, gate_two) = saved[layer][:7]
        (s1, active, slope, normed_two, gated) = saved[layer][7:]
        pre, grad, grad_conv, grad_two, dm, do, gain_two, bias_two = backward_block(
            layer == layers - 1,
            grad,
            slope,
            s1,
            conv_two,
            gate_two,
            out_all[layer],
            ff_all[layer],
            gains[layer, 1],
        )
        gain_rows[layer], bias_rows[layer] = [None, gain_two], [None, bias_two]
        mixed = None
        if later is not None:
            mixed, grad_conv = together(later[0], grad_conv)
            got_dk, grad_conv = chains.finish(started, got_dk, grad_conv)
            dks[layer + 1] = own_dk.astype(F32) + got_dk.astype(F32)
        if layer == layers - 1:
            got_output, grad_conv = together(got_output, grad_conv)
        grad_conv = exchange(grad_conv.reshape(peers, groups, cut, length))
        grad_two = grad_two.reshape(mp, cut, length)
        up_job = Plain(ways, mp, pre, normed_two)
        down_job = Plain(ways, mp, active, dm)
        two_rows = [grad_two, gated.reshape(mp, cut, length)]
        mixed_job = Mixed(ways, groups, two_rows, [normed_one, do])
        late_jobs = [] if mixed is None else [Mixed(ways, groups, [mixed], [later[1]])]
        jobs = [up_job, down_job, mixed_job] + late_jobs
        early = weight_grads("early_grads", ways, mp, place, jobs)
        grad_conv, *early = together(grad_conv, *early)
        if layer == layers - 1:
            other_output, grad_conv = together(other_output, grad_conv)
            more_output = lax.ppermute(other_output, "mp", swap)
        chains.add(("flip", layer), chip_chain(early, dp))
        (grad_conv,) = chains.tie(grad_conv)
        started = chains.start()
        grad_mixed, dk = unmix(grad_conv, gates, conv_one, carried, taps[layer])
        (grad_mixed,) = chains.finish(started, grad_mixed)
        own_dk, other_dk = pick(dk.astype(BF16))
        if layer == layers - 1:
            more_output, grad_mixed = together(more_output, grad_mixed)
        grad_mixed = exchange(grad_mixed).reshape(mp, 2, cut, length)
        if layer == layers - 1:
            output = jnp.concatenate([got_output, more_output], axis=0)
            output = ordered(own_output, output.astype(F32))
            output, grad_mixed = together(output, grad_mixed)
        terms = chains.results.pop(("flip", layer))
        chains.add(layer, scatter_chain(terms, mp, stage_order(mp, 0), True))
        if layer:
            later = grad_mixed, normed_one
        else:
            started = chains.start()
            got_dk = lax.ppermute(other_dk, "mp", swap)
            late_job = Mixed(ways, groups, [grad_mixed], [normed_one])
            late = weight_grads("late_grads", ways, mp, place, [late_job])
            grad_mixed, *late = together(grad_mixed, *late)
            tail = Chains()
            tail.add("late", chip_chain(late, dp))
            last = tail.start()
        grad, gain_one, bias_one = unproject(
            layer == 0,
            groups,
            place,
            grad_mixed,
            grad_two,
            dense_all[layer],
            s0,
            grad,
            gains[layer, 0],
        )
        gain_rows[layer][0], bias_rows[layer][0] = gain_one, bias_one
        if layer:
            grad, other_dk = chains.tie(grad, other_dk)
            got_dk = lax.ppermute(other_dk, "mp", swap)
            started = chains.start()

    (grad,) = tail.finish(last, grad)
    own, other = pick(grad.reshape(groups, chunk, width))
    swapped = lax.ppermute(other.astype(BF16), "mp", swap)
    (gain_rows[0][0],) = chains.finish(started, gain_rows[0][0])
    chains.results.update(tail.results)
    bits = list(range(mp.bit_length() - 1))
    quarters = [bits[i : i + 2] for i in range(0, len(bits), 2)]
    norms = jnp.stack([jnp.stack([jnp.stack(r) for r in rows]) for rows in (gain_rows, bias_rows)])
    shape = norms.shape[:-1]
    norms = norms.reshape(-1, width)
    chains.add("late", last_chain(chains.results.pop("late"), norms, mp, quarters))
    rounds = 0
    while chains.waiting:
        started = chains.start()
        if rounds == 0:
            swapped, got_dk = chains.finish(started, swapped, got_dk)
        else:
            chains.finish(started)
        rounds += 1
    input_grad = ordered(own, swapped.astype(F32))
    dks[0] = own_dk.astype(F32) + got_dk.astype(F32)
    dk = jnp.stack(dks).astype(BF16).astype(F32)
    late, norms = chains.results.pop("late")
    found = [chains.results.pop(layer) for layer in reversed(range(layers))]
    final = [x.astype(BF16) for x in found + [late]]
    if ways == 1:
        dk, norms = dp_sum(dk, dp), dp_sum(norms, dp)
        final = [[dp_sum(x, dp)] for x in found + [late]]
    else:
        dk = dk + flip(dk.astype(BF16), "dp", dp, 1).astype(F32)
        norms = in_two(norms)
        sizes = [x.shape[0] for x in final + [norms]]
        sent = jnp.concatenate(final + [norms], axis=0)
        got = flip(sent, "dp", dp, 1)
        zero = way == 0
        pair = jnp.where(zero, sent, got).astype(F32), jnp.where(zero, got, sent).astype(F32)
        begin, pieces = 0, []
        for size in sizes:
            pieces.append([x[begin : begin + size] for x in pair])
            begin += size
        final, norms = pieces[:-1], pieces[-1]
        half = norms[0].shape[0] // 2
        norms = (norms[0][:half] + norms[0][half:]) + (norms[1][:half] + norms[1][half:])
    norms = norms.reshape(shape)
    dk = dk[:, :, :shard]
    tap_out = jnp.where(keep[:, None, None, :], dk, 0.0)

    def cut_rows(x, *sizes):
        begin = 0
        for size in sizes:
            yield x[begin : begin + size]
            begin += size

    share = 2 * cut // ways
    wide = [[None] * layers for _ in range(4)]
    order = []
    for layer in range(layers - 1, -1, -1):
        now = [(0, layer), (1, layer), (2, layer)] + [(3, layer + 1)] * (layer < layers - 1)
        order.append(now)
    order.append([(3, 0)])
    sizes = [part, part, share, share]
    found = zip(order, final)
    for order, arrays in found:
        pieces = zip(*[cut_rows(x, *[sizes[i] for i, _ in order]) for x in arrays])
        for (i, layer), x in zip(order, pieces):
            wide[i][layer] = x

    def rows_of_both(arrays):
        return jnp.concatenate(arrays, axis=0)

    parts = [[] for _ in range(6)]
    for up, down, early, late in zip(*wide):
        two, out = (early[0][:cut], early[0][cut:]) if ways == 1 else early
        one, value = (late[0][:cut], late[0][cut:]) if ways == 1 else late
        for store, x in zip(parts, (one, two, value, out, rows_of_both(up), rows_of_both(down))):
            store.append(x)
    one, two, value, out, up, down = (jnp.stack(p) for p in parts)
    in_out = jnp.stack([one, two, value], axis=1)[:, :, :shard]
    return (
        output,
        input_grad,
        norms[0],
        norms[1],
        jnp.transpose(in_out, (0, 3, 1, 2)),
        tap_out,
        out[:, :shard],
        jnp.transpose(up, (0, 2, 1)),
        down,
    )


def solution(mesh):
    sizes = dict(mesh.shape)
    specs = (
        P("dp", "mp", None),
        P("dp", "mp", None),
        P(),
        P(),
        P(None, None, None, "mp"),
        P(None, None, "mp", None),
        P(None, "mp", None),
        P(None, None, "mp"),
        P(None, "mp", None),
    )
    return jax.shard_map(
        functools.partial(program, sizes["dp"], sizes["mp"]),
        mesh=mesh,
        in_specs=specs + (P(),),
        out_specs=specs,
        check_vma=False,
    )
```

```python
import functools
import math

import jax
import jax.numpy as jnp
import ml_dtypes
import numpy as np
from jax import lax
from jax.experimental import pallas as pl
from jax.experimental.pallas import tpu as pltpu
from jax.sharding import PartitionSpec as P

EPS = 1e-05
LANES = 128
RADIX = 32
HALF = RADIX // 2
FREQS = HALF + 1
POINTS = LANES * RADIX
SPAN = POINTS // 2
BF16 = jnp.bfloat16
F32 = jnp.float32
VMEM_BYTES = 56 * 2**20
PASSES = 1


def params():
    return pltpu.CompilerParams(vmem_limit_bytes=VMEM_BYTES)


def whole(array):
    rank = array.ndim
    return pl.BlockSpec(array.shape, lambda *_: (0,) * rank, pipeline_mode=pl.Buffered(1))


def add(a, b):
    if a is None:
        return b
    return a if b is None else a + b


def sub(a, b):
    if b is None:
        return a
    return -b if a is None else a - b


def tidy(v):
    for exact in (0.0, 1.0, -1.0):
        if abs(v - exact) < 1e-12:
            return exact
    return v


def scaled(v, factor):
    if v is None or factor == 0.0:
        return None
    if factor == 1.0:
        return v
    return -v if factor == -1.0 else v * factor


def turn(z, angle):
    re, im = z
    c, s = tidy(math.cos(angle)), tidy(math.sin(angle))
    if re is not None and im is not None and abs(abs(c) - abs(s)) < 1e-12:
        r = math.copysign(abs(c), c)
        if c * s > 0:
            return ((re - im) * r, (re + im) * r)
        return ((re + im) * r, (im - re) * r)
    return (sub(scaled(re, c), scaled(im, s)), add(scaled(im, c), scaled(re, s)))


def analyse(x):
    n = len(x)
    if n == 1:
        return [(x[0], None)]
    even, odd = analyse(x[0::2]), analyse(x[1::2])
    if n == 2:
        return [(add(even[0][0], odd[0][0]), None), (sub(even[0][0], odd[0][0]), None)]
    half, quarter = n // 2, n // 4
    out = [None] * (half + 1)
    for k in range(quarter + 1):
        t = turn(odd[k], -2 * math.pi * k / n)
        out[k] = (add(even[k][0], t[0]), add(even[k][1], t[1]))
        if k != quarter:
            out[half - k] = (sub(even[k][0], t[0]), sub(t[1], even[k][1]))
    return out


def synthesise(x, n, upper):
    if n == 2:
        return [sub(x[0][0], x[1][0]) if upper else add(x[0][0], x[1][0])]
    half, quarter = n // 2, n // 4
    even, odd = [], []
    for k in range(quarter + 1):
        a, b = x[k], x[half - k]
        if k == 0:
            even.append((add(a[0], b[0]), None))
            odd.append((sub(a[0], b[0]), None))
        elif k == quarter:
            even.append((a[0] * 2.0, None))
            odd.append((a[1] * -2.0, None))
        else:
            even.append((add(a[0], b[0]), sub(a[1], b[1])))
            odd.append(turn((sub(a[0], b[0]), add(a[1], b[1])), 2 * math.pi * k / n))
    out = [None] * half
    out[0::2] = synthesise(even, half, upper)
    out[1::2] = synthesise(odd, half, upper)
    return out


def split_bf16(matrix):
    matrix = matrix.astype(np.float32)
    high = matrix.astype(ml_dtypes.bfloat16)
    low = (matrix - high.astype(np.float32)).astype(ml_dtypes.bfloat16)
    return jnp.asarray(np.stack([high, low][: 1 if PASSES == 1 else 2]))


def tables():
    j = np.arange(LANES)
    angle = 2 * np.pi * np.outer(j, j) / LANES
    c, s = np.cos(angle), np.sin(angle)
    twist = 2 * np.pi * np.outer(np.arange(FREQS), j) / POINTS
    return [
        split_bf16(np.block([[c, -s], [s, c]])),
        split_bf16(np.block([[c, s], [-s, c]]) / POINTS),
        jnp.asarray(np.cos(twist), F32),
        jnp.asarray(np.sin(twist), F32),
    ]


def lane_product(a, matrix):
    high = a.astype(BF16)
    y = jnp.dot(high, matrix[0], preferred_element_type=F32)
    if PASSES > 1:
        y = y + jnp.dot(high, matrix[1], preferred_element_type=F32)
    if PASSES > 2:
        low = (a - high.astype(F32)).astype(BF16)
        y = y + jnp.dot(low, matrix[0], preferred_element_type=F32)
    return y


class Convolver:
    def __init__(self, sources, groups, pieces, blocks, rows, refs):
        self.sources, self.groups, self.pieces = sources, groups, pieces
        self.blocks, self.rows = blocks, rows
        self.forward, self.backward, self.cos, self.sin, self.left, self.right, self.freq = refs

    def places(self):
        for i in range(self.sources * self.groups * self.pieces):
            chunk, piece = divmod(i, self.pieces)
            group, source = divmod(chunk, self.sources)
            begin = (group * self.pieces + piece) * LANES
            yield i, source, slice(begin, begin + LANES)

    def load(self, ref, dst):
        for i, source, lanes in self.places():
            dst[i] = ref[source, :, lanes].astype(F32)

    def store(self, src, ref, part=None):
        for i, source, lanes in self.places():
            if part is None:
                ref[source, :, lanes] = src[i].astype(ref.dtype)
            else:
                ref[source, part, :, lanes] = src[i].astype(ref.dtype)

    def subtiles(self):
        return [pl.ds(8 * t, 8) for t in range(self.rows // 8)]

    def spectrum(self, read, count, base):
        for b in range(count):
            for rows in self.subtiles():
                x = analyse([read(b, i, rows) for i in range(HALF)] + [None] * HALF)
                for f, (re, im) in enumerate(x):
                    if f:
                        c, s = self.cos[f : f + 1, :], self.sin[f : f + 1, :]
                        if im is None:
                            re, im = re * c, -(re * s)
                        else:
                            re, im = re * c + im * s, im * c - re * s
                    self.left[b * FREQS + f, rows, 0:LANES] = re
                    self.left[b * FREQS + f, rows, LANES:] = jnp.zeros_like(re) if im is None else im
            y = lane_product(self.stacked(b), self.forward)
            begin = (base + b) * FREQS
            self.freq[begin : begin + FREQS] = y.reshape(FREQS, self.rows, 2 * LANES)

    def stacked(self, b):
        return self.left[b * FREQS : (b + 1) * FREQS].reshape(FREQS * self.rows, 2 * LANES)

    def entry(self, row, rows):
        return self.freq[row, rows, 0:LANES], self.freq[row, rows, LANES:]

    def window(self, base, b, f, rows, ahead):
        re, im = self.entry((base + b) * FREQS + f, rows)
        other = b + 1 if ahead else b - 1
        if not ahead and f % 2:
            re, im = -re, -im
        if 0 <= other < self.blocks:
            ore, oim = self.entry((base + other) * FREQS + f, rows)
            if ahead and f % 2:
                return re - ore, im - oim
            return re + ore, im + oim
        return re, im

    def inverse(self, b, upper, write):
        y = lane_product(self.stacked(b), self.backward)
        begin = b * FREQS
        self.right[begin : begin + FREQS] = y.reshape(FREQS, self.rows, 2 * LANES)
        for rows in self.subtiles():
            parts = []
            for f in range(FREQS):
                re = self.right[begin + f, rows, 0:LANES]
                im = self.right[begin + f, rows, LANES:]
                c, s = self.cos[f : f + 1, :], self.sin[f : f + 1, :]
                if f == 0:
                    parts.append((re, None))
                elif f == HALF:
                    parts.append((re * c - im * s, None))
                else:
                    parts.append((re * c - im * s, im * c + re * s))
            for i, value in enumerate(synthesise(parts, RADIX, upper)):
                write(b, i, rows, value)

    def convolve(self, signal, kernel, ahead, write):
        for b in range(self.blocks):
            for rows in self.subtiles():
                for f in range(FREQS):
                    re, im = self.window(signal, b, f, rows, ahead)
                    kre, kim = self.entry(kernel * FREQS + f, rows)
                    if ahead:
                        pre, pim = re * kre + im * kim, im * kre - re * kim
                    else:
                        pre, pim = re * kre - im * kim, re * kim + im * kre
                    self.left[b * FREQS + f, rows, 0:LANES] = pre
                    self.left[b * FREQS + f, rows, LANES:] = pim
            self.inverse(b, not ahead, write)

    def taps(self, signal, grads, write):
        for rows in self.subtiles():
            for f in range(FREQS):
                re = im = None
                for b in range(self.blocks):
                    gre, gim = self.window(grads, b, f, rows, True)
                    sre, sim = self.entry((signal + b) * FREQS + f, rows)
                    re = add(re, sre * gre + sim * gim)
                    im = add(im, sre * gim - sim * gre)
                self.left[f, rows, 0:LANES] = re
                self.left[f, rows, LANES:] = im
        self.inverse(0, False, write)


def kernel_reader(k_ref, j):
    def read(_, i, rows):
        value = k_ref[j, :, i * LANES : (i + 1) * LANES].astype(F32)
        return value[rows.start : rows.start + rows.size]

    return read


def mix_body(shape, v_ref, g_ref, k_ref, *refs):
    (fwd, bwd, cos, sin, out_ref, one_ref, carried_ref, xs, gs, left, right, freq) = refs
    cv = Convolver(*shape, v_ref.shape[1], (fwd, bwd, cos, sin, left, right, freq))
    n = cv.blocks
    cv.load(v_ref, xs)
    cv.load(g_ref, gs)

    def read(b, i, rows):
        return xs[b * HALF + i, rows, :]

    cv.spectrum(kernel_reader(k_ref, 0), 1, n)
    cv.spectrum(kernel_reader(k_ref, 1), 1, n + 1)
    cv.spectrum(read, n, 0)

    def gate(b, i, rows, value):
        r = b * HALF + i
        xs[r, rows, :] = (gs[r, rows, :] * value).astype(BF16).astype(F32)
        gs[r, rows, :] = value

    cv.convolve(0, n, False, gate)
    one_ref[...] = gs[...].astype(BF16)
    carried_ref[...] = xs[...].astype(BF16)
    cv.spectrum(read, n, 0)

    def keep(b, i, rows, value):
        gs[b * HALF + i, rows, :] = value

    cv.convolve(0, n + 1, False, keep)
    cv.store(gs, out_ref)


def unmix_body(shape, d_ref, g_ref, one_ref, k_ref, *refs):
    (fwd, bwd, cos, sin, out_ref, grad_ref, xs, gs, left, right, freq) = refs
    cv = Convolver(*shape, g_ref.shape[1], (fwd, bwd, cos, sin, left, right, freq))
    n = cv.blocks
    cv.load(d_ref, xs)
    cv.load(g_ref, gs)

    def read(b, i, rows):
        return xs[b * HALF + i, rows, :]

    cv.spectrum(kernel_reader(k_ref, 1), 1, n)
    cv.spectrum(read, n, 0)

    def gate(b, i, rows, value):
        r = b * HALF + i
        xs[r, rows, :] = (gs[r, rows, :] * value).astype(BF16).astype(F32)
        gs[r, rows, :] = value

    cv.convolve(0, n, True, gate)
    grad_ref[...] = xs[...].astype(BF16)
    gs[...] = gs[...] * one_ref[...].astype(F32)
    cv.store(gs, out_ref, 0)
    cv.spectrum(kernel_reader(k_ref, 0), 1, n)
    cv.spectrum(read, n, 0)

    def keep(b, i, rows, value):
        gs[b * HALF + i, rows, :] = value

    cv.convolve(0, n, True, keep)
    cv.store(gs, out_ref, 1)


def tap_body(shape, before, d_ref, v_ref, carried_ref, grad_ref, *refs):
    (fwd, bwd, cos, sin), refs = refs[:4], refs[4 + before :]
    (dk_ref, xs, gs, left, right, freq) = refs
    cv = Convolver(*shape, v_ref.shape[1], (fwd, bwd, cos, sin, left, right, freq))
    n = cv.blocks
    cv.load(d_ref, xs)
    cv.load(v_ref, gs)

    def reader(ref):
        return lambda b, i, rows: ref[b * HALF + i, rows, :]

    def half_reader(ref):
        def read(b, i, rows):
            return ref[b * HALF + i].astype(F32)[rows.start : rows.start + rows.size]

        return read

    def put(j):
        def write(_, i, rows, value):
            dk_ref[j, rows, i * LANES : (i + 1) * LANES] = value

        return write

    cv.spectrum(reader(xs), n, 0)
    cv.spectrum(half_reader(carried_ref), n, n)
    cv.taps(n, 0, put(1))
    cv.spectrum(half_reader(grad_ref), n, 0)
    cv.spectrum(reader(gs), n, n)
    cv.taps(n, 0, put(0))


def conv_sizes(gates):
    sources, groups, _, shard, length = gates.shape
    tile = 16
    pieces = length // (groups * LANES)
    total = sources * length
    return sources, groups, shard, length, tile, pieces, total // LANES, total // SPAN


def conv_scratch(tile, rows, blocks, spectra):
    return [
        pltpu.VMEM((rows, tile, LANES), F32),
        pltpu.VMEM((rows, tile, LANES), F32),
        pltpu.VMEM((blocks * FREQS, tile, 2 * LANES), F32),
        pltpu.VMEM((blocks * FREQS, tile, 2 * LANES), F32),
        pltpu.VMEM((spectra * FREQS, tile, 2 * LANES), F32),
    ]


def mix(gates, taps):
    q, g, shard, length, tile, pieces, rows, blocks = conv_sizes(gates)
    consts = tables()
    by_source = (q, None, None, tile, length)
    nat = pl.BlockSpec((None, rows, tile, LANES), lambda a, b: (a, 0, b, 0))
    return pl.pallas_call(
        functools.partial(mix_body, (q, g, pieces, blocks)),
        grid=(g, shard // tile),
        in_specs=[
            pl.BlockSpec(by_source, lambda a, b: (0, a, 1, b, 0)),
            pl.BlockSpec(by_source, lambda a, b: (0, a, 0, b, 0)),
            pl.BlockSpec((None, 2, tile, SPAN), lambda a, b: (a, 0, b, 0)),
        ]
        + [whole(c) for c in consts],
        out_specs=[pl.BlockSpec((q, None, tile, length), lambda a, b: (0, a, b, 0)), nat, nat],
        out_shape=[
            jax.ShapeDtypeStruct((q, g, shard, length), BF16),
            jax.ShapeDtypeStruct((g, rows, shard, LANES), BF16),
            jax.ShapeDtypeStruct((g, rows, shard, LANES), BF16),
        ],
        scratch_shapes=conv_scratch(tile, rows, blocks, blocks + 2),
        compiler_params=params(),
        name="mix",
    )(gates, gates, taps, *consts)


def unmix(grads, gates, conv_one, taps):
    q, g, shard, length, tile, pieces, rows, blocks = conv_sizes(gates)
    consts = tables()
    by_source = (q, None, None, tile, length)
    nat = pl.BlockSpec((None, rows, tile, LANES), lambda a, b: (a, 0, b, 0))
    return pl.pallas_call(
        functools.partial(unmix_body, (q, g, pieces, blocks)),
        grid=(g, shard // tile),
        in_specs=[
            pl.BlockSpec((q, None, tile, length), lambda a, b: (0, a, b, 0)),
            pl.BlockSpec(by_source, lambda a, b: (0, a, 0, b, 0)),
            nat,
            pl.BlockSpec((None, 2, tile, SPAN), lambda a, b: (a, 0, b, 0)),
        ]
        + [whole(c) for c in consts],
        out_specs=[
            pl.BlockSpec((q, None, 2, tile, length), lambda a, b: (0, a, 0, b, 0)),
            nat,
        ],
        out_shape=[
            jax.ShapeDtypeStruct((q, g, 2, shard, length), BF16),
            jax.ShapeDtypeStruct((g, rows, shard, LANES), BF16),
        ],
        scratch_shapes=conv_scratch(tile, rows, blocks, blocks + 1),
        compiler_params=params(),
        name="unmix",
    )(grads, gates, conv_one, taps, *consts)


def tap_grads(grads, gates, carried, grad_one, before=()):
    q, g, shard, length, tile, pieces, rows, blocks = conv_sizes(gates)
    consts = tables()
    nat = pl.BlockSpec((None, rows, tile, LANES), lambda a, b: (a, 0, b, 0))
    return pl.pallas_call(
        functools.partial(tap_body, (q, g, pieces, blocks), len(before)),
        grid=(g, shard // tile),
        in_specs=[
            pl.BlockSpec((q, None, tile, length), lambda a, b: (0, a, b, 0)),
            pl.BlockSpec((q, None, None, tile, length), lambda a, b: (0, a, 1, b, 0)),
            nat,
            nat,
        ]
        + [whole(c) for c in consts]
        + [pl.BlockSpec(memory_space=pl.ANY)] * len(before),
        out_specs=pl.BlockSpec((None, 2, tile, SPAN), lambda a, b: (a, 0, b, 0)),
        out_shape=jax.ShapeDtypeStruct((g, 2, shard, SPAN), F32),
        scratch_shapes=conv_scratch(tile, rows, blocks, 2 * blocks),
        compiler_params=params(),
        name="tap_grads",
    )(grads, gates, carried, grad_one, *consts, *before)


def standardise(stream):
    average = jnp.mean(stream, axis=0, keepdims=True)
    centered = stream - average
    inv_std = lax.rsqrt(jnp.mean(centered * centered, axis=0, keepdims=True) + EPS)
    return centered * inv_std, inv_std


def standardise_back(grad, gain, stream):
    unit, inv_std = standardise(stream)
    g = grad * gain
    mean_grad = jnp.mean(g, axis=0, keepdims=True)
    mean_cross = jnp.mean(g * unit, axis=0, keepdims=True)
    back = inv_std * (g - mean_grad - unit * mean_cross)
    gain_part = jnp.sum(grad * unit, axis=1, keepdims=True)
    bias_part = jnp.sum(grad, axis=1, keepdims=True)
    return back, gain_part, bias_part


def transposed(x):
    return jnp.transpose(x.astype(F32))


def column(row_ref):
    row = row_ref[...]
    return jnp.transpose(jnp.broadcast_to(row, (8, row.shape[1])))[:, 0:1]


def as_row(column):
    return jnp.transpose(jnp.broadcast_to(column, (column.shape[0], LANES)))[0:1]


def gelu_pair(x):
    z = jnp.abs(x) * math.sqrt(0.5)
    t = 1.0 / (1.0 + 0.3275911 * z)
    e = jnp.exp(-(z * z))
    poly = t * (
        0.127414796 + t * (-0.142248368 + t * (0.710706871 + t * (-0.726576014 + t * 0.530702714)))
    )
    tail = poly * e
    phi = jnp.where(x >= 0, 1.0 - tail, tail)
    return x * phi, phi + x * (e * (1.0 / math.sqrt(2 * math.pi)))


def first(axis_is_zero, refs, cut, body):
    if len(refs) == 1:
        body(refs[0].at[:, 0 : 2 * cut], refs[0].at[:, 2 * cut : 3 * cut])
        return

    @pl.when(axis_is_zero)
    def _():
        body(refs[0], refs[1].at[:, 0:cut])

    @pl.when(jnp.logical_not(axis_is_zero))
    def _():
        body(refs[1], refs[0].at[:, 0:cut])


class Pieces:
    def __init__(self, arrays, begins, rows):
        self.arrays, self.begins, self.rows = arrays, begins, rows

    def specs(self):
        mp, _, width = self.arrays[0].shape
        shape = (mp, self.rows, width)
        return [
            pl.BlockSpec(
                shape, lambda *_, at=begin // self.rows: (0, at, 0), pipeline_mode=pl.Buffered(1)
            )
            for begin in self.begins
        ]

    def __len__(self):
        return len(self.arrays)


SCALARS = pl.BlockSpec(memory_space=pltpu.SMEM)


def by_channel(blocks, groups):
    peers = blocks.shape[0] // groups
    order = [h * peers + q for q in range(peers) for h in range(groups)]
    return jnp.concatenate([blocks[m : m + 1] for m in order], axis=0)


def project_body(natural, ways, groups, place_ref, x_ref, gain_ref, bias_ref, *rest):
    dense, rest = rest[:ways], rest[ways:]
    if natural:
        s_ref, op_ref, two_ref, n_ref, pair_w, value_w = rest
        x = transposed(x_ref[...])
        s_ref[...] = x
    else:
        op_ref, two_ref, n_ref, pair_w, value_w = rest
        x = x_ref[...]
    mp, cut, t = two_ref.shape

    @pl.when(pl.program_id(0) == 0)
    def _():
        def body(pair, value):
            pair_w[...] = by_channel(pair, groups)
            value_w[...] = by_channel(value, groups)

        first(place_ref[0] == 0, dense, cut, body)

    unit, _ = standardise(x)
    normed = unit * column(gain_ref) + column(bias_ref)
    n_ref[...] = transposed(normed).astype(BF16)
    normed = normed.astype(BF16)
    width = normed.shape[0]
    y = jnp.dot(
        pair_w[...].reshape(mp * 2 * cut, width), normed, preferred_element_type=F32
    )
    y = y.astype(BF16).reshape(mp, 2, cut, t)
    op_ref[:, 0] = y[:, 0]
    two_ref[...] = y[:, 1]
    y = jnp.dot(value_w[...].reshape(mp * cut, width), normed, preferred_element_type=F32)
    op_ref[:, 1] = y.astype(BF16).reshape(mp, cut, t)


def token_tile(length, most=256):
    return min(length, most)


def project(natural, groups, place, x, dense, gain, bias, cut):
    mp, _, width = dense.arrays[0].shape
    length = x.shape[0] if natural else x.shape[1]
    t = token_tile(length)
    tall = pl.BlockSpec((t, width), lambda i: (i, 0))
    flat = pl.BlockSpec((width, t), lambda i: (0, i))
    out_specs = [
        pl.BlockSpec((mp, 2, cut, t), lambda i: (0, 0, 0, i)),
        pl.BlockSpec((mp, cut, t), lambda i: (0, 0, i)),
        tall,
    ]
    out_shape = [
        jax.ShapeDtypeStruct((mp, 2, cut, length), BF16),
        jax.ShapeDtypeStruct((mp, cut, length), BF16),
        jax.ShapeDtypeStruct((length, width), BF16),
    ]
    if natural:
        out_specs.insert(0, flat)
        out_shape.insert(0, jax.ShapeDtypeStruct((width, length), F32))
    return pl.pallas_call(
        functools.partial(project_body, natural, len(dense), groups),
        grid=(length // t,),
        in_specs=[SCALARS, tall if natural else flat, whole(gain), whole(bias)] + dense.specs(),
        out_specs=out_specs,
        out_shape=out_shape,
        scratch_shapes=[
            pltpu.VMEM((mp, 2 * cut, width), BF16),
            pltpu.VMEM((mp, cut, width), BF16),
        ],
        compiler_params=params(),
        name="project",
    )(place, x, gain, bias, *dense.arrays)


def ff_chunks(refs):
    mp, rows, width = refs[0].shape
    part = rows // 2
    step = min(mp, width // part)
    size = step * part
    for p, ref in enumerate(refs):
        for j in range(mp // step):
            begin = (p * (mp // step) + j) * size
            yield ref, slice(j * step, (j + 1) * step), part, slice(begin, begin + size)


def forward_body(natural, ways, s_ref, c_ref, g_ref, wo_ref, gain_ref, bias_ref, *rest):
    ff, rest = rest[:ways], rest[ways:]
    s1_ref, s2_ref, h_ref, d_ref, n_ref, gated_ref, wo_t, down_t = rest
    width = ff[0].shape[-1]

    @pl.when(pl.program_id(0) == 0)
    def _():
        wo_t[...] = transposed(wo_ref[...]).astype(BF16)
        for ref, blocks, part, units in ff_chunks(ff):
            block = ref[blocks, part:, :].reshape(units.stop - units.start, width)
            down_t[:, units] = transposed(block).astype(BF16)

    gated = (g_ref[...].astype(F32) * c_ref[...].astype(F32)).astype(BF16)
    gated_ref[...] = gated
    s1 = s_ref[...] + jnp.dot(wo_t[...], gated, preferred_element_type=F32)
    s1_ref[...] = s1
    unit, _ = standardise(s1)
    normed = unit * column(gain_ref) + column(bias_ref)
    n_ref[...] = transposed(normed).astype(BF16)
    normed = normed.astype(BF16)
    total = s1
    for ref, blocks, part, units in ff_chunks(ff):
        up = ref[blocks, 0:part, :].reshape(units.stop - units.start, width)
        hidden, slope = gelu_pair(jnp.dot(up, normed, preferred_element_type=F32))
        hidden = hidden.astype(BF16)
        h_ref[units, :] = hidden
        d_ref[units, :] = slope.astype(BF16)
        total = total + jnp.dot(down_t[:, units], hidden, preferred_element_type=F32)
    s2_ref[...] = transposed(total) if natural else total


def forward_block(natural, stream, conv_two, gate_two, w_out, ff, gain, bias):
    width, length = stream.shape
    channels = w_out.shape[0]
    hidden = len(ff) * ff.arrays[0].shape[0] * ff.rows // 2
    t = token_tile(length)
    tall = pl.BlockSpec((t, width), lambda i: (i, 0))
    flat = pl.BlockSpec((width, t), lambda i: (0, i))
    chan = pl.BlockSpec((channels, t), lambda i: (0, i))
    high = pl.BlockSpec((hidden, t), lambda i: (0, i))
    last = (length, width) if natural else (width, length)
    return pl.pallas_call(
        functools.partial(forward_body, natural, len(ff)),
        grid=(length // t,),
        in_specs=[flat, chan, chan, whole(w_out), whole(gain), whole(bias)] + ff.specs(),
        out_specs=[flat, tall if natural else flat, high, high, tall, chan],
        out_shape=[
            jax.ShapeDtypeStruct((width, length), F32),
            jax.ShapeDtypeStruct(last, F32),
            jax.ShapeDtypeStruct((hidden, length), BF16),
            jax.ShapeDtypeStruct((hidden, length), BF16),
            jax.ShapeDtypeStruct((length, width), BF16),
            jax.ShapeDtypeStruct((channels, length), BF16),
        ],
        scratch_shapes=[pltpu.VMEM((width, channels), BF16), pltpu.VMEM((width, hidden), BF16)],
        compiler_params=params(),
        name="forward_block",
    )(stream, conv_two, gate_two, w_out, gain, bias, *ff.arrays)


def backward_body(natural, ways, gs_ref, d_ref, s1_ref, c_ref, g_ref, wo_ref, gain_ref, *rest):
    ff, rest = rest[:ways], rest[ways:]
    pre_ref, gs1_ref, gc_ref, two_ref, dm_ref, do_ref, gain_out, bias_out = rest[:8]
    up_n, gain_sum, bias_sum = rest[8:]
    width = ff[0].shape[-1]

    @pl.when(pl.program_id(0) == 0)
    def _():
        gain_sum[...] = jnp.zeros_like(gain_sum)
        bias_sum[...] = jnp.zeros_like(bias_sum)
        for ref, blocks, part, units in ff_chunks(ff):
            block = ref[blocks, 0:part, :].reshape(units.stop - units.start, width)
            up_n[:, units] = transposed(block).astype(BF16)

    if natural:
        dm_ref[...] = gs_ref[...]
        grad = transposed(gs_ref[...])
    else:
        grad = gs_ref[...]
        dm_ref[...] = transposed(grad).astype(BF16)
    dm = grad.astype(BF16)
    total = None
    for ref, blocks, part, units in ff_chunks(ff):
        down = ref[blocks, part:, :].reshape(units.stop - units.start, width)
        pre = jnp.dot(down, dm, preferred_element_type=F32) * d_ref[units, :].astype(F32)
        pre = pre.astype(BF16)
        pre_ref[units, :] = pre
        total = add(total, jnp.dot(up_n[:, units], pre, preferred_element_type=F32))
    back, gain_part, bias_part = standardise_back(total, column(gain_ref), s1_ref[...])
    gain_sum[...] += gain_part
    bias_sum[...] += bias_part

    @pl.when(pl.program_id(0) == pl.num_programs(0) - 1)
    def _():
        gain_out[...] = as_row(gain_sum[...])
        bias_out[...] = as_row(bias_sum[...])

    grad = grad + back
    gs1_ref[...] = grad
    do_ref[...] = transposed(grad).astype(BF16)
    gated = jnp.dot(wo_ref[...], grad.astype(BF16), preferred_element_type=F32)
    gated = gated.astype(BF16).astype(F32)
    gc_ref[...] = (gated * g_ref[...].astype(F32)).astype(BF16)
    two_ref[...] = (gated * c_ref[...].astype(F32)).astype(BF16)


def backward_block(natural, grad, slope, s1, conv_two, gate_two, w_out, ff, gain):
    width, length = s1.shape
    channels = w_out.shape[0]
    hidden = slope.shape[0]
    t = token_tile(length, 512)
    tall = pl.BlockSpec((t, width), lambda i: (i, 0))
    flat = pl.BlockSpec((width, t), lambda i: (0, i))
    chan = pl.BlockSpec((channels, t), lambda i: (0, i))
    high = pl.BlockSpec((hidden, t), lambda i: (0, i))
    row = pl.BlockSpec((1, width), lambda i: (0, 0))
    return pl.pallas_call(
        functools.partial(backward_body, natural, len(ff)),
        grid=(length // t,),
        in_specs=[tall if natural else flat, high, flat, chan, chan]
        + [whole(w_out), whole(gain)]
        + ff.specs(),
        out_specs=[high, flat, chan, chan, tall, tall, row, row],
        out_shape=[
            jax.ShapeDtypeStruct((hidden, length), BF16),
            jax.ShapeDtypeStruct((width, length), F32),
            jax.ShapeDtypeStruct((channels, length), BF16),
            jax.ShapeDtypeStruct((channels, length), BF16),
            jax.ShapeDtypeStruct((length, width), BF16),
            jax.ShapeDtypeStruct((length, width), BF16),
            jax.ShapeDtypeStruct((1, width), F32),
            jax.ShapeDtypeStruct((1, width), F32),
        ],
        scratch_shapes=[
            pltpu.VMEM((width, hidden), BF16),
            pltpu.VMEM((width, 1), F32),
            pltpu.VMEM((width, 1), F32),
        ],
        compiler_params=params(),
        name="backward_block",
    )(grad, slope, s1, conv_two, gate_two, w_out, gain, *ff.arrays)


def unproject_body(natural, ways, groups, place_ref, gm_ref, two_ref, s_ref, gs_ref, gain_ref, *rest):
    dense, rest = rest[:ways], rest[ways:]
    out_ref, gain_out, bias_out, pair_t, value_t, gain_sum, bias_sum = rest
    mp, cut, t = two_ref.shape
    width = dense[0].shape[-1]

    @pl.when(pl.program_id(0) == 0)
    def _():
        gain_sum[...] = jnp.zeros_like(gain_sum)
        bias_sum[...] = jnp.zeros_like(bias_sum)

        def body(pair, value):
            rows = by_channel(pair, groups).reshape(mp * 2 * cut, width)
            pair_t[...] = transposed(rows).astype(BF16)
            rows = by_channel(value, groups).reshape(mp * cut, width)
            value_t[...] = transposed(rows).astype(BF16)

        first(place_ref[0] == 0, dense, cut, body)

    pair = jnp.concatenate([gm_ref[:, 0:1], two_ref[...][:, None]], axis=1)
    grad = jnp.dot(pair_t[...], pair.reshape(mp * 2 * cut, t), preferred_element_type=F32)
    value = gm_ref[:, 1].reshape(mp * cut, t)
    grad = grad + jnp.dot(value_t[...], value, preferred_element_type=F32)
    back, gain_part, bias_part = standardise_back(grad, column(gain_ref), s_ref[...])
    gain_sum[...] += gain_part
    bias_sum[...] += bias_part

    @pl.when(pl.program_id(0) == pl.num_programs(0) - 1)
    def _():
        gain_out[...] = as_row(gain_sum[...])
        bias_out[...] = as_row(bias_sum[...])

    result = gs_ref[...] + back
    out_ref[...] = transposed(result) if natural else result


def unproject(natural, groups, place, grad_mixed, grad_two, dense, stream, grad, gain):
    width, length = stream.shape
    mp, cut, _ = grad_two.shape
    t = token_tile(length)
    tall = pl.BlockSpec((t, width), lambda i: (i, 0))
    flat = pl.BlockSpec((width, t), lambda i: (0, i))
    row = pl.BlockSpec((1, width), lambda i: (0, 0))
    last = (length, width) if natural else (width, length)
    return pl.pallas_call(
        functools.partial(unproject_body, natural, len(dense), groups),
        grid=(length // t,),
        in_specs=[
            SCALARS,
            pl.BlockSpec((mp, 2, cut, t), lambda i: (0, 0, 0, i)),
            pl.BlockSpec((mp, cut, t), lambda i: (0, 0, i)),
            flat,
            flat,
            whole(gain),
        ]
        + dense.specs(),
        out_specs=[tall if natural else flat, row, row],
        out_shape=[
            jax.ShapeDtypeStruct(last, F32),
            jax.ShapeDtypeStruct((1, width), F32),
            jax.ShapeDtypeStruct((1, width), F32),
        ],
        scratch_shapes=[
            pltpu.VMEM((width, mp * 2 * cut), BF16),
            pltpu.VMEM((width, mp * cut), BF16),
            pltpu.VMEM((width, 1), F32),
            pltpu.VMEM((width, 1), F32),
        ],
        compiler_params=params(),
        name="unproject",
    )(place, grad_mixed, grad_two, stream, grad, gain, *dense.arrays)


GROUP = 8


class Plain:
    def __init__(self, ways, mp, left, right):
        self.left = left.reshape(ways, mp, left.shape[0] // (ways * mp), left.shape[1])
        self.rows, self.rights = self.left.shape[2], [right]

    def lefts(self):
        _, _, part, length = self.left.shape
        shape = (self.left.shape[0], GROUP, part, length)
        spec = pl.BlockSpec(shape, lambda i, place: (0, i ^ (place[1] // GROUP), 0, 0))
        return [(self.left, spec)]

    def pieces(self, way, lefts, rights):
        ways, count, part, length = lefts[0].shape
        for w in range(ways):
            y = rows_product(lefts[0][w].reshape(count * part, length), rights[0])
            yield y.reshape(count, part, -1)


class Mixed:
    def __init__(self, ways, groups, lefts, rights):
        self.ways, self.rights = ways, rights
        self.arrays = [
            x.reshape((x.shape[0] // groups, groups) + x.shape[1:]) for x in lefts
        ]
        self.rows = 2 * self.arrays[0].shape[-2] // ways

    def lefts(self):
        result = []
        for x in self.arrays:
            shape = (GROUP, None) + x.shape[2:]
            zeros = (0,) * (x.ndim - 2)
            runs = x.shape[0] // GROUP

            def index(i, place, runs=runs, zeros=zeros):
                run = i ^ (place[1] // GROUP)
                return (lax.rem(run, runs), run // runs) + zeros

            result.append((x, pl.BlockSpec(shape, index)))
        return result

    def pieces(self, way, lefts, rights):
        if len(lefts) == 1:
            lefts = [lefts[0].at[:, 0], lefts[0].at[:, 1]]
        made = []
        for left, right in zip(lefts, (rights * 2)[:2]):
            count, cut, length = left.shape
            y = rows_product(left[...].reshape(count * cut, length), right)
            made.append(y.reshape(count, cut, -1))
        a, b = made
        for w in range(self.ways):
            if self.ways == 1:
                yield jnp.concatenate([a, b], axis=1)
            else:
                yield jnp.where(way ^ w == 0, a, b)


def rows_product(left, right):
    return jnp.dot(left, right[...], preferred_element_type=F32).astype(BF16)


def grads_body(ways, jobs, before, place_ref, *refs):
    counts = [len(job.lefts()) for job in jobs]
    lefts, refs = refs[: sum(counts)], refs[sum(counts) :]
    rights, refs = refs[: sum(len(j.rights) for j in jobs)], refs[sum(len(j.rights) for j in jobs) :]
    outs = refs[before:]
    low = place_ref[1] % GROUP
    begin = 0
    for job, count in zip(jobs, counts):
        mine, lefts = lefts[:count], lefts[count:]
        right, rights = rights[: len(job.rights)], rights[len(job.rights) :]
        for out, values in zip(outs, job.pieces(place_ref[0], list(mine), list(right))):
            for i in range(GROUP):
                out[i ^ low, begin : begin + job.rows, :] = values[i]
        begin += job.rows


def weight_grads(name, ways, mp, place, jobs, before=()):
    width = jobs[0].rights[0].shape[1]
    rows = sum(job.rows for job in jobs)
    lefts = [pair for job in jobs for pair in job.lefts()]
    rights = [right for job in jobs for right in job.rights]

    def kept(a):
        return pl.BlockSpec(a.shape, lambda i, place: (0, 0), pipeline_mode=pl.Buffered(1))

    out = pl.BlockSpec((GROUP, rows, width), lambda i, place: (i, 0, 0))
    return pl.pallas_call(
        functools.partial(grads_body, ways, jobs, len(before)),
        grid_spec=pltpu.PrefetchScalarGridSpec(
            num_scalar_prefetch=1,
            grid=(mp // GROUP,),
            in_specs=[spec for _, spec in lefts]
            + [kept(a) for a in rights]
            + [pl.BlockSpec(memory_space=pl.ANY)] * len(before),
            out_specs=[out] * ways,
        ),
        out_shape=[jax.ShapeDtypeStruct((mp, rows, width), BF16)] * ways,
        compiler_params=params(),
        name=name,
    )(place, *[x for x, _ in lefts], *rights, *before)


def together(*arrays):
    return lax.optimization_barrier(arrays)


def flip(x, axis, size, bit):
    return lax.ppermute(x, axis, [(i, i ^ bit) for i in range(size)])


def dp_sum(x, dp):
    return butterfly(x, [("dp", dp)])


def butterfly(x, sizes):
    for axis, size in sizes:
        bit = 1
        while bit < size:
            x = x + flip(x, axis, size, bit)
            bit *= 2
    return x


def stage_order(mp, swapped):
    bits = list(range(mp.bit_length() - 1))
    first = [[1], [0]] if swapped else [[0], [1]]
    return first + [bits[i : i + 2] for i in range(2, len(bits), 2)]


def total(parts):
    value = parts[0].astype(F32)
    for part in parts[1:]:
        value = value + part.astype(F32)
    return value


class Hop:
    def __init__(self, x, axis, size, mask):
        self.x, self.where = x, (axis, size, mask)

    def start(self):
        return flip(self.x, *self.where)


def masks(bits):
    return [sum(((k >> i) & 1) << b for i, b in enumerate(bits)) for k in range(1 << len(bits))]


def scatter_steps(terms, left, mp, stages):
    for stage in stages:
        axes = [left.index(b) for b in stage]
        left = [b for b in left if b not in stage]

        def take(t, k):
            index = [slice(None)] * t.ndim
            for i, axis in enumerate(axes):
                index[axis] = (k >> i) & 1
            return t[tuple(index)]

        sums = [
            total([take(t, k) for t in terms]).astype(BF16) for k in range(1 << len(stage))
        ]
        got = yield [Hop(x, "mp", mp, mask) for x, mask in zip(sums[1:], masks(stage)[1:])]
        terms = sums[:1] + got
    return terms


def scatter_chain(terms, mp, stages, split=False):
    bits = mp.bit_length() - 1
    left = list(range(bits - 1, -1, -1))
    terms = [t.reshape((2,) * bits + t.shape[1:]) for t in terms]
    if split:
        rows = terms[0].shape[-2]
        middle = (rows // 2 + 15) // 16 * 16
        orders = stages[:2], stages[1::-1]
        parts = [
            scatter_steps([t[..., span, :] for t in terms], left, mp, order)
            for span, order in zip((slice(0, middle), slice(middle, rows)), orders)
        ]
        hops = [next(part) for part in parts]
        got = yield hops[0] + hops[1]
        hops = [part.send([x]) for part, x in zip(parts, got)]
        got = yield hops[0] + hops[1]
        ended = []
        for part, x in zip(parts, got):
            try:
                part.send([x])
            except StopIteration as end:
                ended.append(end.value)
        terms = [jnp.concatenate(pair, axis=-2) for pair in zip(*ended)]
        left = [b for b in left if b not in stages[0] + stages[1]]
        stages = stages[2:]
    terms = yield from scatter_steps(terms, left, mp, stages)
    return total(terms)


def in_two(x):
    high = x.astype(BF16)
    return jnp.concatenate([high, (x - high.astype(F32)).astype(BF16)], axis=0)


def from_two(x):
    half = x.shape[0] // 2
    return x[:half].astype(F32) + x[half:].astype(F32)


def last_chain(terms, norms, mp, stages):
    bits = mp.bit_length() - 1
    left = list(range(bits - 1, -1, -1))
    terms = [t.reshape((2,) * bits + t.shape[1:]) for t in terms]
    width = norms.shape[1]
    for stage in stages:
        axes = [left.index(b) for b in stage]
        left = [b for b in left if b not in stage]
        sums = []
        for k in range(1 << len(stage)):
            index = [slice(None)] * terms[0].ndim
            for i, axis in enumerate(axes):
                index[axis] = (k >> i) & 1
            sums.append(total([t[tuple(index)] for t in terms]).astype(BF16))
        own = in_two(norms)
        shape, rows = sums[0].shape, sums[0].size // width
        got = yield [
            Hop(jnp.concatenate([x.reshape(rows, width), own], axis=0), "mp", mp, mask)
            for x, mask in zip(sums[1:], masks(stage)[1:])
        ]
        terms = sums[:1] + [x[:rows].reshape(shape) for x in got]
        values = [from_two(x) for x in [own] + [x[rows:] for x in got]]
        while len(values) > 1:
            values = [a + b for a, b in zip(values[0::2], values[1::2])]
        norms = values[0]
    return total(terms), norms


def gather_chain(x, mp, stages):
    me = lax.axis_index("mp")
    done = []
    for stage in stages:
        got = yield [Hop(x, "mp", mp, mask) for mask in masks(stage)[1:]]
        pieces = [x] + got
        place = sum(((me >> b) & 1) << i for i, b in enumerate(stage))
        count = len(pieces)
        if count == 2:
            pieces = [jnp.where(place == a, x, got[0]) for a in range(2)]
        else:
            pieces = [
                lax.select_n(place, *[pieces[a ^ v] for v in range(count)]) for a in range(count)
            ]
        for i, bit in enumerate(stage):
            axis = sum(b > bit for b in done)
            pieces = [
                jnp.stack([pieces[j], pieces[j + 1]], axis=axis) for j in range(0, len(pieces), 2)
            ]
            done.append(bit)
        x = pieces[0]
    return x.reshape((mp,) + x.shape[len(done) :])


def chip_chain(pieces, dp):
    if len(pieces) == 1:
        return pieces
    got = yield [Hop(pieces[1], "dp", dp, 1)]
    return [pieces[0]] + got


class Chains:
    def __init__(self):
        self.waiting, self.results = {}, {}

    def add(self, name, chain):
        self.step(name, chain, None)

    def step(self, name, chain, value):
        try:
            self.waiting[name] = chain, chain.send(value)
        except StopIteration as end:
            self.waiting.pop(name, None)
            self.results[name] = end.value

    def hops(self):
        return [hop for _, hops in self.waiting.values() for hop in hops]

    def operands(self):
        return [hop.x for hop in self.hops()]

    def tie(self, *others):
        hops = self.hops()
        tied = together(*[hop.x for hop in hops], *others)
        for hop, x in zip(hops, tied):
            hop.x = x
        return tied[len(hops) :]

    def start(self):
        return {name: [hop.start() for hop in hops] for name, (_, hops) in self.waiting.items()}

    def finish(self, started, *others):
        flat = [x for got in started.values() for x in got]
        tied = list(together(*flat, *others))
        for name, got in started.items():
            mine, tied = tied[: len(got)], tied[len(got) :]
            self.step(name, self.waiting[name][0], mine)
        return tied


def program(dp, mp, inputs, cotangent, norm_gain, norm_bias, in_weight, kernels, *rest):
    out_weight, up_weight, down_weight, taps_kept = rest
    layers = in_weight.shape[0]
    groups, chunk, width = inputs.shape
    peers = mp // groups
    shard, hidden = in_weight.shape[3], up_weight.shape[2]
    length = groups * chunk
    cut = -(-shard // 16) * 16
    ways = 2 if dp == 2 and shard == cut and hidden % 32 == 0 else 1
    part = hidden // ways
    dense_rows = 4 * cut // ways
    me, way = lax.axis_index("mp"), lax.axis_index("dp")
    place = jnp.stack([way, me]).astype(jnp.int32)
    zero_half = me // peers == 0
    swap = [(i, (i + peers) % mp) for i in range(mp)]
    halves = [[h * peers + q for q in range(peers)] for h in range(groups)]

    def ordered(own, got):
        return jnp.stack([jnp.where(zero_half, own, got), jnp.where(zero_half, got, own)])

    def pick(x):
        return jnp.where(zero_half, x[0], x[1]), jnp.where(zero_half, x[1], x[0])

    def to_one_sequence(x):
        own, other = pick(x)
        return ordered(own, lax.ppermute(other, "mp", swap)).reshape(length, width)

    def to_two_sequences(x):
        own, other = pick(x.reshape(groups, chunk, width))
        got = lax.ppermute(other.astype(BF16), "mp", swap)
        return ordered(own, got.astype(F32))

    def exchange(x):
        return lax.all_to_all(
            x, "mp", split_axis=0, concat_axis=0, tiled=True, axis_index_groups=halves
        )

    def widen(x, axis):
        pads = [(0, 0)] * x.ndim
        pads[axis] = (0, cut - shard)
        return x if cut == shard else jnp.pad(x, pads)

    dense = [jnp.transpose(in_weight[:, :, j], (0, 2, 1)) for j in range(3)] + [out_weight]
    dense = jnp.concatenate([widen(d, 1) for d in dense], axis=1)
    up = jnp.transpose(up_weight, (0, 2, 1))

    def my_rows(x, rows):
        return lax.dynamic_slice_in_dim(x, way * rows, rows, 1) if ways > 1 else x

    dense = my_rows(dense, dense_rows)
    ff = jnp.concatenate([my_rows(up, part), my_rows(down_weight, part)], axis=1)

    def gather(x):
        x = lax.all_gather(x, "mp", axis=0)
        return [x, flip(x, "dp", dp, 1)] if ways > 1 else [x]

    def gathered(x):
        return lax.all_gather(x, "mp", axis=0)

    def shared(x):
        return [x, flip(x, "dp", dp, 1)] if ways > 1 else [x]

    def out_matrix(pieces):
        skip = dense_rows - cut
        rows = [
            a[:, begin + skip : begin + dense_rows]
            for a, begin in zip(pieces.arrays, pieces.begins)
        ]
        rows = jnp.where(way == 1, rows[0], rows[1]) if ways > 1 else rows[0]
        rows = rows.reshape(groups, peers, cut, width)
        return jnp.swapaxes(rows, 0, 1).reshape(mp * cut, width)

    keep = jnp.arange(kernels.shape[-1])[None, :] < taps_kept[:, None]
    kept = jnp.where(keep[:, None, None, :], kernels, jnp.zeros_like(kernels))
    kept = widen(kept, 2)
    taps = []

    def dense_chains(layer):
        result = Chains()
        bits = mp.bit_length() - 1
        for i in range(2):
            rows = dense[layer, i * dense_rows // 2 : (i + 1) * dense_rows // 2]
            stages = [[b] for b in range(bits - 1, 1, -1)] + [[1 - i], [i]]
            result.add(i, gather_chain(rows, mp, stages))
        return result

    chains = dense_chains(0)
    own, other = pick(inputs)
    mine, other = chains.tie(ff.reshape(-1, width), other)
    ff_mine = gathered(mine)
    (other,) = chains.finish(chains.start(), other)
    moves = [other[: chunk // 2], other[chunk // 2 :], kept[0]]
    moved = []
    while len(moved) < 3:
        now = moves[len(moved)]
        started = chains.start()
        got = lax.ppermute(now, "mp", swap)
        if len(moved) < 2:
            got, moves[len(moved) + 1] = chains.finish(started, got, moves[len(moved) + 1])
        else:
            (got,) = chains.finish(started, got)
        moved.append(got)
    while chains.waiting:
        chains.finish(chains.start())
    dense_mine = jnp.concatenate([chains.results.pop(i) for i in range(2)], axis=1)
    other = jnp.concatenate(moved[:2], axis=0)
    got_taps = moved[2]
    stream = ordered(own, other).reshape(length, width)
    none = [0] * ways
    dense_all = [Pieces(shared(dense_mine), none, dense_rows)]

    gains = norm_gain[:, :, None]
    biases = norm_bias[:, :, None]
    saved, out_all = [], []
    own_grad, grad = pick(cotangent)
    less = chunk // 32 * 12
    halves_of_grad = [grad[:less], grad[less:]]
    for layer in range(layers):
        natural = layer == 0
        more = layer + 1 < layers
        got = project(
            natural,
            groups,
            place,
            stream,
            dense_all[layer],
            gains[layer, 0],
            biases[layer, 0],
            cut,
        )
        if natural:
            stream, got = got[0], got[1:]
        operand, gate_two, normed_one = got
        gates = exchange(operand.reshape(peers, groups, 2, cut, length))
        taps.append(ordered(kept[layer], got_taps))
        if more:
            following = Chains()
            whole_bits = list(range(mp.bit_length() - 1))
            stages = [whole_bits[i : i + 2] for i in range(2, len(whole_bits), 2)]
            following.add(0, gather_chain(dense[layer + 1], mp, stages + [whole_bits[:2]]))
            (gates,) = following.tie(gates)
            started = following.start()
        if natural:
            ff_mine, gates = together(ff_mine, gates)
            ff_pair = shared(ff_mine)
        conv_two, conv_one, carried = mix(gates, taps[layer])
        out_all.append(out_matrix(dense_all[layer]))
        if more:
            (conv_two,) = following.finish(started, conv_two)
        conv_two = exchange(conv_two).reshape(mp * cut, length)
        if natural:
            conv_two, *ff_pair = together(conv_two, *ff_pair)
            ff_all = [Pieces(ff_pair, [2 * part * i] * ways, 2 * part) for i in range(layers)]
        if more:
            got_taps, conv_two = following.tie(kept[layer + 1], conv_two)
            started = following.start()
            got_taps = lax.ppermute(got_taps, "mp", swap)
        half = None
        if layer >= layers - 2:
            half = halves_of_grad[layer - layers + 2]
            half, conv_two = together(half, conv_two)
            half = lax.ppermute(half, "mp", swap)
        gate_two = gate_two.reshape(mp * cut, length)
        s1, s2, active, slope, normed_two, gated = forward_block(
            layer == layers - 1,
            stream,
            conv_two,
            gate_two,
            out_all[layer],
            ff_all[layer],
            gains[layer, 1],
            biases[layer, 1],
        )
        if half is not None:
            half, s2 = together(half, s2)
            halves_of_grad[layer - layers + 2] = half
        if more:
            got_taps, s2 = following.finish(started, got_taps, s2)
            while following.waiting:
                following.finish(following.start())
            dense_next = following.results[0]
            dense_all.append(Pieces(shared(dense_next), none, dense_rows))
        saved.append(
            (stream, normed_one, gates, conv_one, carried, conv_two, gate_two)
            + (s1, active, slope, normed_two, gated)
        )
        stream = s2
    own_output, other = pick(stream.reshape(groups, chunk, width))
    other = other.astype(BF16)
    got_output = lax.ppermute(other[: chunk // 2], "mp", swap)
    other_output = other[chunk // 2 :]
    grad = ordered(own_grad, jnp.concatenate(halves_of_grad, axis=0)).reshape(length, width)

    gain_rows, bias_rows = [None] * layers, [None] * layers
    dks = [None] * layers
    later = None
    for layer in reversed(range(layers)):
        (s0, normed_one, gates, conv_one, carried, conv_two, gate_two) = saved[layer][:7]
        (s1, active, slope, normed_two, gated) = saved[layer][7:]
        pre, grad, grad_conv, grad_two, dm, do, gain_two, bias_two = backward_block(
            layer == layers - 1,
            grad,
            slope,
            s1,
            conv_two,
            gate_two,
            out_all[layer],
            ff_all[layer],
            gains[layer, 1],
        )
        gain_rows[layer], bias_rows[layer] = [None, gain_two], [None, bias_two]
        mixed = None
        if later is not None:
            mixed, grad_conv = together(later[0], grad_conv)
            got_dk, grad_conv = chains.finish(started, got_dk, grad_conv)
            dks[layer + 1] = own_dk.astype(F32) + got_dk.astype(F32)
        if layer == layers - 1:
            got_output, grad_conv = together(got_output, grad_conv)
        grad_conv = exchange(grad_conv.reshape(peers, groups, cut, length))
        grad_two = grad_two.reshape(mp, cut, length)
        up_job = Plain(ways, mp, pre, normed_two)
        down_job = Plain(ways, mp, active, dm)
        two_rows = [grad_two, gated.reshape(mp, cut, length)]
        mixed_job = Mixed(ways, groups, two_rows, [normed_one, do])
        late_jobs = [] if mixed is None else [Mixed(ways, groups, [mixed], [later[1]])]
        jobs = [up_job, down_job, mixed_job] + late_jobs
        early = weight_grads("early_grads", ways, mp, place, jobs)
        grad_conv, *early = together(grad_conv, *early)
        if layer == layers - 1:
            other_output, grad_conv = together(other_output, grad_conv)
            more_output = lax.ppermute(other_output, "mp", swap)
        chains.add(("flip", layer), chip_chain(early, dp))
        (grad_conv,) = chains.tie(grad_conv)
        started = chains.start()
        grad_mixed, grad_one = unmix(grad_conv, gates, conv_one, taps[layer])
        (grad_mixed,) = chains.finish(started, grad_mixed)
        if layer == layers - 1:
            more_output, grad_mixed = together(more_output, grad_mixed)
        grad_mixed = exchange(grad_mixed).reshape(mp, 2, cut, length)
        if layer == layers - 1:
            output = jnp.concatenate([got_output, more_output], axis=0)
            output = ordered(own_output, output.astype(F32))
            output, grad_mixed = together(output, grad_mixed)
        terms = chains.results.pop(("flip", layer))
        stages = stage_order(mp, 0)
        if layer == 0:
            stages = [[b] for stage in stages for b in stage]
        chains.add(layer, scatter_chain(terms, mp, stages, True))
        dk = tap_grads(grad_conv, gates, carried, grad_one, [] if layer else chains.operands())
        grad_mixed, dk = together(grad_mixed, dk)
        own_dk, other_dk = pick(dk.astype(BF16))
        if layer:
            later = grad_mixed, normed_one
        else:
            started = chains.start()
            got_dk = lax.ppermute(other_dk, "mp", swap)
            late_job = Mixed(ways, groups, [grad_mixed], [normed_one])
            late = weight_grads("late_grads", ways, mp, place, [late_job])
            grad_mixed, *late = together(grad_mixed, *late)
            tail = Chains()
            tail.add("late", chip_chain(late, dp))
            last = tail.start()
        grad, gain_one, bias_one = unproject(
            layer == 0,
            groups,
            place,
            grad_mixed,
            grad_two,
            dense_all[layer],
            s0,
            grad,
            gains[layer, 0],
        )
        gain_rows[layer][0], bias_rows[layer][0] = gain_one, bias_one
        if layer:
            grad, other_dk = chains.tie(grad, other_dk)
            got_dk = lax.ppermute(other_dk, "mp", swap)
            started = chains.start()

    grad, got_dk = tail.finish(last, grad, got_dk)
    own, other = pick(grad.reshape(groups, chunk, width))
    swapped = lax.ppermute(other.astype(BF16), "mp", swap)
    (gain_rows[0][0],) = chains.finish(started, gain_rows[0][0])
    bits = list(range(mp.bit_length() - 1))
    quarters = [bits[i : i + 2] for i in range(0, len(bits), 2)]
    norms = jnp.stack([jnp.stack([jnp.stack(r) for r in rows]) for rows in (gain_rows, bias_rows)])
    shape = norms.shape[:-2] + (width,)
    norms = norms.reshape(-1, width)
    tail.add("late", last_chain(tail.results.pop("late"), norms, mp, quarters))
    first_round = True
    while chains.waiting or tail.waiting:
        started, last = chains.start(), tail.start()
        if started:
            chains.finish(started)
        if first_round:
            (swapped,) = tail.finish(last, swapped)
        elif last:
            tail.finish(last)
        first_round = False
    input_grad = ordered(own, swapped.astype(F32))
    dks[0] = own_dk.astype(F32) + got_dk.astype(F32)
    dk = jnp.stack(dks).astype(BF16).astype(F32)
    late, norms = tail.results.pop("late")
    found = [chains.results.pop(layer) for layer in reversed(range(layers))]
    final = [x.astype(BF16) for x in found + [late]]
    if ways == 1:
        dk, norms = dp_sum(dk, dp), dp_sum(norms, dp)
        final = [[dp_sum(x, dp)] for x in found + [late]]
    else:
        dk = dk + flip(dk.astype(BF16), "dp", dp, 1).astype(F32)
        norms = in_two(norms)
        sizes = [x.shape[0] for x in final + [norms]]
        sent = jnp.concatenate(final + [norms], axis=0)
        got = flip(sent, "dp", dp, 1)
        zero = way == 0
        pair = jnp.where(zero, sent, got).astype(F32), jnp.where(zero, got, sent).astype(F32)
        begin, pieces = 0, []
        for size in sizes:
            pieces.append([x[begin : begin + size] for x in pair])
            begin += size
        final, norms = pieces[:-1], pieces[-1]
        half = norms[0].shape[0] // 2
        norms = (norms[0][:half] + norms[0][half:]) + (norms[1][:half] + norms[1][half:])
    norms = norms.reshape(shape)
    dk = dk[:, :, :shard]
    tap_out = jnp.where(keep[:, None, None, :], dk, 0.0)

    def cut_rows(x, *sizes):
        begin = 0
        for size in sizes:
            yield x[begin : begin + size]
            begin += size

    share = 2 * cut // ways
    wide = [[None] * layers for _ in range(4)]
    order = []
    for layer in range(layers - 1, -1, -1):
        now = [(0, layer), (1, layer), (2, layer)] + [(3, layer + 1)] * (layer < layers - 1)
        order.append(now)
    order.append([(3, 0)])
    sizes = [part, part, share, share]
    found = zip(order, final)
    for order, arrays in found:
        pieces = zip(*[cut_rows(x, *[sizes[i] for i, _ in order]) for x in arrays])
        for (i, layer), x in zip(order, pieces):
            wide[i][layer] = x

    def rows_of_both(arrays):
        return jnp.concatenate(arrays, axis=0)

    parts = [[] for _ in range(6)]
    for up, down, early, late in zip(*wide):
        two, out = (early[0][:cut], early[0][cut:]) if ways == 1 else early
        one, value = (late[0][:cut], late[0][cut:]) if ways == 1 else late
        for store, x in zip(parts, (one, two, value, out, rows_of_both(up), rows_of_both(down))):
            store.append(x)
    one, two, value, out, up, down = (jnp.stack(p) for p in parts)
    in_out = jnp.stack([one, two, value], axis=1)[:, :, :shard]
    return (
        output,
        input_grad,
        norms[0],
        norms[1],
        jnp.transpose(in_out, (0, 3, 1, 2)),
        tap_out,
        out[:, :shard],
        jnp.transpose(up, (0, 2, 1)),
        down,
    )


def solution(mesh):
    sizes = dict(mesh.shape)
    specs = (
        P("dp", "mp", None),
        P("dp", "mp", None),
        P(),
        P(),
        P(None, None, None, "mp"),
        P(None, None, "mp", None),
        P(None, "mp", None),
        P(None, None, "mp"),
        P(None, "mp", None),
    )
    return jax.shard_map(
        functools.partial(program, sizes["dp"], sizes["mp"]),
        mesh=mesh,
        in_specs=specs + (P(),),
        out_specs=specs,
        check_vma=False,
    )
```

```python
import functools
import math

import jax
import jax.numpy as jnp
import ml_dtypes
import numpy as np
from jax import lax
from jax.experimental import pallas as pl
from jax.experimental.pallas import tpu as pltpu
from jax.sharding import PartitionSpec as P

EPS = 1e-05
LANES = 128
RADIX = 32
HALF = RADIX // 2
FREQS = HALF + 1
POINTS = LANES * RADIX
SPAN = POINTS // 2
BF16 = jnp.bfloat16
F32 = jnp.float32
VMEM_BYTES = 56 * 2**20
PASSES = 1


def params():
    return pltpu.CompilerParams(vmem_limit_bytes=VMEM_BYTES)


def whole(array):
    rank = array.ndim
    return pl.BlockSpec(array.shape, lambda *_: (0,) * rank, pipeline_mode=pl.Buffered(1))


def add(a, b):
    if a is None:
        return b
    return a if b is None else a + b


def sub(a, b):
    if b is None:
        return a
    return -b if a is None else a - b


def tidy(v):
    for exact in (0.0, 1.0, -1.0):
        if abs(v - exact) < 1e-12:
            return exact
    return v


def scaled(v, factor):
    if v is None or factor == 0.0:
        return None
    if factor == 1.0:
        return v
    return -v if factor == -1.0 else v * factor


def turn(z, angle):
    re, im = z
    c, s = tidy(math.cos(angle)), tidy(math.sin(angle))
    if re is not None and im is not None and abs(abs(c) - abs(s)) < 1e-12:
        r = math.copysign(abs(c), c)
        if c * s > 0:
            return ((re - im) * r, (re + im) * r)
        return ((re + im) * r, (im - re) * r)
    return (sub(scaled(re, c), scaled(im, s)), add(scaled(im, c), scaled(re, s)))


def analyse(x):
    n = len(x)
    if n == 1:
        return [(x[0], None)]
    even, odd = analyse(x[0::2]), analyse(x[1::2])
    if n == 2:
        return [(add(even[0][0], odd[0][0]), None), (sub(even[0][0], odd[0][0]), None)]
    half, quarter = n // 2, n // 4
    out = [None] * (half + 1)
    for k in range(quarter + 1):
        t = turn(odd[k], -2 * math.pi * k / n)
        out[k] = (add(even[k][0], t[0]), add(even[k][1], t[1]))
        if k != quarter:
            out[half - k] = (sub(even[k][0], t[0]), sub(t[1], even[k][1]))
    return out


def synthesise(x, n, upper):
    if n == 2:
        return [sub(x[0][0], x[1][0]) if upper else add(x[0][0], x[1][0])]
    half, quarter = n // 2, n // 4
    even, odd = [], []
    for k in range(quarter + 1):
        a, b = x[k], x[half - k]
        if k == 0:
            even.append((add(a[0], b[0]), None))
            odd.append((sub(a[0], b[0]), None))
        elif k == quarter:
            even.append((a[0] * 2.0, None))
            odd.append((a[1] * -2.0, None))
        else:
            even.append((add(a[0], b[0]), sub(a[1], b[1])))
            odd.append(turn((sub(a[0], b[0]), add(a[1], b[1])), 2 * math.pi * k / n))
    out = [None] * half
    out[0::2] = synthesise(even, half, upper)
    out[1::2] = synthesise(odd, half, upper)
    return out


def split_bf16(matrix):
    matrix = matrix.astype(np.float32)
    high = matrix.astype(ml_dtypes.bfloat16)
    low = (matrix - high.astype(np.float32)).astype(ml_dtypes.bfloat16)
    return jnp.asarray(np.stack([high, low][: 1 if PASSES == 1 else 2]))


def tables():
    j = np.arange(LANES)
    angle = 2 * np.pi * np.outer(j, j) / LANES
    c, s = np.cos(angle), np.sin(angle)
    twist = 2 * np.pi * np.outer(np.arange(FREQS), j) / POINTS
    return [
        split_bf16(np.block([[c, -s], [s, c]])),
        split_bf16(np.block([[c, s], [-s, c]]) / POINTS),
        jnp.asarray(np.cos(twist), F32),
        jnp.asarray(np.sin(twist), F32),
    ]


def lane_product(a, matrix):
    high = a.astype(BF16)
    y = jnp.dot(high, matrix[0], preferred_element_type=F32)
    if PASSES > 1:
        y = y + jnp.dot(high, matrix[1], preferred_element_type=F32)
    if PASSES > 2:
        low = (a - high.astype(F32)).astype(BF16)
        y = y + jnp.dot(low, matrix[0], preferred_element_type=F32)
    return y


class Convolver:
    def __init__(self, sources, groups, pieces, blocks, rows, refs):
        self.sources, self.groups, self.pieces = sources, groups, pieces
        self.blocks, self.rows = blocks, rows
        self.forward, self.backward, self.cos, self.sin, self.left, self.right, self.freq = refs

    def places(self):
        for i in range(self.sources * self.groups * self.pieces):
            chunk, piece = divmod(i, self.pieces)
            group, source = divmod(chunk, self.sources)
            begin = (group * self.pieces + piece) * LANES
            yield i, source, slice(begin, begin + LANES)

    def load(self, ref, dst):
        for i, source, lanes in self.places():
            dst[i] = ref[source, :, lanes].astype(F32)

    def store(self, src, ref, part=None):
        for i, source, lanes in self.places():
            if part is None:
                ref[source, :, lanes] = src[i].astype(ref.dtype)
            else:
                ref[source, part, :, lanes] = src[i].astype(ref.dtype)

    def subtiles(self):
        return [pl.ds(8 * t, 8) for t in range(self.rows // 8)]

    def spectrum(self, read, count, base):
        for b in range(count):
            for rows in self.subtiles():
                x = analyse([read(b, i, rows) for i in range(HALF)] + [None] * HALF)
                for f, (re, im) in enumerate(x):
                    if f:
                        c, s = self.cos[f : f + 1, :], self.sin[f : f + 1, :]
                        if im is None:
                            re, im = re * c, -(re * s)
                        else:
                            re, im = re * c + im * s, im * c - re * s
                    self.left[b * FREQS + f, rows, 0:LANES] = re
                    self.left[b * FREQS + f, rows, LANES:] = jnp.zeros_like(re) if im is None else im
            y = lane_product(self.stacked(b), self.forward)
            begin = (base + b) * FREQS
            self.freq[begin : begin + FREQS] = y.reshape(FREQS, self.rows, 2 * LANES)

    def stacked(self, b):
        return self.left[b * FREQS : (b + 1) * FREQS].reshape(FREQS * self.rows, 2 * LANES)

    def entry(self, row, rows):
        return self.freq[row, rows, 0:LANES], self.freq[row, rows, LANES:]

    def window(self, base, b, f, rows, ahead):
        re, im = self.entry((base + b) * FREQS + f, rows)
        other = b + 1 if ahead else b - 1
        if not ahead and f % 2:
            re, im = -re, -im
        if 0 <= other < self.blocks:
            ore, oim = self.entry((base + other) * FREQS + f, rows)
            if ahead and f % 2:
                return re - ore, im - oim
            return re + ore, im + oim
        return re, im

    def inverse(self, b, upper, write):
        y = lane_product(self.stacked(b), self.backward)
        begin = b * FREQS
        self.right[begin : begin + FREQS] = y.reshape(FREQS, self.rows, 2 * LANES)
        for rows in self.subtiles():
            parts = []
            for f in range(FREQS):
                re = self.right[begin + f, rows, 0:LANES]
                im = self.right[begin + f, rows, LANES:]
                c, s = self.cos[f : f + 1, :], self.sin[f : f + 1, :]
                if f == 0:
                    parts.append((re, None))
                elif f == HALF:
                    parts.append((re * c - im * s, None))
                else:
                    parts.append((re * c - im * s, im * c + re * s))
            for i, value in enumerate(synthesise(parts, RADIX, upper)):
                write(b, i, rows, value)

    def convolve(self, signal, kernel, ahead, write):
        for b in range(self.blocks):
            for rows in self.subtiles():
                for f in range(FREQS):
                    re, im = self.window(signal, b, f, rows, ahead)
                    kre, kim = self.entry(kernel * FREQS + f, rows)
                    if ahead:
                        pre, pim = re * kre + im * kim, im * kre - re * kim
                    else:
                        pre, pim = re * kre - im * kim, re * kim + im * kre
                    self.left[b * FREQS + f, rows, 0:LANES] = pre
                    self.left[b * FREQS + f, rows, LANES:] = pim
            self.inverse(b, not ahead, write)

    def taps(self, signal, grads, write):
        for rows in self.subtiles():
            for f in range(FREQS):
                re = im = None
                for b in range(self.blocks):
                    gre, gim = self.window(grads, b, f, rows, True)
                    sre, sim = self.entry((signal + b) * FREQS + f, rows)
                    re = add(re, sre * gre + sim * gim)
                    im = add(im, sre * gim - sim * gre)
                self.left[f, rows, 0:LANES] = re
                self.left[f, rows, LANES:] = im
        self.inverse(0, False, write)


def kernel_reader(k_ref, j):
    def read(_, i, rows):
        value = k_ref[j, :, i * LANES : (i + 1) * LANES].astype(F32)
        return value[rows.start : rows.start + rows.size]

    return read


def mix_body(shape, v_ref, g_ref, k_ref, *refs):
    (fwd, bwd, cos, sin, out_ref, one_ref, carried_ref, xs, gs, left, right, freq) = refs
    cv = Convolver(*shape, v_ref.shape[1], (fwd, bwd, cos, sin, left, right, freq))
    n = cv.blocks
    cv.load(v_ref, xs)
    cv.load(g_ref, gs)

    def read(b, i, rows):
        return xs[b * HALF + i, rows, :]

    cv.spectrum(kernel_reader(k_ref, 0), 1, n)
    cv.spectrum(kernel_reader(k_ref, 1), 1, n + 1)
    cv.spectrum(read, n, 0)

    def gate(b, i, rows, value):
        r = b * HALF + i
        xs[r, rows, :] = (gs[r, rows, :] * value).astype(BF16).astype(F32)
        gs[r, rows, :] = value

    cv.convolve(0, n, False, gate)
    one_ref[...] = gs[...].astype(BF16)
    carried_ref[...] = xs[...].astype(BF16)
    cv.spectrum(read, n, 0)

    def keep(b, i, rows, value):
        gs[b * HALF + i, rows, :] = value

    cv.convolve(0, n + 1, False, keep)
    cv.store(gs, out_ref)


def unmix_body(shape, d_ref, g_ref, one_ref, k_ref, *refs):
    (fwd, bwd, cos, sin, out_ref, grad_ref, xs, gs, left, right, freq) = refs
    cv = Convolver(*shape, g_ref.shape[1], (fwd, bwd, cos, sin, left, right, freq))
    n = cv.blocks
    cv.load(d_ref, xs)
    cv.load(g_ref, gs)

    def read(b, i, rows):
        return xs[b * HALF + i, rows, :]

    cv.spectrum(kernel_reader(k_ref, 1), 1, n)
    cv.spectrum(read, n, 0)

    def gate(b, i, rows, value):
        r = b * HALF + i
        xs[r, rows, :] = (gs[r, rows, :] * value).astype(BF16).astype(F32)
        gs[r, rows, :] = value

    cv.convolve(0, n, True, gate)
    grad_ref[...] = xs[...].astype(BF16)
    gs[...] = gs[...] * one_ref[...].astype(F32)
    cv.store(gs, out_ref, 0)
    cv.spectrum(kernel_reader(k_ref, 0), 1, n)
    cv.spectrum(read, n, 0)

    def keep(b, i, rows, value):
        gs[b * HALF + i, rows, :] = value

    cv.convolve(0, n, True, keep)
    cv.store(gs, out_ref, 1)


def tap_body(shape, before, d_ref, v_ref, carried_ref, grad_ref, *refs):
    (fwd, bwd, cos, sin), refs = refs[:4], refs[4 + before :]
    (dk_ref, xs, gs, left, right, freq) = refs
    cv = Convolver(*shape, v_ref.shape[1], (fwd, bwd, cos, sin, left, right, freq))
    n = cv.blocks
    cv.load(d_ref, xs)
    cv.load(v_ref, gs)

    def reader(ref):
        return lambda b, i, rows: ref[b * HALF + i, rows, :]

    def half_reader(ref):
        def read(b, i, rows):
            return ref[b * HALF + i].astype(F32)[rows.start : rows.start + rows.size]

        return read

    def put(j):
        def write(_, i, rows, value):
            dk_ref[j, rows, i * LANES : (i + 1) * LANES] = value

        return write

    cv.spectrum(reader(xs), n, 0)
    cv.spectrum(half_reader(carried_ref), n, n)
    cv.taps(n, 0, put(1))
    cv.spectrum(half_reader(grad_ref), n, 0)
    cv.spectrum(reader(gs), n, n)
    cv.taps(n, 0, put(0))


def conv_sizes(gates):
    sources, groups, _, shard, length = gates.shape
    tile = 16
    pieces = length // (groups * LANES)
    total = sources * length
    return sources, groups, shard, length, tile, pieces, total // LANES, total // SPAN


def conv_scratch(tile, rows, blocks, spectra):
    return [
        pltpu.VMEM((rows, tile, LANES), F32),
        pltpu.VMEM((rows, tile, LANES), F32),
        pltpu.VMEM((blocks * FREQS, tile, 2 * LANES), F32),
        pltpu.VMEM((blocks * FREQS, tile, 2 * LANES), F32),
        pltpu.VMEM((spectra * FREQS, tile, 2 * LANES), F32),
    ]


def mix(gates, taps):
    q, g, shard, length, tile, pieces, rows, blocks = conv_sizes(gates)
    consts = tables()
    by_source = (q, None, None, tile, length)
    nat = pl.BlockSpec((None, rows, tile, LANES), lambda a, b: (a, 0, b, 0))
    return pl.pallas_call(
        functools.partial(mix_body, (q, g, pieces, blocks)),
        grid=(g, shard // tile),
        in_specs=[
            pl.BlockSpec(by_source, lambda a, b: (0, a, 1, b, 0)),
            pl.BlockSpec(by_source, lambda a, b: (0, a, 0, b, 0)),
            pl.BlockSpec((None, 2, tile, SPAN), lambda a, b: (a, 0, b, 0)),
        ]
        + [whole(c) for c in consts],
        out_specs=[pl.BlockSpec((q, None, tile, length), lambda a, b: (0, a, b, 0)), nat, nat],
        out_shape=[
            jax.ShapeDtypeStruct((q, g, shard, length), BF16),
            jax.ShapeDtypeStruct((g, rows, shard, LANES), BF16),
            jax.ShapeDtypeStruct((g, rows, shard, LANES), BF16),
        ],
        scratch_shapes=conv_scratch(tile, rows, blocks, blocks + 2),
        compiler_params=params(),
        name="mix",
    )(gates, gates, taps, *consts)


def unmix(grads, gates, conv_one, taps):
    q, g, shard, length, tile, pieces, rows, blocks = conv_sizes(gates)
    consts = tables()
    by_source = (q, None, None, tile, length)
    nat = pl.BlockSpec((None, rows, tile, LANES), lambda a, b: (a, 0, b, 0))
    return pl.pallas_call(
        functools.partial(unmix_body, (q, g, pieces, blocks)),
        grid=(g, shard // tile),
        in_specs=[
            pl.BlockSpec((q, None, tile, length), lambda a, b: (0, a, b, 0)),
            pl.BlockSpec(by_source, lambda a, b: (0, a, 0, b, 0)),
            nat,
            pl.BlockSpec((None, 2, tile, SPAN), lambda a, b: (a, 0, b, 0)),
        ]
        + [whole(c) for c in consts],
        out_specs=[
            pl.BlockSpec((q, None, 2, tile, length), lambda a, b: (0, a, 0, b, 0)),
            nat,
        ],
        out_shape=[
            jax.ShapeDtypeStruct((q, g, 2, shard, length), BF16),
            jax.ShapeDtypeStruct((g, rows, shard, LANES), BF16),
        ],
        scratch_shapes=conv_scratch(tile, rows, blocks, blocks + 1),
        compiler_params=params(),
        name="unmix",
    )(grads, gates, conv_one, taps, *consts)


def tap_grads(grads, gates, carried, grad_one, before=()):
    q, g, shard, length, tile, pieces, rows, blocks = conv_sizes(gates)
    consts = tables()
    nat = pl.BlockSpec((None, rows, tile, LANES), lambda a, b: (a, 0, b, 0))
    return pl.pallas_call(
        functools.partial(tap_body, (q, g, pieces, blocks), len(before)),
        grid=(g, shard // tile),
        in_specs=[
            pl.BlockSpec((q, None, tile, length), lambda a, b: (0, a, b, 0)),
            pl.BlockSpec((q, None, None, tile, length), lambda a, b: (0, a, 1, b, 0)),
            nat,
            nat,
        ]
        + [whole(c) for c in consts]
        + [pl.BlockSpec(memory_space=pl.ANY)] * len(before),
        out_specs=pl.BlockSpec((None, 2, tile, SPAN), lambda a, b: (a, 0, b, 0)),
        out_shape=jax.ShapeDtypeStruct((g, 2, shard, SPAN), F32),
        scratch_shapes=conv_scratch(tile, rows, blocks, 2 * blocks),
        compiler_params=params(),
        name="tap_grads",
    )(grads, gates, carried, grad_one, *consts, *before)


def standardise(stream):
    average = jnp.mean(stream, axis=0, keepdims=True)
    centered = stream - average
    inv_std = lax.rsqrt(jnp.mean(centered * centered, axis=0, keepdims=True) + EPS)
    return centered * inv_std, inv_std


def standardise_back(grad, gain, stream):
    unit, inv_std = standardise(stream)
    g = grad * gain
    mean_grad = jnp.mean(g, axis=0, keepdims=True)
    mean_cross = jnp.mean(g * unit, axis=0, keepdims=True)
    back = inv_std * (g - mean_grad - unit * mean_cross)
    gain_part = jnp.sum(grad * unit, axis=1, keepdims=True)
    bias_part = jnp.sum(grad, axis=1, keepdims=True)
    return back, gain_part, bias_part


def transposed(x):
    return jnp.transpose(x.astype(F32))


def column(row_ref):
    row = row_ref[...]
    return jnp.transpose(jnp.broadcast_to(row, (8, row.shape[1])))[:, 0:1]


def as_row(column):
    return jnp.transpose(jnp.broadcast_to(column, (column.shape[0], LANES)))[0:1]


def gelu_pair(x):
    z = jnp.abs(x) * math.sqrt(0.5)
    t = 1.0 / (1.0 + 0.3275911 * z)
    e = jnp.exp(-(z * z))
    poly = t * (
        0.127414796 + t * (-0.142248368 + t * (0.710706871 + t * (-0.726576014 + t * 0.530702714)))
    )
    tail = poly * e
    phi = jnp.where(x >= 0, 1.0 - tail, tail)
    return x * phi, phi + x * (e * (1.0 / math.sqrt(2 * math.pi)))


def first(axis_is_zero, refs, cut, body):
    if len(refs) == 1:
        body(refs[0].at[:, 0 : 2 * cut], refs[0].at[:, 2 * cut : 3 * cut])
        return

    @pl.when(axis_is_zero)
    def _():
        body(refs[0], refs[1].at[:, 0:cut])

    @pl.when(jnp.logical_not(axis_is_zero))
    def _():
        body(refs[1], refs[0].at[:, 0:cut])


class Pieces:
    def __init__(self, arrays, begins, rows):
        self.arrays, self.begins, self.rows = arrays, begins, rows

    def specs(self):
        mp, _, width = self.arrays[0].shape
        shape = (mp, self.rows, width)
        return [
            pl.BlockSpec(
                shape, lambda *_, at=begin // self.rows: (0, at, 0), pipeline_mode=pl.Buffered(1)
            )
            for begin in self.begins
        ]

    def __len__(self):
        return len(self.arrays)


SCALARS = pl.BlockSpec(memory_space=pltpu.SMEM)


def by_channel(blocks, groups):
    peers = blocks.shape[0] // groups
    order = [h * peers + q for q in range(peers) for h in range(groups)]
    return jnp.concatenate([blocks[m : m + 1] for m in order], axis=0)


def project_body(natural, ways, groups, place_ref, x_ref, gain_ref, bias_ref, *rest):
    dense, rest = rest[:ways], rest[ways:]
    if natural:
        s_ref, op_ref, two_ref, n_ref, pair_w, value_w = rest
        x = transposed(x_ref[...])
        s_ref[...] = x
    else:
        op_ref, two_ref, n_ref, pair_w, value_w = rest
        x = x_ref[...]
    mp, cut, t = two_ref.shape

    @pl.when(pl.program_id(0) == 0)
    def _():
        def body(pair, value):
            pair_w[...] = by_channel(pair, groups)
            value_w[...] = by_channel(value, groups)

        first(place_ref[0] == 0, dense, cut, body)

    unit, _ = standardise(x)
    normed = unit * column(gain_ref) + column(bias_ref)
    n_ref[...] = transposed(normed).astype(BF16)
    normed = normed.astype(BF16)
    width = normed.shape[0]
    y = jnp.dot(
        pair_w[...].reshape(mp * 2 * cut, width), normed, preferred_element_type=F32
    )
    y = y.astype(BF16).reshape(mp, 2, cut, t)
    op_ref[:, 0] = y[:, 0]
    two_ref[...] = y[:, 1]
    y = jnp.dot(value_w[...].reshape(mp * cut, width), normed, preferred_element_type=F32)
    op_ref[:, 1] = y.astype(BF16).reshape(mp, cut, t)


def token_tile(length, most=256):
    return min(length, most)


def project(natural, groups, place, x, dense, gain, bias, cut):
    mp, _, width = dense.arrays[0].shape
    length = x.shape[0] if natural else x.shape[1]
    t = token_tile(length)
    tall = pl.BlockSpec((t, width), lambda i: (i, 0))
    flat = pl.BlockSpec((width, t), lambda i: (0, i))
    out_specs = [
        pl.BlockSpec((mp, 2, cut, t), lambda i: (0, 0, 0, i)),
        pl.BlockSpec((mp, cut, t), lambda i: (0, 0, i)),
        tall,
    ]
    out_shape = [
        jax.ShapeDtypeStruct((mp, 2, cut, length), BF16),
        jax.ShapeDtypeStruct((mp, cut, length), BF16),
        jax.ShapeDtypeStruct((length, width), BF16),
    ]
    if natural:
        out_specs.insert(0, flat)
        out_shape.insert(0, jax.ShapeDtypeStruct((width, length), F32))
    return pl.pallas_call(
        functools.partial(project_body, natural, len(dense), groups),
        grid=(length // t,),
        in_specs=[SCALARS, tall if natural else flat, whole(gain), whole(bias)] + dense.specs(),
        out_specs=out_specs,
        out_shape=out_shape,
        scratch_shapes=[
            pltpu.VMEM((mp, 2 * cut, width), BF16),
            pltpu.VMEM((mp, cut, width), BF16),
        ],
        compiler_params=params(),
        name="project",
    )(place, x, gain, bias, *dense.arrays)


def ff_chunks(refs):
    mp, rows, width = refs[0].shape
    part = rows // 2
    step = min(mp, width // part)
    size = step * part
    for p, ref in enumerate(refs):
        for j in range(mp // step):
            begin = (p * (mp // step) + j) * size
            yield ref, slice(j * step, (j + 1) * step), part, slice(begin, begin + size)


def forward_body(natural, ways, s_ref, c_ref, g_ref, wo_ref, gain_ref, bias_ref, *rest):
    ff, rest = rest[:ways], rest[ways:]
    s1_ref, s2_ref, h_ref, d_ref, n_ref, gated_ref, wo_t, down_t = rest
    width = ff[0].shape[-1]

    @pl.when(pl.program_id(0) == 0)
    def _():
        wo_t[...] = transposed(wo_ref[...]).astype(BF16)
        for ref, blocks, part, units in ff_chunks(ff):
            block = ref[blocks, part:, :].reshape(units.stop - units.start, width)
            down_t[:, units] = transposed(block).astype(BF16)

    gated = (g_ref[...].astype(F32) * c_ref[...].astype(F32)).astype(BF16)
    gated_ref[...] = gated
    s1 = s_ref[...] + jnp.dot(wo_t[...], gated, preferred_element_type=F32)
    s1_ref[...] = s1
    unit, _ = standardise(s1)
    normed = unit * column(gain_ref) + column(bias_ref)
    n_ref[...] = transposed(normed).astype(BF16)
    normed = normed.astype(BF16)
    total = s1
    for ref, blocks, part, units in ff_chunks(ff):
        up = ref[blocks, 0:part, :].reshape(units.stop - units.start, width)
        hidden, slope = gelu_pair(jnp.dot(up, normed, preferred_element_type=F32))
        hidden = hidden.astype(BF16)
        h_ref[units, :] = hidden
        d_ref[units, :] = slope.astype(BF16)
        total = total + jnp.dot(down_t[:, units], hidden, preferred_element_type=F32)
    s2_ref[...] = transposed(total) if natural else total


def forward_block(natural, stream, conv_two, gate_two, w_out, ff, gain, bias):
    width, length = stream.shape
    channels = w_out.shape[0]
    hidden = len(ff) * ff.arrays[0].shape[0] * ff.rows // 2
    t = token_tile(length)
    tall = pl.BlockSpec((t, width), lambda i: (i, 0))
    flat = pl.BlockSpec((width, t), lambda i: (0, i))
    chan = pl.BlockSpec((channels, t), lambda i: (0, i))
    high = pl.BlockSpec((hidden, t), lambda i: (0, i))
    last = (length, width) if natural else (width, length)
    return pl.pallas_call(
        functools.partial(forward_body, natural, len(ff)),
        grid=(length // t,),
        in_specs=[flat, chan, chan, whole(w_out), whole(gain), whole(bias)] + ff.specs(),
        out_specs=[flat, tall if natural else flat, high, high, tall, chan],
        out_shape=[
            jax.ShapeDtypeStruct((width, length), F32),
            jax.ShapeDtypeStruct(last, F32),
            jax.ShapeDtypeStruct((hidden, length), BF16),
            jax.ShapeDtypeStruct((hidden, length), BF16),
            jax.ShapeDtypeStruct((length, width), BF16),
            jax.ShapeDtypeStruct((channels, length), BF16),
        ],
        scratch_shapes=[pltpu.VMEM((width, channels), BF16), pltpu.VMEM((width, hidden), BF16)],
        compiler_params=params(),
        name="forward_block",
    )(stream, conv_two, gate_two, w_out, gain, bias, *ff.arrays)


def backward_body(natural, ways, gs_ref, d_ref, s1_ref, c_ref, g_ref, wo_ref, gain_ref, *rest):
    ff, rest = rest[:ways], rest[ways:]
    pre_ref, gs1_ref, gc_ref, two_ref, dm_ref, do_ref, gain_out, bias_out = rest[:8]
    up_n, gain_sum, bias_sum = rest[8:]
    width = ff[0].shape[-1]

    @pl.when(pl.program_id(0) == 0)
    def _():
        gain_sum[...] = jnp.zeros_like(gain_sum)
        bias_sum[...] = jnp.zeros_like(bias_sum)
        for ref, blocks, part, units in ff_chunks(ff):
            block = ref[blocks, 0:part, :].reshape(units.stop - units.start, width)
            up_n[:, units] = transposed(block).astype(BF16)

    if natural:
        dm_ref[...] = gs_ref[...]
        grad = transposed(gs_ref[...])
    else:
        grad = gs_ref[...]
        dm_ref[...] = transposed(grad).astype(BF16)
    dm = grad.astype(BF16)
    total = None
    for ref, blocks, part, units in ff_chunks(ff):
        down = ref[blocks, part:, :].reshape(units.stop - units.start, width)
        pre = jnp.dot(down, dm, preferred_element_type=F32) * d_ref[units, :].astype(F32)
        pre = pre.astype(BF16)
        pre_ref[units, :] = pre
        total = add(total, jnp.dot(up_n[:, units], pre, preferred_element_type=F32))
    back, gain_part, bias_part = standardise_back(total, column(gain_ref), s1_ref[...])
    gain_sum[...] += gain_part
    bias_sum[...] += bias_part

    @pl.when(pl.program_id(0) == pl.num_programs(0) - 1)
    def _():
        gain_out[...] = as_row(gain_sum[...])
        bias_out[...] = as_row(bias_sum[...])

    grad = grad + back
    gs1_ref[...] = grad
    do_ref[...] = transposed(grad).astype(BF16)
    gated = jnp.dot(wo_ref[...], grad.astype(BF16), preferred_element_type=F32)
    gated = gated.astype(BF16).astype(F32)
    gc_ref[...] = (gated * g_ref[...].astype(F32)).astype(BF16)
    two_ref[...] = (gated * c_ref[...].astype(F32)).astype(BF16)


def backward_block(natural, grad, slope, s1, conv_two, gate_two, w_out, ff, gain):
    width, length = s1.shape
    channels = w_out.shape[0]
    hidden = slope.shape[0]
    t = token_tile(length, 512)
    tall = pl.BlockSpec((t, width), lambda i: (i, 0))
    flat = pl.BlockSpec((width, t), lambda i: (0, i))
    chan = pl.BlockSpec((channels, t), lambda i: (0, i))
    high = pl.BlockSpec((hidden, t), lambda i: (0, i))
    row = pl.BlockSpec((1, width), lambda i: (0, 0))
    return pl.pallas_call(
        functools.partial(backward_body, natural, len(ff)),
        grid=(length // t,),
        in_specs=[tall if natural else flat, high, flat, chan, chan]
        + [whole(w_out), whole(gain)]
        + ff.specs(),
        out_specs=[high, flat, chan, chan, tall, tall, row, row],
        out_shape=[
            jax.ShapeDtypeStruct((hidden, length), BF16),
            jax.ShapeDtypeStruct((width, length), F32),
            jax.ShapeDtypeStruct((channels, length), BF16),
            jax.ShapeDtypeStruct((channels, length), BF16),
            jax.ShapeDtypeStruct((length, width), BF16),
            jax.ShapeDtypeStruct((length, width), BF16),
            jax.ShapeDtypeStruct((1, width), F32),
            jax.ShapeDtypeStruct((1, width), F32),
        ],
        scratch_shapes=[
            pltpu.VMEM((width, hidden), BF16),
            pltpu.VMEM((width, 1), F32),
            pltpu.VMEM((width, 1), F32),
        ],
        compiler_params=params(),
        name="backward_block",
    )(grad, slope, s1, conv_two, gate_two, w_out, gain, *ff.arrays)


def unproject_body(natural, ways, groups, place_ref, gm_ref, two_ref, s_ref, gs_ref, gain_ref, *rest):
    dense, rest = rest[:ways], rest[ways:]
    out_ref, gain_out, bias_out, pair_t, value_t, gain_sum, bias_sum = rest
    mp, cut, t = two_ref.shape
    width = dense[0].shape[-1]

    @pl.when(pl.program_id(0) == 0)
    def _():
        gain_sum[...] = jnp.zeros_like(gain_sum)
        bias_sum[...] = jnp.zeros_like(bias_sum)

        def body(pair, value):
            rows = by_channel(pair, groups).reshape(mp * 2 * cut, width)
            pair_t[...] = transposed(rows).astype(BF16)
            rows = by_channel(value, groups).reshape(mp * cut, width)
            value_t[...] = transposed(rows).astype(BF16)

        first(place_ref[0] == 0, dense, cut, body)

    pair = jnp.concatenate([gm_ref[:, 0:1], two_ref[...][:, None]], axis=1)
    grad = jnp.dot(pair_t[...], pair.reshape(mp * 2 * cut, t), preferred_element_type=F32)
    value = gm_ref[:, 1].reshape(mp * cut, t)
    grad = grad + jnp.dot(value_t[...], value, preferred_element_type=F32)
    back, gain_part, bias_part = standardise_back(grad, column(gain_ref), s_ref[...])
    gain_sum[...] += gain_part
    bias_sum[...] += bias_part

    @pl.when(pl.program_id(0) == pl.num_programs(0) - 1)
    def _():
        gain_out[...] = as_row(gain_sum[...])
        bias_out[...] = as_row(bias_sum[...])

    result = gs_ref[...] + back
    out_ref[...] = transposed(result) if natural else result


def unproject(natural, groups, place, grad_mixed, grad_two, dense, stream, grad, gain):
    width, length = stream.shape
    mp, cut, _ = grad_two.shape
    t = token_tile(length)
    tall = pl.BlockSpec((t, width), lambda i: (i, 0))
    flat = pl.BlockSpec((width, t), lambda i: (0, i))
    row = pl.BlockSpec((1, width), lambda i: (0, 0))
    last = (length, width) if natural else (width, length)
    return pl.pallas_call(
        functools.partial(unproject_body, natural, len(dense), groups),
        grid=(length // t,),
        in_specs=[
            SCALARS,
            pl.BlockSpec((mp, 2, cut, t), lambda i: (0, 0, 0, i)),
            pl.BlockSpec((mp, cut, t), lambda i: (0, 0, i)),
            flat,
            flat,
            whole(gain),
        ]
        + dense.specs(),
        out_specs=[tall if natural else flat, row, row],
        out_shape=[
            jax.ShapeDtypeStruct(last, F32),
            jax.ShapeDtypeStruct((1, width), F32),
            jax.ShapeDtypeStruct((1, width), F32),
        ],
        scratch_shapes=[
            pltpu.VMEM((width, mp * 2 * cut), BF16),
            pltpu.VMEM((width, mp * cut), BF16),
            pltpu.VMEM((width, 1), F32),
            pltpu.VMEM((width, 1), F32),
        ],
        compiler_params=params(),
        name="unproject",
    )(place, grad_mixed, grad_two, stream, grad, gain, *dense.arrays)


GROUP = 8


class Plain:
    def __init__(self, ways, mp, left, right):
        self.left = left.reshape(ways, mp, left.shape[0] // (ways * mp), left.shape[1])
        self.rows, self.rights = self.left.shape[2], [right]

    def lefts(self):
        _, _, part, length = self.left.shape
        shape = (self.left.shape[0], GROUP, part, length)
        spec = pl.BlockSpec(shape, lambda i, place: (0, i ^ (place[1] // GROUP), 0, 0))
        return [(self.left, spec)]

    def pieces(self, way, lefts, rights):
        ways, count, part, length = lefts[0].shape
        for w in range(ways):
            y = rows_product(lefts[0][w].reshape(count * part, length), rights[0])
            yield y.reshape(count, part, -1)


class Mixed:
    def __init__(self, ways, groups, lefts, rights):
        self.ways, self.rights = ways, rights
        self.arrays = [
            x.reshape((x.shape[0] // groups, groups) + x.shape[1:]) for x in lefts
        ]
        self.rows = 2 * self.arrays[0].shape[-2] // ways

    def lefts(self):
        result = []
        for x in self.arrays:
            shape = (GROUP, None) + x.shape[2:]
            zeros = (0,) * (x.ndim - 2)
            runs = x.shape[0] // GROUP

            def index(i, place, runs=runs, zeros=zeros):
                run = i ^ (place[1] // GROUP)
                return (lax.rem(run, runs), run // runs) + zeros

            result.append((x, pl.BlockSpec(shape, index)))
        return result

    def pieces(self, way, lefts, rights):
        if len(lefts) == 1:
            lefts = [lefts[0].at[:, 0], lefts[0].at[:, 1]]
        made = []
        for left, right in zip(lefts, (rights * 2)[:2]):
            count, cut, length = left.shape
            y = rows_product(left[...].reshape(count * cut, length), right)
            made.append(y.reshape(count, cut, -1))
        a, b = made
        for w in range(self.ways):
            if self.ways == 1:
                yield jnp.concatenate([a, b], axis=1)
            else:
                yield jnp.where(way ^ w == 0, a, b)


def rows_product(left, right):
    return jnp.dot(left, right[...], preferred_element_type=F32).astype(BF16)


def grads_body(ways, jobs, before, place_ref, *refs):
    counts = [len(job.lefts()) for job in jobs]
    lefts, refs = refs[: sum(counts)], refs[sum(counts) :]
    rights, refs = refs[: sum(len(j.rights) for j in jobs)], refs[sum(len(j.rights) for j in jobs) :]
    outs = refs[before:]
    low = place_ref[1] % GROUP
    begin = 0
    for job, count in zip(jobs, counts):
        mine, lefts = lefts[:count], lefts[count:]
        right, rights = rights[: len(job.rights)], rights[len(job.rights) :]
        for out, values in zip(outs, job.pieces(place_ref[0], list(mine), list(right))):
            for i in range(GROUP):
                out[i ^ low, begin : begin + job.rows, :] = values[i]
        begin += job.rows


def weight_grads(name, ways, mp, place, jobs, before=()):
    width = jobs[0].rights[0].shape[1]
    rows = sum(job.rows for job in jobs)
    lefts = [pair for job in jobs for pair in job.lefts()]
    rights = [right for job in jobs for right in job.rights]

    def kept(a):
        return pl.BlockSpec(a.shape, lambda i, place: (0, 0), pipeline_mode=pl.Buffered(1))

    out = pl.BlockSpec((GROUP, rows, width), lambda i, place: (i, 0, 0))
    return pl.pallas_call(
        functools.partial(grads_body, ways, jobs, len(before)),
        grid_spec=pltpu.PrefetchScalarGridSpec(
            num_scalar_prefetch=1,
            grid=(mp // GROUP,),
            in_specs=[spec for _, spec in lefts]
            + [kept(a) for a in rights]
            + [pl.BlockSpec(memory_space=pl.ANY)] * len(before),
            out_specs=[out] * ways,
        ),
        out_shape=[jax.ShapeDtypeStruct((mp, rows, width), BF16)] * ways,
        compiler_params=params(),
        name=name,
    )(place, *[x for x, _ in lefts], *rights, *before)


def together(*arrays):
    return lax.optimization_barrier(arrays)


def flip(x, axis, size, bit):
    return lax.ppermute(x, axis, [(i, i ^ bit) for i in range(size)])


def dp_sum(x, dp):
    return butterfly(x, [("dp", dp)])


def butterfly(x, sizes):
    for axis, size in sizes:
        bit = 1
        while bit < size:
            x = x + flip(x, axis, size, bit)
            bit *= 2
    return x


def stage_order(mp, swapped):
    bits = list(range(mp.bit_length() - 1))
    first = [[1], [0]] if swapped else [[0], [1]]
    return first + [bits[i : i + 2] for i in range(2, len(bits), 2)]


def total(parts):
    value = parts[0].astype(F32)
    for part in parts[1:]:
        value = value + part.astype(F32)
    return value


class Hop:
    def __init__(self, x, axis, size, mask):
        self.x, self.where = x, (axis, size, mask)

    def start(self):
        return flip(self.x, *self.where)


def masks(bits):
    return [sum(((k >> i) & 1) << b for i, b in enumerate(bits)) for k in range(1 << len(bits))]


def scatter_steps(terms, left, mp, stages):
    for stage in stages:
        axes = [left.index(b) for b in stage]
        left = [b for b in left if b not in stage]

        def take(t, k):
            index = [slice(None)] * t.ndim
            for i, axis in enumerate(axes):
                index[axis] = (k >> i) & 1
            return t[tuple(index)]

        sums = [
            total([take(t, k) for t in terms]).astype(BF16) for k in range(1 << len(stage))
        ]
        got = yield [Hop(x, "mp", mp, mask) for x, mask in zip(sums[1:], masks(stage)[1:])]
        terms = sums[:1] + got
    return terms


def scatter_chain(terms, mp, stages, split=False):
    bits = mp.bit_length() - 1
    left = list(range(bits - 1, -1, -1))
    terms = [t.reshape((2,) * bits + t.shape[1:]) for t in terms]
    if split:
        rows = terms[0].shape[-2]
        middle = (rows // 2 + 15) // 16 * 16
        orders = stages[:2], stages[1::-1]
        parts = [
            scatter_steps([t[..., span, :] for t in terms], left, mp, order)
            for span, order in zip((slice(0, middle), slice(middle, rows)), orders)
        ]
        hops = [next(part) for part in parts]
        got = yield hops[0] + hops[1]
        hops = [part.send([x]) for part, x in zip(parts, got)]
        got = yield hops[0] + hops[1]
        ended = []
        for part, x in zip(parts, got):
            try:
                part.send([x])
            except StopIteration as end:
                ended.append(end.value)
        terms = [jnp.concatenate(pair, axis=-2) for pair in zip(*ended)]
        left = [b for b in left if b not in stages[0] + stages[1]]
        stages = stages[2:]
    terms = yield from scatter_steps(terms, left, mp, stages)
    return total(terms)


def in_two(x):
    high = x.astype(BF16)
    return jnp.concatenate([high, (x - high.astype(F32)).astype(BF16)], axis=0)


def from_two(x):
    half = x.shape[0] // 2
    return x[:half].astype(F32) + x[half:].astype(F32)


def last_chain(terms, norms, mp, stages):
    bits = mp.bit_length() - 1
    left = list(range(bits - 1, -1, -1))
    terms = [t.reshape((2,) * bits + t.shape[1:]) for t in terms]
    width = norms.shape[1]
    for stage in stages:
        axes = [left.index(b) for b in stage]
        left = [b for b in left if b not in stage]
        sums = []
        for k in range(1 << len(stage)):
            index = [slice(None)] * terms[0].ndim
            for i, axis in enumerate(axes):
                index[axis] = (k >> i) & 1
            sums.append(total([t[tuple(index)] for t in terms]).astype(BF16))
        own = in_two(norms)
        shape, rows = sums[0].shape, sums[0].size // width
        got = yield [
            Hop(jnp.concatenate([x.reshape(rows, width), own], axis=0), "mp", mp, mask)
            for x, mask in zip(sums[1:], masks(stage)[1:])
        ]
        terms = sums[:1] + [x[:rows].reshape(shape) for x in got]
        values = [from_two(x) for x in [own] + [x[rows:] for x in got]]
        while len(values) > 1:
            values = [a + b for a, b in zip(values[0::2], values[1::2])]
        norms = values[0]
    return total(terms), norms


def gather_chain(x, mp, stages):
    me = lax.axis_index("mp")
    done = []
    for stage in stages:
        got = yield [Hop(x, "mp", mp, mask) for mask in masks(stage)[1:]]
        pieces = [x] + got
        place = sum(((me >> b) & 1) << i for i, b in enumerate(stage))
        count = len(pieces)
        if count == 2:
            pieces = [jnp.where(place == a, x, got[0]) for a in range(2)]
        else:
            pieces = [
                lax.select_n(place, *[pieces[a ^ v] for v in range(count)]) for a in range(count)
            ]
        for i, bit in enumerate(stage):
            axis = sum(b > bit for b in done)
            pieces = [
                jnp.stack([pieces[j], pieces[j + 1]], axis=axis) for j in range(0, len(pieces), 2)
            ]
            done.append(bit)
        x = pieces[0]
    return x.reshape((mp,) + x.shape[len(done) :])


def chip_chain(pieces, dp):
    if len(pieces) == 1:
        return pieces
    got = yield [Hop(pieces[1], "dp", dp, 1)]
    return [pieces[0]] + got


class Chains:
    def __init__(self):
        self.waiting, self.results = {}, {}

    def add(self, name, chain):
        self.step(name, chain, None)

    def step(self, name, chain, value):
        try:
            self.waiting[name] = chain, chain.send(value)
        except StopIteration as end:
            self.waiting.pop(name, None)
            self.results[name] = end.value

    def hops(self):
        return [hop for _, hops in self.waiting.values() for hop in hops]

    def operands(self):
        return [hop.x for hop in self.hops()]

    def tie(self, *others):
        hops = self.hops()
        tied = together(*[hop.x for hop in hops], *others)
        for hop, x in zip(hops, tied):
            hop.x = x
        return tied[len(hops) :]

    def start(self):
        return {name: [hop.start() for hop in hops] for name, (_, hops) in self.waiting.items()}

    def finish(self, started, *others):
        flat = [x for got in started.values() for x in got]
        tied = list(together(*flat, *others))
        for name, got in started.items():
            mine, tied = tied[: len(got)], tied[len(got) :]
            self.step(name, self.waiting[name][0], mine)
        return tied


def program(dp, mp, inputs, cotangent, norm_gain, norm_bias, in_weight, kernels, *rest):
    out_weight, up_weight, down_weight, taps_kept = rest
    layers = in_weight.shape[0]
    groups, chunk, width = inputs.shape
    peers = mp // groups
    shard, hidden = in_weight.shape[3], up_weight.shape[2]
    length = groups * chunk
    cut = -(-shard // 16) * 16
    ways = 2 if dp == 2 and shard == cut and hidden % 32 == 0 else 1
    part = hidden // ways
    dense_rows = 4 * cut // ways
    me, way = lax.axis_index("mp"), lax.axis_index("dp")
    place = jnp.stack([way, me]).astype(jnp.int32)
    zero_half = me // peers == 0
    swap = [(i, (i + peers) % mp) for i in range(mp)]
    halves = [[h * peers + q for q in range(peers)] for h in range(groups)]

    def ordered(own, got):
        return jnp.stack([jnp.where(zero_half, own, got), jnp.where(zero_half, got, own)])

    def pick(x):
        return jnp.where(zero_half, x[0], x[1]), jnp.where(zero_half, x[1], x[0])

    def to_one_sequence(x):
        own, other = pick(x)
        return ordered(own, lax.ppermute(other, "mp", swap)).reshape(length, width)

    def to_two_sequences(x):
        own, other = pick(x.reshape(groups, chunk, width))
        got = lax.ppermute(other.astype(BF16), "mp", swap)
        return ordered(own, got.astype(F32))

    def exchange(x):
        return lax.all_to_all(
            x, "mp", split_axis=0, concat_axis=0, tiled=True, axis_index_groups=halves
        )

    def widen(x, axis):
        pads = [(0, 0)] * x.ndim
        pads[axis] = (0, cut - shard)
        return x if cut == shard else jnp.pad(x, pads)

    dense = [jnp.transpose(in_weight[:, :, j], (0, 2, 1)) for j in range(3)] + [out_weight]
    dense = jnp.concatenate([widen(d, 1) for d in dense], axis=1)
    up = jnp.transpose(up_weight, (0, 2, 1))

    def my_rows(x, rows):
        return lax.dynamic_slice_in_dim(x, way * rows, rows, 1) if ways > 1 else x

    dense = my_rows(dense, dense_rows)
    ff = jnp.concatenate([my_rows(up, part), my_rows(down_weight, part)], axis=1)

    def gather(x):
        x = lax.all_gather(x, "mp", axis=0)
        return [x, flip(x, "dp", dp, 1)] if ways > 1 else [x]

    def gathered(x):
        return lax.all_gather(x, "mp", axis=0)

    def shared(x):
        return [x, flip(x, "dp", dp, 1)] if ways > 1 else [x]

    def out_matrix(pieces):
        skip = dense_rows - cut
        rows = [
            a[:, begin + skip : begin + dense_rows]
            for a, begin in zip(pieces.arrays, pieces.begins)
        ]
        rows = jnp.where(way == 1, rows[0], rows[1]) if ways > 1 else rows[0]
        rows = rows.reshape(groups, peers, cut, width)
        return jnp.swapaxes(rows, 0, 1).reshape(mp * cut, width)

    keep = jnp.arange(kernels.shape[-1])[None, :] < taps_kept[:, None]
    kept = jnp.where(keep[:, None, None, :], kernels, jnp.zeros_like(kernels))
    kept = widen(kept, 2)
    taps = []

    def dense_chains(layer):
        result = Chains()
        bits = mp.bit_length() - 1
        for i in range(2):
            rows = dense[layer, i * dense_rows // 2 : (i + 1) * dense_rows // 2]
            stages = [[b] for b in range(bits - 1, 1, -1)] + [[1 - i], [i]]
            result.add(i, gather_chain(rows, mp, stages))
        return result

    chains = dense_chains(0)
    own, other = pick(inputs)
    mine, other = chains.tie(ff.reshape(-1, width), other)
    ff_mine = gathered(mine)
    (other,) = chains.finish(chains.start(), other)
    moves = [other[: chunk // 2], other[chunk // 2 :], kept[0]]
    moved = []
    while len(moved) < 3:
        now = moves[len(moved)]
        started = chains.start()
        got = lax.ppermute(now, "mp", swap)
        if len(moved) < 2:
            got, moves[len(moved) + 1] = chains.finish(started, got, moves[len(moved) + 1])
        else:
            chains.finish(started)
        moved.append(got)
    while chains.waiting:
        chains.finish(chains.start())
    dense_mine = jnp.concatenate([chains.results.pop(i) for i in range(2)], axis=1)
    other = jnp.concatenate(moved[:2], axis=0)
    got_taps = moved[2]
    stream = ordered(own, other).reshape(length, width)
    none = [0] * ways
    dense_all = [Pieces(shared(dense_mine), none, dense_rows)]

    gains = norm_gain[:, :, None]
    biases = norm_bias[:, :, None]
    saved, out_all = [], []
    own_grad, grad = pick(cotangent)
    less = chunk // 32 * 12
    halves_of_grad = [grad[:less], grad[less:]]
    for layer in range(layers):
        natural = layer == 0
        more = layer + 1 < layers
        got = project(
            natural,
            groups,
            place,
            stream,
            dense_all[layer],
            gains[layer, 0],
            biases[layer, 0],
            cut,
        )
        if natural:
            stream, got = got[0], got[1:]
        operand, gate_two, normed_one = got
        gates = exchange(operand.reshape(peers, groups, 2, cut, length))
        if natural:
            gates, got_taps = together(gates, got_taps)
        taps.append(ordered(kept[layer], got_taps))
        if more:
            following = Chains()
            whole_bits = list(range(mp.bit_length() - 1))
            stages = [whole_bits[i : i + 2] for i in range(2, len(whole_bits), 2)]
            following.add(0, gather_chain(dense[layer + 1], mp, stages + [whole_bits[:2]]))
            (gates,) = following.tie(gates)
            started = following.start()
        if natural:
            ff_mine, gates = together(ff_mine, gates)
            ff_pair = shared(ff_mine)
        conv_two, conv_one, carried = mix(gates, taps[layer])
        out_all.append(out_matrix(dense_all[layer]))
        if more:
            (conv_two,) = following.finish(started, conv_two)
        conv_two = exchange(conv_two).reshape(mp * cut, length)
        if natural:
            conv_two, *ff_pair = together(conv_two, *ff_pair)
            ff_all = [Pieces(ff_pair, [2 * part * i] * ways, 2 * part) for i in range(layers)]
        if more:
            got_taps, conv_two = following.tie(kept[layer + 1], conv_two)
            started = following.start()
            got_taps = lax.ppermute(got_taps, "mp", swap)
        half = None
        if layer >= layers - 2:
            half = halves_of_grad[layer - layers + 2]
            half, conv_two = together(half, conv_two)
            half = lax.ppermute(half, "mp", swap)
        gate_two = gate_two.reshape(mp * cut, length)
        s1, s2, active, slope, normed_two, gated = forward_block(
            layer == layers - 1,
            stream,
            conv_two,
            gate_two,
            out_all[layer],
            ff_all[layer],
            gains[layer, 1],
            biases[layer, 1],
        )
        if half is not None:
            half, s2 = together(half, s2)
            halves_of_grad[layer - layers + 2] = half
        if more:
            got_taps, s2 = following.finish(started, got_taps, s2)
            while following.waiting:
                following.finish(following.start())
            dense_next = following.results[0]
            dense_all.append(Pieces(shared(dense_next), none, dense_rows))
        saved.append(
            (stream, normed_one, gates, conv_one, carried, conv_two, gate_two)
            + (s1, active, slope, normed_two, gated)
        )
        stream = s2
    own_output, other = pick(stream.reshape(groups, chunk, width))
    other = other.astype(BF16)
    got_output = lax.ppermute(other[: chunk // 2], "mp", swap)
    other_output = other[chunk // 2 :]
    grad = ordered(own_grad, jnp.concatenate(halves_of_grad, axis=0)).reshape(length, width)

    gain_rows, bias_rows = [None] * layers, [None] * layers
    dks = [None] * layers
    later = None
    for layer in reversed(range(layers)):
        (s0, normed_one, gates, conv_one, carried, conv_two, gate_two) = saved[layer][:7]
        (s1, active, slope, normed_two, gated) = saved[layer][7:]
        pre, grad, grad_conv, grad_two, dm, do, gain_two, bias_two = backward_block(
            layer == layers - 1,
            grad,
            slope,
            s1,
            conv_two,
            gate_two,
            out_all[layer],
            ff_all[layer],
            gains[layer, 1],
        )
        gain_rows[layer], bias_rows[layer] = [None, gain_two], [None, bias_two]
        mixed = None
        if later is not None:
            mixed, grad_conv = together(later[0], grad_conv)
            got_dk, grad_conv = chains.finish(started, got_dk, grad_conv)
            dks[layer + 1] = own_dk.astype(F32) + got_dk.astype(F32)
        if layer == layers - 1:
            got_output, grad_conv = together(got_output, grad_conv)
        grad_conv = exchange(grad_conv.reshape(peers, groups, cut, length))
        grad_two = grad_two.reshape(mp, cut, length)
        up_job = Plain(ways, mp, pre, normed_two)
        down_job = Plain(ways, mp, active, dm)
        two_rows = [grad_two, gated.reshape(mp, cut, length)]
        mixed_job = Mixed(ways, groups, two_rows, [normed_one, do])
        late_jobs = [] if mixed is None else [Mixed(ways, groups, [mixed], [later[1]])]
        jobs = [up_job, down_job, mixed_job] + late_jobs
        early = weight_grads("early_grads", ways, mp, place, jobs)
        grad_conv, *early = together(grad_conv, *early)
        if layer == layers - 1:
            other_output, grad_conv = together(other_output, grad_conv)
            more_output = lax.ppermute(other_output, "mp", swap)
        chains.add(("flip", layer), chip_chain(early, dp))
        (grad_conv,) = chains.tie(grad_conv)
        started = chains.start()
        grad_mixed, grad_one = unmix(grad_conv, gates, conv_one, taps[layer])
        (grad_mixed,) = chains.finish(started, grad_mixed)
        if layer == layers - 1:
            more_output, grad_mixed = together(more_output, grad_mixed)
        grad_mixed = exchange(grad_mixed).reshape(mp, 2, cut, length)
        if layer == layers - 1:
            output = jnp.concatenate([got_output, more_output], axis=0)
            output = ordered(own_output, output.astype(F32))
            output, grad_mixed = together(output, grad_mixed)
        terms = chains.results.pop(("flip", layer))
        stages = stage_order(mp, 0)
        if layer == 0:
            stages = [[b] for stage in stages for b in stage]
        chains.add(layer, scatter_chain(terms, mp, stages, True))
        dk = tap_grads(grad_conv, gates, carried, grad_one, [] if layer else chains.operands())
        grad_mixed, dk = together(grad_mixed, dk)
        own_dk, other_dk = pick(dk.astype(BF16))
        if layer:
            later = grad_mixed, normed_one
        else:
            started = chains.start()
            got_dk = lax.ppermute(other_dk, "mp", swap)
            late_job = Mixed(ways, groups, [grad_mixed], [normed_one])
            late = weight_grads("late_grads", ways, mp, place, [late_job])
            grad_mixed, *late = together(grad_mixed, *late)
            tail = Chains()
            tail.add("late", chip_chain(late, dp))
            last = tail.start()
        grad, gain_one, bias_one = unproject(
            layer == 0,
            groups,
            place,
            grad_mixed,
            grad_two,
            dense_all[layer],
            s0,
            grad,
            gains[layer, 0],
        )
        gain_rows[layer][0], bias_rows[layer][0] = gain_one, bias_one
        if layer:
            grad, other_dk = chains.tie(grad, other_dk)
            got_dk = lax.ppermute(other_dk, "mp", swap)
            started = chains.start()

    grad, got_dk = tail.finish(last, grad, got_dk)
    own, other = pick(grad.reshape(groups, chunk, width))
    swapped = lax.ppermute(other.astype(BF16), "mp", swap)
    (gain_rows[0][0],) = chains.finish(started, gain_rows[0][0])
    bits = list(range(mp.bit_length() - 1))
    quarters = [bits[i : i + 2] for i in range(0, len(bits), 2)]
    norms = jnp.stack([jnp.stack([jnp.stack(r) for r in rows]) for rows in (gain_rows, bias_rows)])
    shape = norms.shape[:-2] + (width,)
    norms = norms.reshape(-1, width)
    tail.add("late", last_chain(tail.results.pop("late"), norms, mp, quarters))
    first_round = True
    while chains.waiting or tail.waiting:
        started, last = chains.start(), tail.start()
        if started:
            chains.finish(started)
        if first_round:
            (swapped,) = tail.finish(last, swapped)
        elif last:
            tail.finish(last)
        first_round = False
    input_grad = ordered(own, swapped.astype(F32))
    dks[0] = own_dk.astype(F32) + got_dk.astype(F32)
    dk = jnp.stack(dks).astype(BF16).astype(F32)
    late, norms = tail.results.pop("late")
    found = [chains.results.pop(layer) for layer in reversed(range(layers))]
    final = [x.astype(BF16) for x in found + [late]]
    if ways == 1:
        dk, norms = dp_sum(dk, dp), dp_sum(norms, dp)
        final = [[dp_sum(x, dp)] for x in found + [late]]
    else:
        dk = dk + flip(dk.astype(BF16), "dp", dp, 1).astype(F32)
        norms = in_two(norms)
        sizes = [x.shape[0] for x in final + [norms]]
        sent = jnp.concatenate(final + [norms], axis=0)
        got = flip(sent, "dp", dp, 1)
        zero = way == 0
        pair = jnp.where(zero, sent, got).astype(F32), jnp.where(zero, got, sent).astype(F32)
        begin, pieces = 0, []
        for size in sizes:
            pieces.append([x[begin : begin + size] for x in pair])
            begin += size
        final, norms = pieces[:-1], pieces[-1]
        half = norms[0].shape[0] // 2
        norms = (norms[0][:half] + norms[0][half:]) + (norms[1][:half] + norms[1][half:])
    norms = norms.reshape(shape)
    dk = dk[:, :, :shard]
    tap_out = jnp.where(keep[:, None, None, :], dk, 0.0)

    def cut_rows(x, *sizes):
        begin = 0
        for size in sizes:
            yield x[begin : begin + size]
            begin += size

    share = 2 * cut // ways
    wide = [[None] * layers for _ in range(4)]
    order = []
    for layer in range(layers - 1, -1, -1):
        now = [(0, layer), (1, layer), (2, layer)] + [(3, layer + 1)] * (layer < layers - 1)
        order.append(now)
    order.append([(3, 0)])
    sizes = [part, part, share, share]
    found = zip(order, final)
    for order, arrays in found:
        pieces = zip(*[cut_rows(x, *[sizes[i] for i, _ in order]) for x in arrays])
        for (i, layer), x in zip(order, pieces):
            wide[i][layer] = x

    def rows_of_both(arrays):
        return jnp.concatenate(arrays, axis=0)

    parts = [[] for _ in range(6)]
    for up, down, early, late in zip(*wide):
        two, out = (early[0][:cut], early[0][cut:]) if ways == 1 else early
        one, value = (late[0][:cut], late[0][cut:]) if ways == 1 else late
        for store, x in zip(parts, (one, two, value, out, rows_of_both(up), rows_of_both(down))):
            store.append(x)
    one, two, value, out, up, down = (jnp.stack(p) for p in parts)
    in_out = jnp.stack([one, two, value], axis=1)[:, :, :shard]
    return (
        output,
        input_grad,
        norms[0],
        norms[1],
        jnp.transpose(in_out, (0, 3, 1, 2)),
        tap_out,
        out[:, :shard],
        jnp.transpose(up, (0, 2, 1)),
        down,
    )


def solution(mesh):
    sizes = dict(mesh.shape)
    specs = (
        P("dp", "mp", None),
        P("dp", "mp", None),
        P(),
        P(),
        P(None, None, None, "mp"),
        P(None, None, "mp", None),
        P(None, "mp", None),
        P(None, None, "mp"),
        P(None, "mp", None),
    )
    return jax.shard_map(
        functools.partial(program, sizes["dp"], sizes["mp"]),
        mesh=mesh,
        in_specs=specs + (P(),),
        out_specs=specs,
        check_vma=False,
    )
```
